128 devices in a mesh: dp: 8 (over z, y_lo), seq: 16 (over y_hi, x, core).
Axes of the slice: x: 4, y: 4 (y_hi: 2, y_lo: 2; y = y_hi * 2 + y_lo), z: 4, core: 2. Of those that a mesh axis runs over, the one named last changes fastest.
Arguments:
- hidden_in: bfloat16 [2, 16, 2048, 640], P(None, 'dp', 'seq'), may hold values from -6 to 6
- segment_ids: int32 [2, 16, 2048], P(None, 'dp', 'seq'), may hold values from 0 to 7, as said below
- cotangent: bfloat16 [2, 16, 2048, 640], P(None, 'dp', 'seq'), may hold values from -6 to 6
- attn_gain: bfloat16 [640], P(('dp', 'seq')), may hold values from 0.099609375 to 1.8984375
- query_weight: bfloat16 [640, 1024], P(('dp', 'seq')), may hold values from -0.25 to 0.25
- key_weight: bfloat16 [640, 256], P(('dp', 'seq')), may hold values from -0.25 to 0.25
- value_weight: bfloat16 [640, 256], P(('dp', 'seq')), may hold values from -0.25 to 0.25
- query_gain: bfloat16 [256], P(('dp', 'seq')), may hold values from 0.099609375 to 1.8984375
- key_gain: bfloat16 [256], P(('dp', 'seq')), may hold values from 0.099609375 to 1.8984375
- output_weight: bfloat16 [1024, 640], P(('dp', 'seq')), may hold values from -0.1875 to 0.1875
- post_attn_gain: bfloat16 [640], P(('dp', 'seq')), may hold values from 0.099609375 to 1.8984375
- ffn_gain: bfloat16 [640], P(('dp', 'seq')), may hold values from 0.099609375 to 1.8984375
- gate_weight: bfloat16 [640, 2048], P(('dp', 'seq')), may hold values from -0.25 to 0.25
- up_weight: bfloat16 [640, 2048], P(('dp', 'seq')), may hold values from -0.25 to 0.25
- down_weight: bfloat16 [2048, 640], P(('dp', 'seq')), may hold values from -0.125 to 0.125
- post_ffn_gain: bfloat16 [640], P(('dp', 'seq')), may hold values from 0.099609375 to 1.8984375
Outputs:
- block_out: bfloat16 [2, 16, 2048, 640], P(None, 'dp', 'seq')
- input_grad: bfloat16 [2, 16, 2048, 640], P(None, 'dp', 'seq')
- grad_attn_gain: float32 [640], P(('dp', 'seq'))
- grad_query_weight: float32 [640, 1024], P(('dp', 'seq'))
- grad_key_weight: float32 [640, 256], P(('dp', 'seq'))
- grad_value_weight: float32 [640, 256], P(('dp', 'seq'))
- grad_query_gain: float32 [256], P(('dp', 'seq'))
- grad_key_gain: float32 [256], P(('dp', 'seq'))
- grad_output_weight: float32 [1024, 640], P(('dp', 'seq'))
- grad_post_attn_gain: float32 [640], P(('dp', 'seq'))
- grad_ffn_gain: float32 [640], P(('dp', 'seq'))
- grad_gate_weight: float32 [640, 2048], P(('dp', 'seq'))
- grad_up_weight: float32 [640, 2048], P(('dp', 'seq'))
- grad_down_weight: float32 [2048, 640], P(('dp', 'seq'))
- grad_post_ffn_gain: float32 [640], P(('dp', 'seq'))
The draws below stay inside these ranges and needn't reach their ends.
Inputs may be any that keep to these rules, and one draw needn't show every extreme that they name: `segment_ids`: in every row the ids start at 0 and never fall; among the 4 rows that one index of dp holds, one row drawn from the seed is a single document.
All inputs are finite; a program needn't handle non-finite values.
Results may differ from the reference program's by a relative error of at most 0.029.
Values may be sent and summed in bfloat16 or wider, within the bound.
No kernel may reach another device: no remote copies, remote signals or barrier semaphores. Data moves between devices by JAX's collectives and lax.ppermute only.
A program may use at most 128 MiB of HBM per device.

```python
import math
import jax
import jax.numpy as jnp
from jax import lax

D = 640
HEADS = 4
HD = 256
FF = 2048
WINDOW = 512
BLOCK = 128
MICRO = 2
ROWS_DEV = 2
HALO = 4
ROWS = 16
LENGTH = 2048
N_SEQ = 16


def draw_segment_ids(key, part):
    key = jax.random.fold_in(key, 7)
    tick_key, pick_key = jax.random.split(key)
    tick_draws = jax.random.randint(tick_key, (MICRO, ROWS, LENGTH), 0, 2 * BLOCK)
    places = jnp.arange(LENGTH, dtype=jnp.int32)
    forced = (places % (2 * BLOCK) == 0) & (places > 0)
    begins = ((tick_draws == 0) | forced[None, None, :]).astype(jnp.int32)
    begins = begins.at[:, :, 0].set(0)
    groups = ROWS // ROWS_DEV
    chosen_slot = jax.random.randint(pick_key, (groups,), 0, MICRO * ROWS_DEV)
    micro_ids = jnp.arange(MICRO, dtype=jnp.int32)[:, None]
    row_ids = jnp.arange(ROWS, dtype=jnp.int32)[None, :]
    slot_ids = micro_ids * ROWS_DEV + row_ids % ROWS_DEV
    single = slot_ids == chosen_slot[row_ids // ROWS_DEV]
    begins = jnp.where(single[:, :, None], 0, begins)
    counted = jnp.cumsum(begins, axis=-1).astype(jnp.int32)
    return jnp.minimum(counted, N_SEQ // 2 - 1).astype(jnp.int32)


def shard_levels(own_key, dims, pieces, least, high):
    loudness, own = 1.0, jax.random.fold_in(own_key, 6)
    for dim, parts in pieces:
        heights = jnp.exp(jax.random.uniform(jax.random.fold_in(own, dim), (parts,), jnp.float32, least / len(pieces), high / len(pieces)))
        loudness = loudness * jnp.repeat(heights, dims[dim] // parts).reshape([-1 if axis == dim else 1 for axis in range(len(dims))])
    return loudness


def noise(stream_key, extent, deviation, limit, shards=(), kind=jnp.bfloat16):
    result = jax.random.normal(stream_key, extent, jnp.float32) * deviation
    if len(shards) > 0:
        result = shard_levels(stream_key, extent, shards, -0.22, 0.18) * result
    return jnp.clip(result, min=-limit, max=limit).astype(kind)


def setup_inputs(seed: int = 0) -> dict:
    splits = jax.random.split(jax.random.key(seed), 17)
    hidden_in = noise(splits[0], (MICRO, ROWS, LENGTH, D), 1.0, 6.0, ((1, 8), (2, 16)))
    segment_ids = draw_segment_ids(jax.random.fold_in(splits[16], 71), 0)
    cotangent = noise(splits[2], (MICRO, ROWS, LENGTH, D), 1.0, 6.0, ((1, 8), (2, 16)))
    attn_gain = jnp.clip(1.0 + 0.18 * jax.random.normal(splits[3], (D,), jnp.float32), 0.099609375, 1.8984375).astype(jnp.bfloat16)
    query_weight = noise(splits[4], (D, HEADS * HD), D ** -0.5, 0.25, ((0, 128),))
    key_weight = noise(splits[5], (D, HD), D ** -0.5, 0.25, ((0, 128),))
    value_weight = noise(splits[6], (D, HD), D ** -0.5, 0.25, ((0, 128),))
    query_gain = jnp.clip(1.0 + 0.18 * jax.random.normal(splits[7], (HD,), jnp.float32), 0.099609375, 1.8984375).astype(jnp.bfloat16)
    key_gain = jnp.clip(1.0 + 0.18 * jax.random.normal(splits[8], (HD,), jnp.float32), 0.099609375, 1.8984375).astype(jnp.bfloat16)
    output_weight = noise(splits[9], (HEADS * HD, D), (HEADS * HD) ** -0.5, 0.1875, ((0, 128),))
    post_attn_gain = jnp.clip(1.0 + 0.18 * jax.random.normal(splits[10], (D,), jnp.float32), 0.099609375, 1.8984375).astype(jnp.bfloat16)
    ffn_gain = jnp.clip(1.0 + 0.18 * jax.random.normal(splits[11], (D,), jnp.float32), 0.099609375, 1.8984375).astype(jnp.bfloat16)
    gate_weight = noise(splits[12], (D, FF), D ** -0.5, 0.25, ((0, 128),))
    up_weight = noise(splits[13], (D, FF), D ** -0.5, 0.25, ((0, 128),))
    down_weight = noise(splits[14], (FF, D), FF ** -0.5, 0.125, ((0, 128),))
    post_ffn_gain = jnp.clip(1.0 + 0.18 * jax.random.normal(splits[15], (D,), jnp.float32), 0.099609375, 1.8984375).astype(jnp.bfloat16)
    return {"hidden_in": hidden_in, "segment_ids": segment_ids, "cotangent": cotangent, "attn_gain": attn_gain, "query_weight": query_weight, "key_weight": key_weight, "value_weight": value_weight, "query_gain": query_gain, "key_gain": key_gain, "output_weight": output_weight, "post_attn_gain": post_attn_gain, "ffn_gain": ffn_gain, "gate_weight": gate_weight, "up_weight": up_weight, "down_weight": down_weight, "post_ffn_gain": post_ffn_gain}


EPSILON = 1e-06
ROPE_BASE = 10000.0
MASKED = -1e+30

@jax.custom_vjp
def low(v):
    return lax.optimization_barrier(v.astype(jnp.bfloat16)).astype(jnp.float32)

@jax.custom_vjp
def low_back(v):
    return v

def low_keep(v):
    return (low(v), None)

def low_pass(kept, grad):
    return (grad,)

def back_keep(v):
    return (v, None)

def back_low(kept, grad):
    return (low(grad),)
low.defvjp(low_keep, low_pass)
low_back.defvjp(back_keep, back_low)

def product(left_array, right_array):
    return jnp.dot(left_array, right_array, precision=lax.Precision.HIGHEST, preferred_element_type=jnp.float32)

def normalize(values, gain_vector):
    return values * lax.rsqrt(lax.optimization_barrier(jnp.mean(values * values, -1, keepdims=True)) + EPSILON) * gain_vector

def rope_tables(positions):
    half_size = HD // 2
    frequency = jnp.exp(jnp.arange(half_size, dtype=jnp.float32) * (-2.0 * math.log(ROPE_BASE) / HD))
    angles = positions.astype(jnp.float32)[..., None] * frequency
    return (jnp.cos(angles), jnp.sin(angles))

def rotate(values, cosine_table, sine_table):
    half_size = values.shape[-1] // 2
    first_half = values[..., :half_size]
    second_half = values[..., half_size:]
    return jnp.concatenate([first_half * cosine_table - second_half * sine_table, second_half * cosine_table + first_half * sine_table], axis=-1)

def doc_positions(segment_row):
    places = jnp.arange(LENGTH, dtype=jnp.int32)
    begins = jnp.concatenate([jnp.ones((1,), dtype=jnp.bool_), segment_row[1:] != segment_row[:-1]])
    starts = lax.cummax(jnp.where(begins, places, 0).astype(jnp.int32), axis=0)
    return (places - starts, starts)

def row_forward(hidden_row, cosine_table, sine_table, starts, params):
    attn_gain, query_weight, key_weight, value_weight, query_gain, key_gain, output_weight, post_attn_gain, ffn_gain, gate_weight, up_weight, down_weight, post_ffn_gain = params
    normed = low(normalize(hidden_row, attn_gain))
    query_pre = low_back(product(normed, query_weight)).reshape(LENGTH, HEADS, HD)
    key_pre = low_back(product(normed, key_weight))
    values = low(low_back(product(normed, value_weight)))
    queries = low(rotate(normalize(query_pre, query_gain), cosine_table[:, None, :], sine_table[:, None, :]))
    keys_all = low(rotate(normalize(key_pre, key_gain), cosine_table, sine_table))
    padding = jnp.zeros((HALO * BLOCK, HD), jnp.float32)
    padded_keys = jnp.concatenate([padding, keys_all], axis=0)
    padded_values = jnp.concatenate([padding, values], axis=0)
    score_scale = HD ** (-0.5)

    def attend_block(block_index):
        first_query = block_index * BLOCK
        block_queries = lax.dynamic_slice_in_dim(queries, first_query, BLOCK, 0)
        block_keys = lax.dynamic_slice_in_dim(padded_keys, first_query, (HALO + 1) * BLOCK, 0)
        block_values = lax.dynamic_slice_in_dim(padded_values, first_query, (HALO + 1) * BLOCK, 0)
        block_starts = lax.dynamic_slice_in_dim(starts, first_query, BLOCK, 0)
        query_places = first_query + jnp.arange(BLOCK, dtype=jnp.int32)
        key_places = first_query - HALO * BLOCK + jnp.arange((HALO + 1) * BLOCK, dtype=jnp.int32)
        visible = (key_places[None, :] <= query_places[:, None]) & (query_places[:, None] - key_places[None, :] < WINDOW) & (key_places[None, :] >= block_starts[:, None])
        scores = low_back(jnp.einsum('qhd,kd->hqk', block_queries, block_keys, precision=lax.Precision.HIGHEST, preferred_element_type=jnp.float32) * score_scale)
        scores = jnp.where(visible[None], scores, MASKED)
        row_top = lax.optimization_barrier(jnp.max(scores, -1, keepdims=True))
        exponent_terms = jnp.exp(scores - row_top)
        soft_weights = low(exponent_terms / lax.optimization_barrier(jnp.sum(exponent_terms, -1, keepdims=True)))
        mixed = jnp.einsum('hqk,kd->qhd', soft_weights, block_values, precision=lax.Precision.HIGHEST, preferred_element_type=jnp.float32)
        return low(low_back(mixed)).reshape(BLOCK, HEADS * HD)
    attended = lax.map(jax.checkpoint(attend_block), jnp.arange(LENGTH // BLOCK, dtype=jnp.int32)).reshape(LENGTH, HEADS * HD)
    projected = low_back(product(attended, output_weight))
    middle = hidden_row + normalize(projected, post_attn_gain)
    ffn_in = low(normalize(middle, ffn_gain))
    gate_value = low_back(product(ffn_in, gate_weight))
    up_value = low_back(product(ffn_in, up_weight))
    inner_act = low(jax.nn.gelu(gate_value, approximate=True) * up_value)
    down_value = low_back(product(inner_act, down_weight))
    return middle + normalize(down_value, post_ffn_gain)

def reference(hidden_in, segment_ids, cotangent, attn_gain, query_weight, key_weight, value_weight, query_gain, key_gain, output_weight, post_attn_gain, ffn_gain, gate_weight, up_weight, down_weight, post_ffn_gain):
    params = tuple((weight_arg.astype(jnp.float32) for weight_arg in (attn_gain, query_weight, key_weight, value_weight, query_gain, key_gain, output_weight, post_attn_gain, ffn_gain, gate_weight, up_weight, down_weight, post_ffn_gain)))
    rows_all = MICRO * ROWS
    flat_hidden = hidden_in.astype(jnp.float32).reshape(rows_all, LENGTH, D)
    flat_cotangent = cotangent.astype(jnp.float32).reshape(rows_all, LENGTH, D)
    flat_segments = segment_ids.reshape(rows_all, LENGTH)

    def per_row(totals, row_inputs):
        hidden_row, cotangent_row, segment_row = row_inputs
        positions, starts = doc_positions(segment_row)
        cosine_table, sine_table = rope_tables(positions)

        def forward(hidden_value, weight_values):
            return row_forward(hidden_value, cosine_table, sine_table, starts, weight_values)
        output, pullback = jax.vjp(forward, hidden_row, params)
        hidden_grad, weight_grads = pullback(cotangent_row)
        totals = tuple((running + fresh_grad for running, fresh_grad in zip(totals, weight_grads)))
        return (totals, (output.astype(jnp.bfloat16), hidden_grad.astype(jnp.bfloat16)))
    initial = tuple((jnp.zeros_like(param_value) for param_value in params))
    grad_totals, (outputs, input_grads) = lax.scan(per_row, initial, (flat_hidden, flat_cotangent, flat_segments))
    block_out = outputs.reshape(MICRO, ROWS, LENGTH, D)
    input_grad = input_grads.reshape(MICRO, ROWS, LENGTH, D)
    return (block_out, input_grad, grad_totals[0], grad_totals[1], grad_totals[2], grad_totals[3], grad_totals[4], grad_totals[5], grad_totals[6], grad_totals[7], grad_totals[8], grad_totals[9], grad_totals[10], grad_totals[11], grad_totals[12])
```

```python
import math

import jax
import jax.numpy as jnp
from jax import lax
from jax.sharding import PartitionSpec as P

WINDOW = 512
HALO = 4


EPSILON = 1e-06
ROPE_BASE = 10000.0
MASKED = -1e30


def shifted(value, axis, by):
    count = lax.axis_size(axis)
    pairs = [(i, i + by) for i in range(count) if 0 <= i + by < count]
    return lax.ppermute(value, axis, pairs)


AXES = ("dp", "seq")
SIZE = {"x": 4, "y": 4, "z": 4, "c": 2}
FIRST_ORDER = ("z", "y", "x")
SECOND_ORDER = ("x", "z", "y")
THIRD_ORDER = ("y", "x", "z")


def shard_of(z, y, x, c):
    return z * 32 + (y % 2) * 16 + (y // 2) * 8 + x * 2 + c


def moved(axis, by):
    pairs = []
    for z in range(4):
        for y in range(4):
            for x in range(4):
                for c in range(2):
                    place = {"z": z, "y": y, "x": x, "c": c}
                    place[axis] = (place[axis] + by) % SIZE[axis]
                    pairs.append((shard_of(z, y, x, c), shard_of(**place)))
    return pairs


def send(value, axis, by):
    return lax.ppermute(value, AXES, moved(axis, by))


def my_place():
    dp, seq = lax.axis_index("dp"), lax.axis_index("seq")
    return {"z": dp // 2, "y": (seq // 8) * 2 + dp % 2, "x": (seq // 2) % 4, "c": seq % 2}


def exchange(value, axis):
    return jnp.stack([value] + [send(value, axis, -by) for by in range(1, SIZE[axis])])


def collect(value, axis):
    total = value[0].astype(jnp.float32)
    for by in range(1, SIZE[axis]):
        total = total + send(value[by], axis, by).astype(jnp.float32)
    return total


def gather_part(value, order, middle):
    value = exchange(exchange(value, order[0]), order[1])
    return exchange(exchange(middle(value), order[2]), "c")


def scatter_part(value, order, middle):
    value = collect(value, "c").astype(jnp.bfloat16)
    value = middle(collect(value, order[2]).astype(jnp.bfloat16))
    value = collect(value, order[1]).astype(jnp.bfloat16)
    return collect(value, order[0])


def arrival_shards(order):
    me = my_place()
    grid = jnp.arange(128, dtype=jnp.int32)
    place = {
        "c": (me["c"] + grid // 64) % 2,
        order[2]: (me[order[2]] + grid // 16) % 4,
        order[1]: (me[order[1]] + grid // 4) % 4,
        order[0]: (me[order[0]] + grid) % 4,
    }
    return shard_of(**place)


def selection(order, rows):
    shards = arrival_shards(order)
    natural = (shards[:, None] * rows + jnp.arange(rows, dtype=jnp.int32)[None]).reshape(-1)
    return (jnp.arange(128 * rows, dtype=jnp.int32)[:, None] == natural[None, :]).astype(
        jnp.bfloat16
    )


def mat_product(left_array, right_array):
    return jnp.dot(left_array, right_array, preferred_element_type=jnp.float32)


def left_contract(left_array, right_array):
    return lax.dot_general(
        left_array, right_array, (((0,), (0,)), ((), ())), preferred_element_type=jnp.float32
    )


def right_contract(left_array, right_array):
    return lax.dot_general(
        left_array, right_array, (((1,), (1,)), ((), ())), preferred_element_type=jnp.float32
    )


def normalize_parts(values):
    inverse = lax.rsqrt(jnp.mean(values * values, -1, keepdims=True) + EPSILON)
    return (values * inverse, inverse)


def norm_backward(grad_hat, unit_value, inverse):
    return inverse * (grad_hat - unit_value * jnp.mean(grad_hat * unit_value, -1, keepdims=True))


def gelu_tanh(values):
    return jax.nn.gelu(values, approximate=True)


def rope_tables(positions, head_size):
    half_size = head_size // 2
    frequency = jnp.exp(
        jnp.arange(half_size, dtype=jnp.float32) * (-2.0 * math.log(ROPE_BASE) / head_size)
    )
    angles = positions.astype(jnp.float32)[..., None] * frequency
    return (jnp.cos(angles), jnp.sin(angles))


def rotate(values, cosine_table, sine_table):
    half_size = values.shape[-1] // 2
    first_half = values[..., :half_size]
    second_half = values[..., half_size:]
    return jnp.concatenate(
        [
            first_half * cosine_table - second_half * sine_table,
            second_half * cosine_table + first_half * sine_table,
        ],
        axis=-1,
    )


def visible_mask(segments, segments_all, block_size):
    query_local = jnp.arange(block_size, dtype=jnp.int32)[:, None]
    key_local = jnp.arange((HALO + 1) * block_size, dtype=jnp.int32)[None, :] - HALO * block_size
    inside = (key_local <= query_local) & (query_local - key_local < WINDOW)
    present = key_local + lax.axis_index("seq") * block_size >= 0
    same_doc = segments[:, :, None] == segments_all[:, None, :]
    return ((inside & present)[None] & same_doc)[:, None]


def masked_scores(queries, key_all, visible):
    score_scale = queries.shape[-1] ** (-0.5)
    raw_scores = (
        jnp.einsum("rqhd,rkd->rhqk", queries, key_all, preferred_element_type=jnp.float32)
        * score_scale
    )
    return jnp.where(visible, raw_scores, MASKED)


def gather_rim(key_value):
    pieces = []
    for distance in range(1, HALO + 1):
        pieces.append(shifted(key_value, "seq", distance))
    return jnp.concatenate(pieces[::-1] + [key_value], axis=2)


def return_rim(grad_all, block_size):

    def rim_piece(distance):
        first_key = (HALO - distance) * block_size
        return grad_all[:, :, first_key : first_key + block_size]

    summed = rim_piece(0)
    for distance in range(1, HALO + 1):
        summed = summed + shifted(
            rim_piece(distance).astype(jnp.bfloat16), "seq", -distance
        ).astype(jnp.float32)
    return summed


def forward_pass(hidden, positions, segments, weights):
    (
        attn_gain,
        query_weight,
        key_weight,
        value_weight,
        query_gain,
        key_gain,
        output_weight,
        post_attn_gain,
        ffn_gain,
        gate_weight,
        up_weight,
        down_weight,
        post_ffn_gain,
    ) = weights
    row_count, block_size, model_width = hidden.shape
    tokens = row_count * block_size
    head_size = key_weight.shape[1]
    head_count = query_weight.shape[1] // head_size
    flat_hidden = hidden.reshape(tokens, model_width).astype(jnp.float32)
    unit_in, inverse_in = normalize_parts(flat_hidden)
    normed = (unit_in * attn_gain.astype(jnp.float32)).astype(jnp.bfloat16)
    query_pre = mat_product(normed, query_weight).reshape(
        row_count, block_size, head_count, head_size
    )
    key_pre = mat_product(normed, key_weight).reshape(row_count, block_size, head_size)
    values = (
        mat_product(normed, value_weight)
        .astype(jnp.bfloat16)
        .reshape(row_count, block_size, head_size)
    )
    query_unit, query_inverse = normalize_parts(query_pre)
    key_unit, key_inverse = normalize_parts(key_pre)
    cosine_table, sine_table = rope_tables(positions, head_size)
    queries = rotate(
        query_unit * query_gain.astype(jnp.float32),
        cosine_table[:, :, None],
        sine_table[:, :, None],
    ).astype(jnp.bfloat16)
    keys_own = rotate(key_unit * key_gain.astype(jnp.float32), cosine_table, sine_table).astype(
        jnp.bfloat16
    )
    key_value = gather_rim(jnp.stack([keys_own, values]))
    segments_all = jnp.concatenate(
        [shifted(segments, "seq", distance) for distance in range(HALO, 0, -1)] + [segments], axis=1
    )
    visible = visible_mask(segments, segments_all, block_size)
    scores = masked_scores(queries, key_value[0], visible)
    row_top = jnp.max(scores, -1, keepdims=True)
    exponent_terms = jnp.exp(scores - row_top)
    row_total = jnp.sum(exponent_terms, -1, keepdims=True)
    log_total = row_top + jnp.log(row_total)
    soft_low = (exponent_terms / row_total).astype(jnp.bfloat16)
    attended = (
        jnp.einsum("rhqk,rkd->rqhd", soft_low, key_value[1], preferred_element_type=jnp.float32)
        .astype(jnp.bfloat16)
        .reshape(tokens, head_count * head_size)
    )
    projected = mat_product(attended, output_weight)
    proj_unit, proj_inverse = normalize_parts(projected)
    middle = flat_hidden + proj_unit * post_attn_gain.astype(jnp.float32)
    mid_unit, mid_inverse = normalize_parts(middle)
    ffn_in = (mid_unit * ffn_gain.astype(jnp.float32)).astype(jnp.bfloat16)
    gate_value = mat_product(ffn_in, gate_weight)
    up_value = mat_product(ffn_in, up_weight)
    inner_act = (gelu_tanh(gate_value) * up_value).astype(jnp.bfloat16)
    down_value = mat_product(inner_act, down_weight)
    down_unit, down_inverse = normalize_parts(down_value)
    output = (
        (middle + down_unit * post_ffn_gain.astype(jnp.float32))
        .astype(jnp.bfloat16)
        .reshape(row_count, block_size, model_width)
    )
    kept_values = (
        unit_in,
        inverse_in,
        normed,
        query_unit,
        query_inverse,
        key_unit,
        key_inverse,
        cosine_table,
        sine_table,
        queries,
        key_value,
        visible,
        log_total,
        attended,
        proj_unit,
        proj_inverse,
        mid_unit,
        mid_inverse,
        ffn_in,
        gate_value,
        up_value,
        inner_act,
        down_unit,
        down_inverse,
    )
    return (output, kept_values)


def backward_pass(cotangent, kept_values, weights):
    (
        attn_gain,
        query_weight,
        key_weight,
        value_weight,
        query_gain,
        key_gain,
        output_weight,
        post_attn_gain,
        ffn_gain,
        gate_weight,
        up_weight,
        down_weight,
        post_ffn_gain,
    ) = weights
    (
        unit_in,
        inverse_in,
        normed,
        query_unit,
        query_inverse,
        key_unit,
        key_inverse,
        cosine_table,
        sine_table,
        queries,
        key_value,
        visible,
        log_total,
        attended,
        proj_unit,
        proj_inverse,
        mid_unit,
        mid_inverse,
        ffn_in,
        gate_value,
        up_value,
        inner_act,
        down_unit,
        down_inverse,
    ) = kept_values
    row_count, block_size, model_width = cotangent.shape
    tokens = row_count * block_size
    head_size = key_weight.shape[1]
    head_count = query_weight.shape[1] // head_size
    out_grad = cotangent.reshape(tokens, model_width).astype(jnp.float32)
    grad_post_ffn = jnp.sum(out_grad * down_unit, 0)
    down_grad = norm_backward(
        out_grad * post_ffn_gain.astype(jnp.float32), down_unit, down_inverse
    ).astype(jnp.bfloat16)
    grad_down = left_contract(inner_act, down_grad)
    inner_grad = right_contract(down_grad, down_weight)
    activated, gelu_pull = jax.vjp(gelu_tanh, gate_value)
    up_grad = (inner_grad * activated).astype(jnp.bfloat16)
    gate_grad = gelu_pull(inner_grad * up_value)[0].astype(jnp.bfloat16)
    grad_gate = left_contract(ffn_in, gate_grad)
    grad_up = left_contract(ffn_in, up_grad)
    ffn_in_grad = right_contract(gate_grad, gate_weight) + right_contract(up_grad, up_weight)
    grad_ffn = jnp.sum(ffn_in_grad * mid_unit, 0)
    middle_grad = out_grad + norm_backward(
        ffn_in_grad * ffn_gain.astype(jnp.float32), mid_unit, mid_inverse
    )
    grad_post_attn = jnp.sum(middle_grad * proj_unit, 0)
    proj_grad = norm_backward(
        middle_grad * post_attn_gain.astype(jnp.float32), proj_unit, proj_inverse
    ).astype(jnp.bfloat16)
    grad_output = left_contract(attended, proj_grad)
    attended_grad = (
        right_contract(proj_grad, output_weight)
        .astype(jnp.bfloat16)
        .reshape(row_count, block_size, head_count, head_size)
    )
    scores = masked_scores(queries, key_value[0], visible)
    soft_weights = jnp.exp(scores - log_total)
    prob_grad = jnp.einsum(
        "rqhd,rkd->rhqk", attended_grad, key_value[1], preferred_element_type=jnp.float32
    )
    row_dot = jnp.sum(soft_weights * prob_grad, -1, keepdims=True)
    score_grad = (soft_weights * (prob_grad - row_dot)).astype(jnp.bfloat16)
    score_scale = head_size ** (-0.5)
    query_grad = (
        jnp.einsum("rhqk,rkd->rqhd", score_grad, key_value[0], preferred_element_type=jnp.float32)
        * score_scale
    )
    key_all_grad = (
        jnp.einsum("rhqk,rqhd->rkd", score_grad, queries, preferred_element_type=jnp.float32)
        * score_scale
    )
    value_all_grad = jnp.einsum(
        "rhqk,rqhd->rkd",
        soft_weights.astype(jnp.bfloat16),
        attended_grad,
        preferred_element_type=jnp.float32,
    )
    key_value_grad = return_rim(jnp.stack([key_all_grad, value_all_grad]), block_size)
    value_grad = key_value_grad[1].astype(jnp.bfloat16).reshape(tokens, head_size)
    key_rot_grad = rotate(key_value_grad[0], cosine_table, -sine_table)
    grad_key_gain = jnp.sum(key_rot_grad * key_unit, (0, 1))
    key_pre_grad = (
        norm_backward(key_rot_grad * key_gain.astype(jnp.float32), key_unit, key_inverse)
        .astype(jnp.bfloat16)
        .reshape(tokens, head_size)
    )
    query_rot_grad = rotate(query_grad, cosine_table[:, :, None], -sine_table[:, :, None])
    grad_query_gain = jnp.sum(query_rot_grad * query_unit, (0, 1, 2))
    query_pre_grad = (
        norm_backward(query_rot_grad * query_gain.astype(jnp.float32), query_unit, query_inverse)
        .astype(jnp.bfloat16)
        .reshape(tokens, head_count * head_size)
    )
    grad_query = left_contract(normed, query_pre_grad)
    grad_key = left_contract(normed, key_pre_grad)
    grad_value = left_contract(normed, value_grad)
    normed_grad = (
        right_contract(query_pre_grad, query_weight)
        + right_contract(key_pre_grad, key_weight)
        + right_contract(value_grad, value_weight)
    )
    grad_attn = jnp.sum(normed_grad * unit_in, 0)
    input_grad = (
        (
            middle_grad
            + norm_backward(normed_grad * attn_gain.astype(jnp.float32), unit_in, inverse_in)
        )
        .astype(jnp.bfloat16)
        .reshape(row_count, block_size, model_width)
    )
    weight_grads = (
        grad_attn,
        grad_query,
        grad_key,
        grad_value,
        grad_query_gain,
        grad_key_gain,
        grad_output,
        grad_post_attn,
        grad_ffn,
        grad_gate,
        grad_up,
        grad_down,
        grad_post_ffn,
    )
    return (input_grad, weight_grads)


def low_product(left_array, right_array):
    return mat_product(left_array, right_array).astype(jnp.bfloat16)


def gain_column(gain):
    return jnp.pad(gain, (0, 5 - gain.shape[0]))[:, None]


def on_device(
    hidden_in,
    segment_ids,
    cotangent,
    attn_gain,
    query_weight,
    key_weight,
    value_weight,
    query_gain,
    key_gain,
    output_weight,
    post_attn_gain,
    ffn_gain,
    gate_weight,
    up_weight,
    down_weight,
    post_ffn_gain,
):
    micro_count, rows_dev, block_size, model_width = hidden_in.shape
    rows = micro_count * rows_dev
    gains = jnp.concatenate(
        [
            gain_column(gain)
            for gain in (attn_gain, post_attn_gain, ffn_gain, post_ffn_gain, query_gain, key_gain)
        ],
        axis=1,
    )
    gains = jnp.pad(gains, ((0, 0), (0, 128 - gains.shape[1])))
    cut = 640
    first = jnp.concatenate(
        [query_weight, key_weight, value_weight, gains, gate_weight[:, :cut], up_weight[:, :cut]], 1
    )
    second = jnp.concatenate([gate_weight[:, cut:], up_weight[:, cut:]], 1)
    third = jnp.concatenate([output_weight, down_weight], 0)

    def dense(value):
        return value.reshape(80, value.shape[-1])

    first = gather_part(first, FIRST_ORDER, dense).reshape(640, -1)
    second = gather_part(second, SECOND_ORDER, dense).reshape(640, -1)
    third = gather_part(third, THIRD_ORDER, lambda value: value.reshape(16, 24, 640))
    third = third.reshape(128, 24, 640)
    first_pick = selection(FIRST_ORDER, 5)
    second_pick = selection(SECOND_ORDER, 5)
    out_pick = selection(THIRD_ORDER, 8)
    down_pick = selection(THIRD_ORDER, 16)
    first = low_product(first_pick, first)
    second = low_product(second_pick, second)
    output_full = low_product(out_pick, third[:, :8].reshape(1024, 640))
    down_full = low_product(down_pick, third[:, 8:].reshape(2048, 640))
    head_gains = first.reshape(128, 5, -1)[:, :2, 1540:1542].reshape(256, 2)
    weights = (
        first[:, 1536],
        first[:, :1024],
        first[:, 1024:1280],
        first[:, 1280:1536],
        head_gains[:, 0],
        head_gains[:, 1],
        output_full,
        first[:, 1537],
        first[:, 1538],
        jnp.concatenate([first[:, 1664 : 1664 + cut], second[:, : 2048 - cut]], 1),
        jnp.concatenate([first[:, 1664 + cut :], second[:, 2048 - cut :]], 1),
        down_full,
        first[:, 1539],
    )
    positions = lax.axis_index("seq") * block_size + jnp.arange(block_size, dtype=jnp.int32)
    positions = jnp.broadcast_to(positions[None], (rows, block_size))
    output, kept_values = forward_pass(
        hidden_in.reshape(rows, block_size, model_width),
        positions,
        segment_ids.reshape(rows, block_size),
        weights,
    )
    input_grad, grads = backward_pass(
        cotangent.reshape(rows, block_size, model_width), kept_values, weights
    )
    head_grads = jnp.pad(
        jnp.stack([grads[4], grads[5]], -1).reshape(128, 2, 2), ((0, 0), (0, 3), (0, 0))
    ).reshape(640, 2)
    gain_grads = jnp.stack([grads[0], grads[7], grads[8], grads[12]], -1)
    gain_grads = jnp.concatenate([gain_grads, head_grads], 1)
    gain_grads = jnp.pad(gain_grads, ((0, 0), (0, 122)))
    grad_first = jnp.concatenate(
        [grads[1], grads[2], grads[3], gain_grads, grads[9][:, :cut], grads[10][:, :cut]], 1
    ).astype(jnp.bfloat16)
    grad_second = jnp.concatenate([grads[9][:, cut:], grads[10][:, cut:]], 1).astype(jnp.bfloat16)
    grad_first = low_product(first_pick.T, grad_first).reshape(2, 4, 80, -1)
    grad_second = low_product(second_pick.T, grad_second).reshape(2, 4, 80, -1)
    grad_output = low_product(out_pick.T, grads[6].astype(jnp.bfloat16)).reshape(128, 8, 640)
    grad_down = low_product(down_pick.T, grads[11].astype(jnp.bfloat16)).reshape(128, 16, 640)
    grad_third = jnp.concatenate([grad_output, grad_down], 1).reshape(2, 4, 16, 24, 640)

    def loose(value):
        return value.reshape(4, 4, 5, value.shape[-1])

    grad_first = scatter_part(grad_first, FIRST_ORDER, loose)
    grad_second = scatter_part(grad_second, SECOND_ORDER, loose)
    grad_third = scatter_part(grad_third, THIRD_ORDER, lambda value: value.reshape(4, 4, 24, 640))
    return (
        output.reshape(hidden_in.shape),
        input_grad.reshape(hidden_in.shape),
        grad_first[:, 1536],
        grad_first[:, :1024],
        grad_first[:, 1024:1280],
        grad_first[:, 1280:1536],
        grad_first[:2, 1540],
        grad_first[:2, 1541],
        grad_third[:8],
        grad_first[:, 1537],
        grad_first[:, 1538],
        jnp.concatenate([grad_first[:, 1664 : 1664 + cut], grad_second[:, : 2048 - cut]], 1),
        jnp.concatenate([grad_first[:, 1664 + cut :], grad_second[:, 2048 - cut :]], 1),
        grad_third[8:],
        grad_first[:, 1539],
    )


def solution(mesh):
    return jax.shard_map(
        on_device,
        mesh=mesh,
        in_specs=(
            P(None, "dp", "seq", None),
            P(None, "dp", "seq"),
            P(None, "dp", "seq", None),
            P(("dp", "seq")),
            P(("dp", "seq"), None),
            P(("dp", "seq"), None),
            P(("dp", "seq"), None),
            P(("dp", "seq")),
            P(("dp", "seq")),
            P(("dp", "seq"), None),
            P(("dp", "seq")),
            P(("dp", "seq")),
            P(("dp", "seq"), None),
            P(("dp", "seq"), None),
            P(("dp", "seq"), None),
            P(("dp", "seq")),
        ),
        out_specs=(
            P(None, "dp", "seq", None),
            P(None, "dp", "seq", None),
            P(("dp", "seq")),
            P(("dp", "seq"), None),
            P(("dp", "seq"), None),
            P(("dp", "seq"), None),
            P(("dp", "seq")),
            P(("dp", "seq")),
            P(("dp", "seq"), None),
            P(("dp", "seq")),
            P(("dp", "seq")),
            P(("dp", "seq"), None),
            P(("dp", "seq"), None),
            P(("dp", "seq"), None),
            P(("dp", "seq")),
        ),
        check_vma=False,
    )
```

```python
import functools
import math

import jax
import jax.numpy as jnp
from jax import lax
from jax.experimental import pallas as pl
from jax.experimental.pallas import tpu as pltpu
from jax.sharding import PartitionSpec as P

WINDOW = 512
HALO = 4
BLOCK = 128
ROWS = 4
TOKENS = 512
WIDTH = 640
HEADS = 4
HEAD = 256
HIDDEN = 2048
SPAN = (HALO + 1) * BLOCK
CHUNK = 512
EPSILON = 1e-06
ROPE_BASE = 10000.0
MASKED = -1e30
SCALE = HEAD ** (-0.5)
F32 = jnp.float32
BF16 = jnp.bfloat16

AXES = ("dp", "seq")
SIZE = {"x": 4, "y": 4, "z": 4, "c": 2}
ORDERS = (("z", "y", "x"), ("z", "x", "y"))
ATT_COLS = 896
OUT_COLS = 384
ATT_PACK = ATT_COLS + OUT_COLS


def shard_of(z, y, x, c):
    return z * 32 + (y % 2) * 16 + (y // 2) * 8 + x * 2 + c


def moved(axis_of_core, by):
    pairs = []
    for z in range(4):
        for y in range(4):
            for x in range(4):
                for c in range(2):
                    place = {"z": z, "y": y, "x": x, "c": c}
                    axis = axis_of_core[c]
                    place[axis] = (place[axis] + by) % SIZE[axis]
                    pairs.append((shard_of(z, y, x, c), shard_of(**place)))
    return pairs


def send(value, phase, by):
    axes = (ORDERS[0][phase], ORDERS[1][phase])
    return lax.ppermute(value, AXES, moved(axes, by))


def swap(value):
    return lax.ppermute(value, AXES, moved(("c", "c"), 1))


def shift_seq(value, by):
    pairs = []
    for dp in range(8):
        for seq in range(16):
            if 0 <= seq + by < 16:
                pairs.append((dp * 16 + seq, dp * 16 + seq + by))
    return lax.ppermute(value, AXES, pairs)


def my_place():
    dp, seq = lax.axis_index("dp"), lax.axis_index("seq")
    return {"z": dp // 2, "y": (seq // 8) * 2 + dp % 2, "x": (seq // 2) % 4, "c": seq % 2}


def arrived(value, phase):
    return [value] + [send(value, phase, -by) for by in range(1, 4)]


def collect(pieces, phase):
    total = pieces[0].astype(F32)
    for by in range(1, 4):
        total = total + send(pieces[by], phase, by).astype(F32)
    return total


def chip_table(order):
    me = my_place()
    grid = jnp.arange(64, dtype=jnp.int32)
    place = {
        order[2]: (me[order[2]] + grid // 16) % 4,
        order[1]: (me[order[1]] + grid // 4) % 4,
        order[0]: (me[order[0]] + grid) % 4,
        "c": 0,
    }
    return shard_of(**place) // 2


def row_index(chips, rows_held):
    shards = chips[:, None] * 2 + jnp.arange(2, dtype=jnp.int32)[None]
    row = jnp.arange(rows_held, dtype=jnp.int32)
    natural = jnp.where(row < 5, shards[:, :, None] * 5 + row, -1)
    head = jnp.where(row < 2, shards[:, :, None] * 2 + row, -1)
    return natural.reshape(1, -1), head.reshape(1, -1)


def dot(a, b):
    return jnp.dot(a, b, preferred_element_type=F32)


def dot_nt(a, b):
    return lax.dot_general(a, b, (((1,), (1,)), ((), ())), preferred_element_type=F32)


def dot_tn(a, b):
    return lax.dot_general(a, b, (((0,), (0,)), ((), ())), preferred_element_type=F32)


def one_hot(index_row, count):
    places = lax.broadcasted_iota(jnp.int32, (count, index_row.shape[1]), 0)
    return jnp.where(places == index_row, 1.0, 0.0).astype(BF16)


def inverse_rms(values):
    return lax.rsqrt(jnp.mean(values * values, -1, keepdims=True) + EPSILON)


def norm_backward(grad_hat, unit_value, inverse):
    return inverse * (grad_hat - unit_value * jnp.mean(grad_hat * unit_value, -1, keepdims=True))


def rotate(values, cosine, sine):
    first, second = values[:, : HEAD // 2], values[:, HEAD // 2 :]
    return jnp.concatenate(
        [first * cosine - second * sine, second * cosine + first * sine], axis=-1
    )


def attention_kernel(
    meta, nat_a, nat_b, head_b, cosine, sine, own_segments, all_segments, hidden, *refs
):
    halos, own, other = refs[:4], refs[4:8], refs[8:12]
    (
        attended_ref,
        probs_ref,
        queries_ref,
        keys_ref,
        values_ref,
        query_pre_ref,
        key_pre_ref,
        normed_ref,
        weights_ref,
        output_weight_ref,
        gains_ref,
        head_gains_ref,
    ) = refs[12:24]
    part_a, part_b, gains_s, head_gains_s, weights_s = refs[24:]
    row = pl.program_id(0)

    @pl.when(row == 0)
    def _():
        first_core = meta[128] == 0

        @pl.when(first_core)
        def _():
            for j in range(4):
                part_a[j * 256 : (j + 1) * 256] = own[j][...]
                part_b[j * 256 : (j + 1) * 256] = other[j][...]

        @pl.when(jnp.logical_not(first_core))
        def _():
            for j in range(4):
                part_a[j * 256 : (j + 1) * 256] = other[j][...]
                part_b[j * 256 : (j + 1) * 256] = own[j][...]

        pick_a = one_hot(nat_a[...], WIDTH)
        pick_b = one_hot(nat_b[...], WIDTH)
        pick_h = one_hot(head_b[...], HEAD)
        weights_s[:, :ATT_COLS] = dot(pick_a, part_a[:, :ATT_COLS]).astype(BF16)
        weights_s[:, ATT_COLS:] = dot(pick_b, part_b[:, :WIDTH]).astype(BF16)
        weights_ref[...] = weights_s[...]
        gain_block = part_b[:, WIDTH : WIDTH + 128]
        gains = lax.dot_general(
            gain_block, pick_b, (((0,), (1,)), ((), ())), preferred_element_type=F32
        )[:8]
        head_gains = lax.dot_general(
            gain_block, pick_h, (((0,), (1,)), ((), ())), preferred_element_type=F32
        )[:8]
        gains_s[...] = gains
        gains_ref[...] = gains
        head_gains_s[...] = head_gains
        head_gains_ref[...] = head_gains

        def place(i, carry):
            output_weight_ref[meta[i], :, :OUT_COLS] = part_a[
                pl.ds(pl.multiple_of(i * 16, 16), 16), ATT_COLS:
            ]
            output_weight_ref[meta[64 + i], :, OUT_COLS:] = part_b[
                pl.ds(pl.multiple_of(i * 16, 16), 16), ATT_COLS : ATT_COLS + WIDTH - OUT_COLS
            ]
            return carry

        lax.fori_loop(0, 64, place, 0)

    tokens = jnp.concatenate([halo[...] for halo in halos] + [hidden[0]], 0).astype(F32)
    normed = (tokens * inverse_rms(tokens) * gains_s[0:1]).astype(BF16)
    normed_ref[0] = normed
    key_value = dot(normed, weights_s[:, HEADS * HEAD :])
    key_pre = key_value[:, :HEAD]
    values = key_value[:, HEAD:].astype(BF16)
    query_pre = dot(normed[HALO * BLOCK :], weights_s[:, : HEADS * HEAD])
    key_pre_ref[0] = key_pre
    query_pre_ref[0] = query_pre
    values_ref[0] = values
    keys = rotate(
        key_pre * inverse_rms(key_pre) * head_gains_s[5:6], cosine[...], sine[...]
    ).astype(BF16)
    keys_ref[0] = keys
    cosine_own, sine_own = cosine[HALO * BLOCK :], sine[HALO * BLOCK :]
    queries = []
    for h in range(HEADS):
        pre = query_pre[:, h * HEAD : (h + 1) * HEAD]
        queries.append(
            rotate(pre * inverse_rms(pre) * head_gains_s[4:5], cosine_own, sine_own).astype(BF16)
        )
    queries = jnp.concatenate(queries, 0)
    queries_ref[0] = queries
    query_place = lax.broadcasted_iota(jnp.int32, (BLOCK, SPAN), 0)
    key_place = lax.broadcasted_iota(jnp.int32, (BLOCK, SPAN), 1) - HALO * BLOCK
    visible = (
        (key_place <= query_place)
        & (query_place - key_place < WINDOW)
        & (key_place + meta[129] >= 0)
        & (own_segments[0] == all_segments[0])
    )
    bias = jnp.where(visible, 0.0, MASKED)
    bias = jnp.concatenate([bias] * HEADS, 0)
    scores = dot_nt(queries, keys) * SCALE
    scores = jnp.where(bias == 0.0, scores, MASKED)
    terms = jnp.exp(scores - jnp.max(scores, -1, keepdims=True))
    probs = (terms / jnp.sum(terms, -1, keepdims=True)).astype(BF16)
    probs_ref[0] = probs
    attended = dot(probs, values).astype(BF16)
    for h in range(HEADS):
        attended_ref[0, :, h * HEAD : (h + 1) * HEAD] = attended[h * BLOCK : (h + 1) * BLOCK]


def whole(shape):
    return pl.BlockSpec(shape, lambda r: (0,) * len(shape))


def by_row(shape):
    return pl.BlockSpec((1,) + shape, lambda r: (r,) + (0,) * len(shape))


def smem():
    return pl.BlockSpec(memory_space=pltpu.SMEM)


def params(megabytes=60):
    return pltpu.CompilerParams(vmem_limit_bytes=megabytes * 2**20)


def attention_forward(meta, index, tables, segments, hidden, halos, own, other):
    slab = whole((256, ATT_PACK))
    halo_spec = pl.BlockSpec((BLOCK, WIDTH), lambda r: (r, 0))
    outs = [
        ((ROWS, BLOCK, HEADS * HEAD), BF16),
        ((ROWS, HEADS * BLOCK, SPAN), BF16),
        ((ROWS, HEADS * BLOCK, HEAD), BF16),
        ((ROWS, SPAN, HEAD), BF16),
        ((ROWS, SPAN, HEAD), BF16),
        ((ROWS, BLOCK, HEADS * HEAD), F32),
        ((ROWS, SPAN, HEAD), F32),
        ((ROWS, SPAN, WIDTH), BF16),
    ]
    fixed = [
        ((WIDTH, 1536), BF16),
        ((64, 16, WIDTH), BF16),
        ((8, WIDTH), F32),
        ((8, HEAD), F32),
    ]
    return pl.pallas_call(
        attention_kernel,
        grid=(ROWS,),
        out_shape=[jax.ShapeDtypeStruct(s, d) for s, d in outs + fixed],
        in_specs=[smem()]
        + [whole((1, 1024))] * 3
        + [whole((SPAN, HEAD // 2))] * 2
        + [by_row((BLOCK, 1)), by_row((1, SPAN)), by_row((BLOCK, WIDTH))]
        + [halo_spec] * 4
        + [slab] * 8,
        out_specs=[by_row(s[1:]) for s, _ in outs] + [whole(s) for s, _ in fixed],
        scratch_shapes=[
            pltpu.VMEM((1024, ATT_PACK), BF16),
            pltpu.VMEM((1024, ATT_PACK), BF16),
            pltpu.VMEM((8, WIDTH), F32),
            pltpu.VMEM((8, HEAD), F32),
            pltpu.VMEM((WIDTH, 1536), BF16),
        ],
        compiler_params=params(),
        cost_estimate=pl.CostEstimate(
            flops=10**10, bytes_accessed=25 * 10**6, transcendentals=2 * 10**6
        ),
        name="attention_forward",
    )(meta, *index, *tables, *segments, hidden, *halos, *own, *other)


def gelu_parts(gate):
    square = gate * gate
    slope = 0.7978845608 * (1.0 + 0.044715 * square)
    bent = jnp.tanh(gate * slope)
    return square, bent


def feed_kernel(
    meta, nat_a, nat_b, hidden, cotangent, attended, output_weight, gains, *refs
):
    own, other = refs[:4], refs[4:8]
    own_down, other_down = refs[8:12], refs[12:16]
    (
        block_out_ref,
        middle_grad_ref,
        attended_grad_ref,
        grad_output_ref,
        keep_ref,
        give_ref,
        keep_down_ref,
        give_down_ref,
        gain_grads_ref,
    ) = refs[16:25]
    gate_w, up_w, down_w, gate_s, up_s, inner_s, down_s, grad_down, arrivals = refs[25:]
    first_core = meta[128] == 0
    core = meta[128]

    def fetch(sources, target, first):
        return [
            pltpu.make_async_copy(
                sources[j], target.at[j * 160 : (j + 1) * 160], arrivals.at[first + j]
            )
            for j in range(4)
        ]

    @pl.when(first_core)
    def _():
        for copy in fetch(own, gate_w, 0) + fetch(other, up_w, 4):
            copy.start()

    @pl.when(jnp.logical_not(first_core))
    def _():
        for copy in fetch(other, gate_w, 0) + fetch(own, up_w, 4):
            copy.start()

    def shard_own(i):
        return meta[core * 64 + i] * 2 + core

    def shard_other(i):
        return meta[(1 - core) * 64 + i] * 2 + 1 - core

    for j in range(4):

        def place(i, carry, j=j):
            down_w[shard_own(j * 16 + i)] = own_down[j][i]
            down_w[shard_other(j * 16 + i)] = other_down[j][i]
            return carry

        lax.fori_loop(0, 16, place, 0)

    pick_a = one_hot(nat_a[...], WIDTH)
    pick_b = one_hot(nat_b[...], WIDTH)
    projected = dot(attended[...], output_weight[...])
    proj_inverse = inverse_rms(projected)
    proj_unit = projected * proj_inverse
    middle = hidden[...].astype(F32) + proj_unit * gains[1:2]
    mid_inverse = inverse_rms(middle)
    mid_unit = middle * mid_inverse
    ffn_in = (mid_unit * gains[2:3]).astype(BF16)
    input_a = dot(ffn_in, pick_a).astype(BF16)
    input_b = dot(ffn_in, pick_b).astype(BF16)

    def pick(value_first, value_second):
        return jnp.where(first_core, value_first, value_second)

    input_kept, input_given = pick(input_a, input_b), pick(input_b, input_a)
    down_s[...] = jnp.zeros_like(down_s)
    for copy in fetch(own, gate_w, 0) + fetch(own, up_w, 4):
        copy.wait()

    def forward(n, carry):
        columns = pl.ds(pl.multiple_of(n * CHUNK, CHUNK), CHUNK)
        gate = dot(input_a, gate_w[:, columns])
        up = dot(input_b, up_w[:, columns])
        gate_s[:, columns] = gate
        up_s[:, columns] = up
        _, bent = gelu_parts(gate)
        inner = (0.5 * gate * (1.0 + bent) * up).astype(BF16)
        inner_s[:, columns] = inner
        rows = down_w[pl.ds(pl.multiple_of(n * (CHUNK // 16), CHUNK // 16), CHUNK // 16)]
        down_s[...] += dot(inner, rows.reshape(CHUNK, WIDTH))
        return carry

    lax.fori_loop(0, HIDDEN // CHUNK, forward, 0)
    down = down_s[...]
    down_inverse = inverse_rms(down)
    down_unit = down * down_inverse
    block_out_ref[...] = (middle + down_unit * gains[3:4]).astype(BF16)
    out_grad = cotangent[...].astype(F32)
    grad_post_ffn = jnp.sum(out_grad * down_unit, 0, keepdims=True)
    down_grad = norm_backward(out_grad * gains[3:4], down_unit, down_inverse).astype(BF16)
    down_s[...] = jnp.zeros_like(down_s)

    def backward(n, carry):
        columns = pl.ds(pl.multiple_of(n * CHUNK, CHUNK), CHUNK)
        blocks = pl.ds(pl.multiple_of(n * (CHUNK // 16), CHUNK // 16), CHUNK // 16)
        inner_grad = dot_nt(down_grad, down_w[blocks].reshape(CHUNK, WIDTH))
        gate = gate_s[:, columns]
        square, bent = gelu_parts(gate)
        half = 0.5 * (1.0 + bent)
        slope = half + (0.5 * 0.7978845608) * gate * (1.0 - bent * bent) * (
            1.0 + (3 * 0.044715) * square
        )
        up_grad = (inner_grad * (gate * half)).astype(BF16)
        gate_grad = (inner_grad * up_s[:, columns] * slope).astype(BF16)
        grad_down[blocks] = (
            dot_tn(inner_s[:, columns], down_grad).astype(BF16).reshape(CHUNK // 16, 16, WIDTH)
        )
        kept, given = pick(gate_grad, up_grad), pick(up_grad, gate_grad)
        keep_ref[:, columns] = dot_tn(input_kept, kept).astype(BF16)
        give_ref[:, columns] = dot_tn(input_given, given).astype(BF16)
        part_a = dot_nt(gate_grad, gate_w[:, columns])
        part_b = dot_nt(up_grad, up_w[:, columns])
        down_s[...] += dot_nt(part_a.astype(BF16), pick_a) + dot_nt(part_b.astype(BF16), pick_b)
        return carry

    lax.fori_loop(0, HIDDEN // CHUNK, backward, 0)

    def hand(i, carry):
        keep_down_ref[i] = grad_down[shard_own(i)]
        give_down_ref[i] = grad_down[shard_other(i)]
        return carry

    lax.fori_loop(0, 64, hand, 0)
    ffn_in_grad = down_s[...]
    grad_ffn = jnp.sum(ffn_in_grad * mid_unit, 0, keepdims=True)
    middle_grad = out_grad + norm_backward(ffn_in_grad * gains[2:3], mid_unit, mid_inverse)
    middle_grad_ref[...] = middle_grad
    grad_post_attn = jnp.sum(middle_grad * proj_unit, 0, keepdims=True)
    proj_grad = norm_backward(middle_grad * gains[1:2], proj_unit, proj_inverse).astype(BF16)
    grad_output_ref[...] = (
        dot_tn(attended[...], proj_grad).astype(BF16).reshape(64, 16, WIDTH)
    )
    attended_grad_ref[...] = dot_nt(proj_grad, output_weight[...]).astype(BF16)
    gain_grads_ref[...] = jnp.concatenate(
        [
            jnp.zeros((1, WIDTH), F32),
            grad_post_attn,
            grad_ffn,
            grad_post_ffn,
            jnp.zeros((4, WIDTH), F32),
        ],
        0,
    )


def feed_forward(meta, index, hidden, cotangent, attended, output_weight, gains, own, other, own_down, other_down):
    outs = [
        ((TOKENS, WIDTH), BF16),
        ((TOKENS, WIDTH), F32),
        ((TOKENS, HEADS * HEAD), BF16),
        ((64, 16, WIDTH), BF16),
        ((WIDTH, HIDDEN), BF16),
        ((WIDTH, HIDDEN), BF16),
        ((64, 16, WIDTH), BF16),
        ((64, 16, WIDTH), BF16),
        ((8, WIDTH), F32),
    ]
    vmem = pl.BlockSpec(memory_space=pltpu.VMEM)
    return pl.pallas_call(
        feed_kernel,
        out_shape=[jax.ShapeDtypeStruct(s, d) for s, d in outs],
        in_specs=[smem()]
        + [vmem] * 7
        + [pl.BlockSpec(memory_space=pl.ANY)] * 8
        + [vmem] * 8,
        out_specs=[vmem] * len(outs),
        scratch_shapes=[
            pltpu.VMEM((WIDTH, HIDDEN), BF16),
            pltpu.VMEM((WIDTH, HIDDEN), BF16),
            pltpu.VMEM((128, 16, WIDTH), BF16),
            pltpu.VMEM((TOKENS, HIDDEN), F32),
            pltpu.VMEM((TOKENS, HIDDEN), F32),
            pltpu.VMEM((TOKENS, HIDDEN), BF16),
            pltpu.VMEM((TOKENS, WIDTH), F32),
            pltpu.VMEM((128, 16, WIDTH), BF16),
            pltpu.SemaphoreType.DMA((8,)),
        ],
        compiler_params=params(),
        cost_estimate=pl.CostEstimate(
            flops=2 * 10**10, bytes_accessed=25 * 10**6, transcendentals=2 * 10**6
        ),
        name="feed_forward",
    )(meta, *index, hidden, cotangent, attended, output_weight, gains, *own, *other, *own_down, *other_down)


def attention_back_kernel(
    meta,
    nat_a,
    nat_b,
    head_b,
    cosine,
    sine,
    hidden,
    halo4,
    halo3,
    halo2,
    halo1,
    attended_grad,
    probs,
    queries,
    keys,
    values,
    query_pre,
    key_pre,
    normed,
    weights,
    gains,
    head_gains,
    feed_gain_grads,
    grad_output,
    own_ref,
    out4,
    out3,
    out2,
    out1,
    keep_ref,
    give_ref,
    query_grads,
    normed_own,
    key_value_total,
    gain_total,
    head_total,
    part_a,
    part_b,
):
    row = pl.program_id(0)

    @pl.when(row == 0)
    def _():
        key_value_total[...] = jnp.zeros_like(key_value_total)
        gain_total[...] = feed_gain_grads[...]
        head_total[...] = jnp.zeros_like(head_total)

    mixed_grad = jnp.concatenate(
        [attended_grad[0, :, h * HEAD : (h + 1) * HEAD] for h in range(HEADS)], 0
    )
    prob_grad = dot_nt(mixed_grad, values[0])
    soft = probs[0].astype(F32)
    row_dot = jnp.sum(soft * prob_grad, -1, keepdims=True)
    score_grad = (soft * (prob_grad - row_dot)).astype(BF16)
    query_grad = dot(score_grad, keys[0]) * SCALE
    key_grad = dot_tn(score_grad, queries[0]) * SCALE
    value_grad = dot_tn(probs[0], mixed_grad).astype(BF16)
    cosine_own, sine_own = cosine[HALO * BLOCK :], -sine[HALO * BLOCK :]
    query_gain, key_gain = head_gains[4:5], head_gains[5:6]
    query_gain_grad = jnp.zeros((1, HEAD), F32)
    pre_grads = []
    for h in range(HEADS):
        pre = query_pre[0, :, h * HEAD : (h + 1) * HEAD]
        inverse = inverse_rms(pre)
        unit = pre * inverse
        turned = rotate(query_grad[h * BLOCK : (h + 1) * BLOCK], cosine_own, sine_own)
        query_gain_grad += jnp.sum(turned * unit, 0, keepdims=True)
        pre_grads.append(norm_backward(turned * query_gain, unit, inverse).astype(BF16))
    query_pre_grad = jnp.concatenate(pre_grads, 1)
    pre = key_pre[0]
    inverse = inverse_rms(pre)
    unit = pre * inverse
    turned = rotate(key_grad, cosine[...], -sine[...])
    key_gain_grad = jnp.sum(turned * unit, 0, keepdims=True)
    key_pre_grad = norm_backward(turned * key_gain, unit, inverse).astype(BF16)
    head_total[4:5] += query_gain_grad
    head_total[5:6] += key_gain_grad
    key_value_grad = jnp.concatenate([key_pre_grad, value_grad], 1)
    key_value_total[...] += dot_tn(normed[0], key_value_grad)
    rows = pl.ds(pl.multiple_of(row * BLOCK, BLOCK), BLOCK)
    query_grads[rows] = query_pre_grad
    normed_own[rows] = normed[0, HALO * BLOCK :]
    normed_grad = dot_nt(key_value_grad, weights[:, HEADS * HEAD :])
    own = normed_grad[HALO * BLOCK :] + dot_nt(query_pre_grad, weights[:, : HEADS * HEAD])
    own_ref[0] = own
    for j, out in enumerate((out4, out3, out2, out1)):
        out[...] = normed_grad[j * BLOCK : (j + 1) * BLOCK].astype(BF16)
    tokens = jnp.concatenate([halo4[...], halo3[...], halo2[...], halo1[...]], 0).astype(F32)
    unit_in = tokens * inverse_rms(tokens)
    own_tokens = hidden[0].astype(F32)
    own_unit = own_tokens * inverse_rms(own_tokens)
    gain_total[0:1] += jnp.sum(unit_in * normed_grad[: HALO * BLOCK], 0, keepdims=True) + jnp.sum(
        own_unit * own, 0, keepdims=True
    )

    @pl.when(row == ROWS - 1)
    def _():
        pick_a = one_hot(nat_a[...], WIDTH)
        pick_b = one_hot(nat_b[...], WIDTH)
        pick_h = one_hot(head_b[...], HEAD)
        query_total = dot_tn(normed_own[...], query_grads[...]).astype(BF16)
        part_a[:, :ATT_COLS] = dot_tn(pick_a, query_total[:, :ATT_COLS]).astype(BF16)
        part_b[:, :128] = dot_tn(pick_b, query_total[:, ATT_COLS:]).astype(BF16)
        part_b[:, 128:WIDTH] = dot_tn(pick_b, key_value_total[...].astype(BF16)).astype(BF16)
        blank = jnp.zeros((120, WIDTH), F32)
        gain_rows = jnp.concatenate([gain_total[...], blank], 0).astype(BF16)
        head_rows = jnp.concatenate([head_total[...], blank[:, :HEAD]], 0).astype(BF16)
        gain_block = lax.dot_general(
            pick_b, gain_rows, (((0,), (1,)), ((), ())), preferred_element_type=F32
        ) + lax.dot_general(
            pick_h, head_rows, (((0,), (1,)), ((), ())), preferred_element_type=F32
        )
        part_b[:, WIDTH : WIDTH + 128] = gain_block.astype(BF16)
        part_b[:, WIDTH + 128 :] = jnp.zeros((1024, ATT_PACK - WIDTH - 128), BF16)

        def place(i, carry):
            here = pl.ds(pl.multiple_of(i * 16, 16), 16)
            part_a[here, ATT_COLS:] = grad_output[meta[i], :, :OUT_COLS]
            part_b[here, ATT_COLS : ATT_COLS + WIDTH - OUT_COLS] = grad_output[
                meta[64 + i], :, OUT_COLS:
            ]
            return carry

        lax.fori_loop(0, 64, place, 0)
        first_core = meta[128] == 0

        @pl.when(first_core)
        def _():
            keep_ref[...] = part_a[...]
            give_ref[...] = part_b[...]

        @pl.when(jnp.logical_not(first_core))
        def _():
            keep_ref[...] = part_b[...]
            give_ref[...] = part_a[...]


def attention_backward(meta, index, tables, hidden, halos, attended_grad, saved, fixed, grad_output):
    halo_spec = pl.BlockSpec((BLOCK, WIDTH), lambda r: (r, 0))
    pack = whole((1024, ATT_PACK))
    return pl.pallas_call(
        attention_back_kernel,
        grid=(ROWS,),
        out_shape=[jax.ShapeDtypeStruct((ROWS, BLOCK, WIDTH), F32)]
        + [jax.ShapeDtypeStruct((TOKENS, WIDTH), BF16)] * 4
        + [jax.ShapeDtypeStruct((1024, ATT_PACK), BF16)] * 2,
        in_specs=[smem()]
        + [whole((1, 1024))] * 3
        + [whole((SPAN, HEAD // 2))] * 2
        + [by_row((BLOCK, WIDTH))]
        + [halo_spec] * 4
        + [
            by_row((BLOCK, HEADS * HEAD)),
            by_row((HEADS * BLOCK, SPAN)),
            by_row((HEADS * BLOCK, HEAD)),
            by_row((SPAN, HEAD)),
            by_row((SPAN, HEAD)),
            by_row((BLOCK, HEADS * HEAD)),
            by_row((SPAN, HEAD)),
            by_row((SPAN, WIDTH)),
            whole((WIDTH, 1536)),
            whole((8, WIDTH)),
            whole((8, HEAD)),
            whole((8, WIDTH)),
            whole((64, 16, WIDTH)),
        ],
        out_specs=[by_row((BLOCK, WIDTH))] + [halo_spec] * 4 + [pack] * 2,
        scratch_shapes=[
            pltpu.VMEM((TOKENS, HEADS * HEAD), BF16),
            pltpu.VMEM((TOKENS, WIDTH), BF16),
            pltpu.VMEM((WIDTH, 2 * HEAD), F32),
            pltpu.VMEM((8, WIDTH), F32),
            pltpu.VMEM((8, HEAD), F32),
            pltpu.VMEM((1024, ATT_PACK), BF16),
            pltpu.VMEM((1024, ATT_PACK), BF16),
        ],
        compiler_params=params(),
        cost_estimate=pl.CostEstimate(
            flops=15 * 10**9, bytes_accessed=25 * 10**6, transcendentals=10**4
        ),
        name="attention_backward",
    )(meta, *index, *tables, hidden, *halos, attended_grad, *saved, *fixed, grad_output)


def padded_rows(value):
    return jnp.pad(value, ((0, 8 - value.shape[0]), (0, 0)))


def on_device(
    hidden_in,
    segment_ids,
    cotangent,
    attn_gain,
    query_weight,
    key_weight,
    value_weight,
    query_gain,
    key_gain,
    output_weight,
    post_attn_gain,
    ffn_gain,
    gate_weight,
    up_weight,
    down_weight,
    post_ffn_gain,
):
    me = my_place()
    core = me["c"]
    first_core = core == 0
    place = lax.axis_index("seq") * BLOCK

    def pick(value_first, value_second):
        return jnp.where(first_core, value_first, value_second)

    hidden = hidden_in.reshape(ROWS, BLOCK, WIDTH)
    segments = segment_ids.reshape(ROWS, BLOCK)
    segment_rows = jnp.pad(segments.astype(BF16), ((0, 12), (0, WIDTH - BLOCK)))
    block = jnp.concatenate([hidden.reshape(TOKENS, WIDTH), segment_rows], 0)
    two_back = shift_seq(block, 2)
    four_back = shift_seq(two_back, 2)
    crossed = swap(two_back)
    mixed = swap(pick(block, four_back))
    one_back = pick(crossed, mixed)
    three_back = pick(mixed, crossed)
    halos = [four_back, three_back, two_back, one_back]
    all_segments = jnp.concatenate(
        [halo[TOKENS : TOKENS + ROWS, :BLOCK].astype(F32) for halo in halos]
        + [segments.astype(F32)],
        1,
    ).reshape(ROWS, 1, SPAN)
    own_segments = segments.astype(F32).reshape(ROWS, BLOCK, 1)

    gains = jnp.concatenate(
        [
            jnp.pad(gain, (0, 5 - gain.shape[0]))[:, None]
            for gain in (attn_gain, post_attn_gain, ffn_gain, post_ffn_gain, query_gain, key_gain)
        ],
        1,
    )
    head_cut = ATT_COLS
    second = jnp.concatenate([query_weight[:, head_cut:], key_weight, value_weight, gains], 1)
    second = jnp.pad(second, ((0, 0), (0, ATT_COLS - second.shape[1])))
    out_second = jnp.pad(output_weight[:, OUT_COLS:], ((0, 0), (0, 2 * OUT_COLS - WIDTH)))
    pack_a = jnp.concatenate(
        [padded_rows(query_weight[:, :head_cut]), output_weight[:, :OUT_COLS], padded_rows(gate_weight)],
        1,
    )
    pack_b = jnp.concatenate([padded_rows(second), out_second, padded_rows(up_weight)], 1)
    kept = pick(pack_a, pack_b)
    received = swap(pick(pack_b, pack_a))
    pair = jnp.concatenate([pick(kept, received), pick(received, kept)], 0)
    packed = jnp.concatenate([pair, down_weight], 1)
    packed = jnp.stack(arrived(packed, 0))
    packed = jnp.stack(arrived(packed, 1))
    att_slab = packed[..., :ATT_PACK].reshape(256, ATT_PACK)
    feed_slab = packed[..., ATT_PACK : ATT_PACK + HIDDEN].reshape(16, 2, 8, HIDDEN)
    feed_slab = feed_slab[:, :, :5].reshape(160, HIDDEN)
    down_slab = packed[..., ATT_PACK + HIDDEN :].reshape(16, 16, WIDTH)
    att_own = arrived(att_slab, 2)
    att_other = [swap(value) for value in att_own]
    feed_own = arrived(feed_slab, 2)
    feed_other = [swap(value) for value in feed_own]
    down_own = arrived(down_slab, 2)
    down_other = [swap(value) for value in down_own]

    chips = [chip_table(order) for order in ORDERS]
    meta = jnp.concatenate(chips + [core[None], place[None]]).astype(jnp.int32)
    nat_a, _ = row_index(chips[0], 8)
    nat_b, head_b = row_index(chips[1], 8)
    dense = [row_index(chip, 5)[0] for chip in chips]
    positions = place + jnp.arange(-HALO * BLOCK, BLOCK, dtype=jnp.int32)
    frequency = jnp.exp(
        jnp.arange(HEAD // 2, dtype=F32) * (-2.0 * math.log(ROPE_BASE) / HEAD)
    )
    angles = positions.astype(F32)[:, None] * frequency[None]
    tables = (jnp.cos(angles), jnp.sin(angles))
    index = (nat_a, nat_b, head_b)

    forward = attention_forward(
        meta, index, tables, (own_segments, all_segments), hidden, halos, att_own, att_other
    )
    attended, saved = forward[0], forward[1:8]
    weights, output_full, gain_rows, head_gains = forward[8:]
    (
        block_out,
        middle_grad,
        attended_grad,
        grad_output,
        keep_feed,
        give_feed,
        keep_down,
        give_down,
        feed_gain_grads,
    ) = feed_forward(
        meta,
        dense,
        hidden.reshape(TOKENS, WIDTH),
        cotangent.reshape(TOKENS, WIDTH),
        attended.reshape(TOKENS, HEADS * HEAD),
        output_full.reshape(HEADS * HEAD, WIDTH),
        gain_rows,
        feed_own,
        feed_other,
        down_own,
        down_other,
    )
    back = attention_backward(
        meta,
        index,
        tables,
        hidden,
        halos,
        attended_grad.reshape(ROWS, BLOCK, HEADS * HEAD),
        saved,
        (weights, gain_rows, head_gains, feed_gain_grads),
        grad_output,
    )
    normed_grad, (to_four, to_three, to_two, to_one), (keep_att, give_att) = (
        back[0],
        back[1:5],
        back[5:7],
    )

    def add_low(a, b):
        return (a.astype(F32) + b.astype(F32)).astype(BF16)

    feed_sum = add_low(keep_feed, swap(give_feed)).reshape(4, 160, HIDDEN)
    down_sum = add_low(keep_down, swap(give_down)).reshape(4, 16, 16, WIDTH)
    feed_sum = collect(feed_sum, 2).reshape(16, 2, 5, HIDDEN)
    feed_sum = jnp.pad(feed_sum, ((0, 0), (0, 0), (0, 3), (0, 0))).reshape(16, 16, HIDDEN)
    down_sum = collect(down_sum, 2)
    both = jnp.concatenate([feed_sum, down_sum], -1).astype(BF16).reshape(4, 4, 16, -1)
    both = collect(both, 1).astype(BF16)
    both = collect(both, 0)
    feed_mine = pick(both[:5, :HIDDEN], both[8:13, :HIDDEN])
    feed_theirs = swap(pick(both[8:13, :HIDDEN], both[:5, :HIDDEN]))
    grad_gate = pick(feed_mine, feed_theirs)
    grad_up = pick(feed_theirs, feed_mine)
    grad_down = both[:, HIDDEN:]

    att_sum = add_low(keep_att, swap(give_att)).reshape(4, 256, ATT_PACK)
    att_sum = collect(att_sum, 2).astype(BF16).reshape(4, 4, 16, ATT_PACK)
    att_sum = collect(att_sum, 1).astype(BF16)
    att_sum = collect(att_sum, 0)
    att_mine = pick(att_sum[:8], att_sum[8:])
    att_theirs = swap(pick(att_sum[8:], att_sum[:8]))
    grad_a = pick(att_mine, att_theirs)
    grad_b = pick(att_theirs, att_mine)
    grad_query = jnp.concatenate([grad_a[:5, :ATT_COLS], grad_b[:5, :128]], 1)
    grad_key = grad_b[:5, 128 : 128 + HEAD]
    grad_value = grad_b[:5, 128 + HEAD : 128 + 2 * HEAD]
    gain_grads = grad_b[:, WIDTH : WIDTH + 6]
    grad_out = jnp.concatenate(
        [grad_a[:, ATT_COLS:], grad_b[:, ATT_COLS : ATT_COLS + WIDTH - OUT_COLS]], 1
    )

    mixed = swap(pick(to_three, to_one))
    crossed = swap(pick(to_one, to_three))
    far = pick(to_four, add_low(to_four, mixed))
    near = add_low(to_two, crossed)
    near = add_low(near, shift_seq(far, -2))
    returned = shift_seq(near, -2).astype(F32) + jnp.where(first_core, mixed.astype(F32), 0.0)
    normed_grad = normed_grad.reshape(TOKENS, WIDTH) + returned
    tokens = hidden.reshape(TOKENS, WIDTH).astype(F32)
    inverse = inverse_rms(tokens)
    input_grad = middle_grad + norm_backward(
        normed_grad * gain_rows[0:1], tokens * inverse, inverse
    )
    return (
        block_out.reshape(hidden_in.shape),
        input_grad.astype(BF16).reshape(hidden_in.shape),
        gain_grads[:5, 0],
        grad_query,
        grad_key,
        grad_value,
        gain_grads[:2, 4],
        gain_grads[:2, 5],
        grad_out,
        gain_grads[:5, 1],
        gain_grads[:5, 2],
        grad_gate,
        grad_up,
        grad_down,
        gain_grads[:5, 3],
    )


def solution(mesh):
    rows = P(None, "dp", "seq", None)
    shard = P(("dp", "seq"), None)
    vector = P(("dp", "seq"))
    return jax.shard_map(
        on_device,
        mesh=mesh,
        in_specs=(rows, P(None, "dp", "seq"), rows)
        + (vector, shard, shard, shard, vector, vector, shard, vector)
        + (vector, shard, shard, shard, vector),
        out_specs=(rows, rows)
        + (vector, shard, shard, shard, vector, vector, shard, vector)
        + (vector, shard, shard, shard, vector),
        check_vma=False,
    )
```

```python
import functools
import math

import jax
import jax.numpy as jnp
from jax import lax
from jax.experimental import pallas as pl
from jax.experimental.pallas import tpu as pltpu
from jax.sharding import PartitionSpec as P

WINDOW = 512
HALO = 4
BLOCK = 128
TOKENS = 512
KEYS = 1024
WIDTH = 640
HEADS = 4
HEAD = 256
HIDDEN = 2048
SPAN = (HALO + 1) * BLOCK
CHUNK = 512
TAGGED = BLOCK + 16
EPSILON = 1e-06
ROPE_BASE = 10000.0
MASKED = -1e30
SCALE = HEAD ** (-0.5)
F32 = jnp.float32
BF16 = jnp.bfloat16

AXES = ("dp", "seq")
SIZE = {"x": 4, "y": 4, "z": 4, "c": 2}
GATHER = (("z", "y", "x"), ("z", "x", "y"))
SCATTER = (("y", "x", "z"), ("y", "z", "x"))
ATT_COLS = 768
OUT_COLS = 384
DOWN_PACK = OUT_COLS + WIDTH
PACK = ATT_COLS + OUT_COLS + HIDDEN


def shard_of(z, y, x, c):
    return z * 32 + (y % 2) * 16 + (y // 2) * 8 + x * 2 + c


def moved(axis_of_core, by):
    pairs = []
    for z in range(4):
        for y in range(4):
            for x in range(4):
                for c in range(2):
                    place = {"z": z, "y": y, "x": x, "c": c}
                    axis = axis_of_core[c]
                    place[axis] = (place[axis] + by) % SIZE[axis]
                    pairs.append((shard_of(z, y, x, c), shard_of(**place)))
    return pairs


def send(value, orders, phase, by):
    axes = (orders[0][phase], orders[1][phase])
    return lax.ppermute(value, AXES, moved(axes, by))


def swap(value):
    return lax.ppermute(value, AXES, moved(("c", "c"), 1))


def exchange(value, flip):
    pairs = []
    for i in range(128):
        pairs.append((i, i ^ (3 if flip else 2)))
    return lax.ppermute(value, AXES, pairs)


def next_chunk(value, back):
    pairs = []
    for dp in range(8):
        for yh in range(2):
            for x in range(4):
                for c in range(2):
                    if x >= 2 and yh == 1:
                        continue
                    here = dp * 16 + yh * 8 + x * 2 + c
                    there = dp * 16 + (yh + (x >= 2)) * 8 + (3 - x) * 2 + c
                    pairs.append((there, here) if back else (here, there))
    return lax.ppermute(value, AXES, pairs)


def my_place():
    dp, seq = lax.axis_index("dp"), lax.axis_index("seq")
    return {"z": dp // 2, "y": (seq // 8) * 2 + dp % 2, "x": (seq // 2) % 4, "c": seq % 2}


def arrived(value, phase):
    two, one, three = [send(value, GATHER, phase, -by) for by in (2, 1, 3)]
    return [one, two, three]


def received(pieces, phase):
    return [send(pieces[by], SCATTER, phase, by) for by in (2, 1, 3)]


def add_up(own, others):
    total = own.astype(F32)
    for other in others:
        total = total + other.astype(F32)
    return total


def chip_at(meta, order, j3, j2, j1):
    place = {
        order[2]: (meta["zyx".index(order[2])] + j3) & 3,
        order[1]: (meta["zyx".index(order[1])] + j2) & 3,
        order[0]: (meta["zyx".index(order[0])] + j1) & 3,
    }
    z, y, x = place["z"], place["y"], place["x"]
    return z * 16 + (y & 1) * 8 + (y >> 1) * 4 + x


def chip_of(meta, order, i):
    return chip_at(meta, order, i >> 4, (i >> 2) & 3, i & 3)


def slab_rows(meta, order, rows_held):
    line = lax.broadcasted_iota(jnp.int32, (1, 128 * rows_held), 1)
    if rows_held == 8:
        both, row = line >> 3, line & 7
    else:
        both = lax.shift_right_logical(line * 52429, 18)
        row = line - both * 5
    return chip_of(meta, order, both >> 1) * 2 + (both & 1), row


def dot(a, b):
    return jnp.dot(a, b, preferred_element_type=F32)


def dot_nt(a, b):
    return lax.dot_general(a, b, (((1,), (1,)), ((), ())), preferred_element_type=F32)


def dot_tn(a, b):
    return lax.dot_general(a, b, (((0,), (0,)), ((), ())), preferred_element_type=F32)


def add_rows(values):
    total = values[:8]
    for first in range(8, values.shape[0], 8):
        total = total + values[first : first + 8]
    return total


def one_hot(index_row, count):
    places = lax.broadcasted_iota(jnp.int32, (count, index_row.shape[1]), 0)
    return jnp.where(places == index_row, 1.0, 0.0).astype(BF16)


def inverse_rms(values):
    return lax.rsqrt(jnp.mean(values * values, -1, keepdims=True) + EPSILON)


def norm_backward(grad_hat, unit_value, inverse):
    return inverse * (grad_hat - unit_value * jnp.mean(grad_hat * unit_value, -1, keepdims=True))


def rotate(values, cosine, sine):
    first, second = values[:, : HEAD // 2], values[:, HEAD // 2 :]
    return jnp.concatenate(
        [first * cosine - second * sine, second * cosine + first * sine], axis=-1
    )


def vmem():
    return pl.BlockSpec(memory_space=pltpu.VMEM)


def smem():
    return pl.BlockSpec(memory_space=pltpu.SMEM)


def anywhere():
    return pl.BlockSpec(memory_space=pl.ANY)


def whole(shape):
    return pl.BlockSpec(shape, lambda r: (0,) * len(shape))


def by_row(shape):
    return pl.BlockSpec((1,) + shape, lambda r: (r,) + (0,) * len(shape))


def from_row(shape, first):
    return pl.BlockSpec((1,) + shape, lambda r: (r + first,) + (0,) * len(shape))


def call(
    kernel,
    name,
    outs,
    in_specs,
    args,
    out_specs=None,
    scratch=(),
    after=(),
    aliases=None,
    grid=(),
    megabytes=58,
    flops=0,
    moved_bytes=0,
):
    after = list(after)
    count = len(in_specs)

    def body(*refs):
        kernel(*refs[:count], *refs[count + len(after) :])

    return pl.pallas_call(
        body,
        grid=grid,
        out_shape=[jax.ShapeDtypeStruct(s, d) for s, d in outs],
        in_specs=list(in_specs) + [anywhere()] * len(after),
        out_specs=[vmem()] * len(outs) if out_specs is None else out_specs,
        scratch_shapes=list(scratch),
        input_output_aliases=aliases or {},
        compiler_params=pltpu.CompilerParams(vmem_limit_bytes=megabytes * 2**20),
        cost_estimate=pl.CostEstimate(
            flops=flops, bytes_accessed=moved_bytes, transcendentals=0
        ),
        name=name,
    )(*args, *after)


def line_picks(meta, orders):
    shard_a, row_a = slab_rows(meta, orders[0], 8)
    shard_b, row_b = slab_rows(meta, orders[1], 8)
    pick_a = one_hot(jnp.where(row_a < 5, shard_a * 5 + row_a, -1), WIDTH)
    pick_b = one_hot(jnp.where(row_b < 5, shard_b * 5 + row_b, -1), WIDTH)
    return pick_a, pick_b, jnp.where(row_b == 5, shard_b, -1)


def gain_picks(shard_line):
    wide = lax.broadcasted_iota(jnp.int32, (WIDTH, shard_line.shape[1]), 0)
    first = shard_line * 5
    pick = jnp.where((wide >= first) & (wide < first + 5) & (first >= 0), 1.0, 0.0).astype(BF16)
    head = lax.broadcasted_iota(jnp.int32, (HEAD, shard_line.shape[1]), 0)
    pick_head = jnp.where((head >> 1) == shard_line, 1.0, 0.0).astype(BF16)
    return pick, pick_head


def gain_lanes(count, width, per_shard, first):
    lane = lax.broadcasted_iota(jnp.int32, (count, width), 0)
    entry = lax.broadcasted_iota(jnp.int32, (count, width), 1)
    if per_shard == 5:
        place = entry - lax.shift_right_logical(entry * 52429, 18) * 5
    else:
        place = entry & 1
    return lane == place + first


def both_parts(meta, own, other, part_a, part_b, rows):
    @pl.when(meta[3] == 0)
    def _():
        for j in range(4):
            part_a[j * rows : (j + 1) * rows] = own[j][...]
            part_b[j * rows : (j + 1) * rows] = other[j][...]

    @pl.when(meta[3] != 0)
    def _():
        for j in range(4):
            part_a[j * rows : (j + 1) * rows] = other[j][...]
            part_b[j * rows : (j + 1) * rows] = own[j][...]


def weights_kernel(meta, *refs):
    own, other = refs[:4], refs[4:8]
    weights_ref, gains_ref, head_gains_ref, part_a, part_b = refs[8:]
    both_parts(meta, own, other, part_a, part_b, 256)
    pick_a, pick_b, gain_shard = line_picks(meta, GATHER)
    weights_ref[:, :ATT_COLS] = dot(pick_a, part_a[...]).astype(BF16)
    weights_ref[:, ATT_COLS:] = dot(pick_b, part_b[...]).astype(BF16)
    pick, pick_head = gain_picks(gain_shard)
    block = part_b[:, :128]
    contract = (((0,), (1,)), ((), ()))
    wide = lax.dot_general(block, pick, contract, preferred_element_type=F32)[:24]
    head = lax.dot_general(block, pick_head, contract, preferred_element_type=F32)[:24]
    gains_ref[...] = jnp.zeros_like(gains_ref)
    head_gains_ref[...] = jnp.zeros_like(head_gains_ref)
    for g in range(4):
        chosen = jnp.where(gain_lanes(24, WIDTH, 5, 5 * g), wide, 0.0)
        gains_ref[g : g + 1] = jnp.sum(chosen, 0, keepdims=True)
    for g in range(2):
        chosen = jnp.where(gain_lanes(24, HEAD, 2, 20 + 2 * g), head, 0.0)
        head_gains_ref[4 + g : 5 + g] = jnp.sum(chosen, 0, keepdims=True)


def prepare_kernel(weights, gains, head_gains, cosine, sine, mine, before, *refs):
    normed_ref, keys_ref, values_ref, key_pre_ref, query_pre_ref, queries_ref = refs
    tokens = jnp.concatenate(
        [part[j, :BLOCK] for part in (before, mine) for j in range(4)], 0
    ).astype(F32)
    normed = (tokens * inverse_rms(tokens) * gains[0:1]).astype(BF16)
    normed_ref[...] = normed
    key_value = dot(normed, weights[:, HEADS * HEAD :])
    key_pre = key_value[:, :HEAD]
    key_pre_ref[...] = key_pre
    values_ref[...] = key_value[:, HEAD:].astype(BF16)
    query_pre = dot(normed[TOKENS:], weights[:, : HEADS * HEAD])
    query_pre_ref[...] = query_pre
    query_gain, key_gain = head_gains[4:5], head_gains[5:6]
    keys = rotate(key_pre * inverse_rms(key_pre) * key_gain, cosine[...], sine[...])
    keys_ref[...] = keys.astype(BF16)
    for h in range(HEADS):
        pre = query_pre[:, h * HEAD : (h + 1) * HEAD]
        turned = rotate(
            pre * inverse_rms(pre) * query_gain, cosine[TOKENS:], sine[TOKENS:]
        ).astype(BF16)
        for j in range(4):
            queries_ref[j, h * BLOCK : (h + 1) * BLOCK] = turned[j * BLOCK : (j + 1) * BLOCK]


def attention_kernel(first, meta, mine, before, *refs):
    step = pl.program_id(0)
    if first == 0:
        cosine, sine, slabs, refs = refs[0], refs[1], refs[2:10], refs[10:]
        made, kept, refs = refs[:3], refs[3:9], refs[9:]

        @pl.when(step == 0)
        def _():
            weights_kernel(meta, *slabs, *made, refs[-2], refs[-1])
            prepare_kernel(*made, cosine, sine, mine, before, *kept)

        _, keys_ref, values_ref, _, _, queries_ref = kept
    else:
        keys_ref, values_ref, queries_ref = refs[:3]
        refs = refs[3:]
    attended_ref, probs_ref, line_s = refs[:3]
    place = step + first
    lines = [
        part[j, BLOCK:].astype(F32)[0:1, :BLOCK] for part in (before, mine) for j in range(4)
    ]
    line_s[...] = jnp.broadcast_to(jnp.concatenate(lines, 1), line_s.shape)
    start = pl.multiple_of(place * BLOCK, BLOCK)
    window = pl.ds(start, SPAN)
    square = (BLOCK, BLOCK)
    diagonal = lax.broadcasted_iota(jnp.int32, square, 0) == lax.broadcasted_iota(
        jnp.int32, square, 1
    )
    own_line = line_s[0:1, pl.ds(pl.multiple_of(start + TOKENS, BLOCK), BLOCK)]
    own_column = jnp.sum(jnp.where(diagonal, own_line, 0.0), 1, keepdims=True)
    query_place = lax.broadcasted_iota(jnp.int32, (BLOCK, SPAN), 0)
    key_place = lax.broadcasted_iota(jnp.int32, (BLOCK, SPAN), 1) - HALO * BLOCK
    visible = (
        (key_place <= query_place)
        & (query_place - key_place < WINDOW)
        & (key_place + meta[4] + start >= 0)
        & (own_column == line_s[0:1, window])
    )
    bias = jnp.where(visible, 0.0, MASKED)
    queries = queries_ref[place if first == 0 else 0]
    scores = dot_nt(queries, keys_ref[window]) * SCALE + jnp.concatenate([bias] * HEADS, 0)
    terms = jnp.exp(scores - jnp.max(scores, -1, keepdims=True))
    probs = (terms * (1.0 / jnp.sum(terms, -1, keepdims=True))).astype(BF16)
    probs_ref[0] = probs
    mixed = dot(probs, values_ref[window]).astype(BF16)
    for h in range(HEADS):
        attended_ref[0, :, h * HEAD : (h + 1) * HEAD] = mixed[h * BLOCK : (h + 1) * BLOCK]


MADE = [((WIDTH, 1536), BF16), ((8, WIDTH), F32), ((8, HEAD), F32)]
KEPT = [
    ((KEYS, WIDTH), BF16),
    ((KEYS, HEAD), BF16),
    ((KEYS, HEAD), BF16),
    ((KEYS, HEAD), F32),
    ((TOKENS, HEADS * HEAD), F32),
    ((4, HEADS * BLOCK, HEAD), BF16),
]


def attention_blocks(first, count, meta, mine, before, tables, slabs, kept, after):
    outs = [((count, BLOCK, HEADS * HEAD), BF16), ((count, HEADS * BLOCK, SPAN), BF16)]
    making = first == 0
    fixed = MADE + KEPT if making else []
    if making:
        more = [*tables, *slabs]
        more_specs = [whole((KEYS, HEAD // 2))] * 2 + [whole((256, ATT_COLS))] * 8
    else:
        more = [kept[1], kept[2], kept[5]]
        more_specs = [whole((KEYS, HEAD))] * 2 + [from_row((HEADS * BLOCK, HEAD), first)]
    return call(
        functools.partial(attention_kernel, first),
        "attention_blocks",
        fixed + outs,
        [smem()] + [whole((4, TAGGED, WIDTH))] * 2 + more_specs,
        [meta, mine, before, *more],
        out_specs=[whole(s) for s, _ in fixed] + [by_row(s[1:]) for s, _ in outs],
        scratch=[pltpu.VMEM((8, KEYS), F32)]
        + [pltpu.VMEM((1024, ATT_COLS), BF16)] * (2 if making else 0),
        after=after,
        grid=(count,),
        megabytes=60,
        flops=count * 4 * 10**9,
        moved_bytes=count * 10**7,
    )


def gelu_parts(gate):
    square = gate * gate
    bent = jnp.tanh(gate * (0.7978845608 + (0.7978845608 * 0.044715) * square))
    half = 0.5 + 0.5 * bent
    slope = half + gate * (1.0 - bent * bent) * (
        (0.5 * 0.7978845608) + (0.5 * 0.7978845608 * 3 * 0.044715) * square
    )
    return gate * half, slope


def feed_kernel(meta, table, gains, mine, *refs):
    cotangents, refs = refs[:4], refs[4:]
    attended, refs = refs[:2], refs[2:]
    own, other, own_down, other_down = refs[:4]
    refs = refs[4:]
    block_out_ref, middle_grad_ref, attended_grad_ref, gain_ref = refs[:4]
    keep_ref, give_ref, keep_down_ref, give_down_ref = refs[4:8]
    (
        gate_w,
        up_w,
        down_w,
        output_w,
        active_s,
        slope_s,
        inner_s,
        inputs_s,
        grads_s,
        keep_s,
        give_s,
        grad_down,
        keep_down_s,
        give_down_s,
        arrivals,
        leaving,
        cotangent,
    ) = refs[8:]
    for j in range(4):
        cotangent[meta[6] ^ j] = cotangents[j][...]
    core = meta[3]
    first_core = core == 0

    def fetch(sources, target, first):
        return [
            pltpu.make_async_copy(
                sources.at[j], target.at[j * 160 : (j + 1) * 160], arrivals.at[first + j]
            )
            for j in range(4)
        ]

    @pl.when(first_core)
    def _():
        for copy in fetch(own, gate_w, 0) + fetch(other, up_w, 4):
            copy.start()

    @pl.when(jnp.logical_not(first_core))
    def _():
        for copy in fetch(other, gate_w, 0) + fetch(own, up_w, 4):
            copy.start()

    for j in range(4):

        def place(i, carry, j=j):
            mine, theirs = own_down[j, i], other_down[j, i]
            down_w[table[2, j * 16 + i]] = mine[:, OUT_COLS:]
            down_w[table[3, j * 16 + i]] = theirs[:, OUT_COLS:]
            mine, theirs = mine[:, :OUT_COLS], theirs[:, :OUT_COLS]
            output_w[table[0, j * 16 + i], :, :OUT_COLS] = jnp.where(first_core, mine, theirs)
            output_w[table[1, j * 16 + i], :, OUT_COLS:] = jnp.where(first_core, theirs, mine)[
                :, : WIDTH - OUT_COLS
            ]
            return carry

        lax.fori_loop(0, 16, place, 0, unroll=8)

    picks = []
    for order in GATHER + SCATTER:
        shard, row = slab_rows(meta, order, 5)
        picks.append(one_hot(shard * 5 + row, WIDTH))
    post_attn_gain, ffn_gain, post_ffn_gain = gains[1:2], gains[2:3], gains[3:4]
    output_weight = output_w[...].reshape(HEADS * HEAD, WIDTH)
    all_attended = jnp.concatenate(
        [part[...].reshape(-1, HEADS * HEAD) for part in attended], 0
    )
    projected = dot(all_attended, output_weight)
    proj_inverse = inverse_rms(projected)
    proj_unit = projected * proj_inverse
    tokens = jnp.concatenate([mine[j, :BLOCK] for j in range(4)], 0)
    middle = tokens.astype(F32) + proj_unit * post_attn_gain
    mid_inverse = inverse_rms(middle)
    mid_unit = middle * mid_inverse
    ffn_in = (mid_unit * ffn_gain).astype(BF16)
    input_a = dot(ffn_in, picks[0]).astype(BF16)
    input_b = dot(ffn_in, picks[1]).astype(BF16)
    inputs_s[core] = dot(ffn_in, picks[2]).astype(BF16)
    inputs_s[1 - core] = dot(ffn_in, picks[3]).astype(BF16)
    for copy in fetch(own, gate_w, 0) + fetch(own, up_w, 4):
        copy.wait()
    down = jnp.zeros((TOKENS, WIDTH), F32)
    for n in range(HIDDEN // CHUNK):
        columns = slice(n * CHUNK, (n + 1) * CHUNK)
        gate = dot(input_a, gate_w[:, columns])
        up = dot(input_b, up_w[:, columns])
        active, slope = gelu_parts(gate)
        active_s[:, columns] = active
        slope_s[:, columns] = slope * up
        inner = (active * up).astype(BF16)
        inner_s[:, columns] = inner
        blocks = slice(n * (CHUNK // 16), (n + 1) * (CHUNK // 16))
        down += dot(inner, down_w[blocks].reshape(CHUNK, WIDTH))
    down_inverse = inverse_rms(down)
    down_unit = down * down_inverse
    block_out = (middle + down_unit * post_ffn_gain).astype(BF16)
    block_out_ref[...] = block_out.reshape(4, BLOCK, WIDTH)
    out_grad = cotangent[...].reshape(TOKENS, WIDTH).astype(F32)
    gain_ref[16:24] = add_rows(out_grad * down_unit)
    down_grad = norm_backward(out_grad * post_ffn_gain, down_unit, down_inverse).astype(BF16)
    sum_a = jnp.zeros((TOKENS, WIDTH), F32)
    sum_b = jnp.zeros((TOKENS, WIDTH), F32)
    sent = []
    for n in range(HIDDEN // CHUNK):
        columns = slice(n * CHUNK, (n + 1) * CHUNK)
        blocks = slice(n * (CHUNK // 16), (n + 1) * (CHUNK // 16))
        inner_grad = dot_nt(down_grad, down_w[blocks].reshape(CHUNK, WIDTH))
        gate_grad = (inner_grad * slope_s[:, columns]).astype(BF16)
        up_grad = (inner_grad * active_s[:, columns]).astype(BF16)
        grads_s[core] = gate_grad
        grads_s[1 - core] = up_grad
        grad_down[blocks] = (
            dot_tn(inner_s[:, columns], down_grad).astype(BF16).reshape(CHUNK // 16, 16, WIDTH)
        )
        keep_s[:, columns] = dot_tn(inputs_s[0], grads_s[0]).astype(BF16)
        give_s[:, columns] = dot_tn(inputs_s[1], grads_s[1]).astype(BF16)
        for source, target, k in ((keep_s, keep_ref, n), (give_s, give_ref, 4 + n)):
            copy = pltpu.make_async_copy(
                source.at[:, columns], target.at[:, columns], leaving.at[k]
            )
            copy.start()
            sent.append(copy)
        sum_a += dot_nt(gate_grad, gate_w[:, columns])
        sum_b += dot_nt(up_grad, up_w[:, columns])
    ffn_in_grad = dot_nt(sum_a.astype(BF16), picks[0]) + dot_nt(sum_b.astype(BF16), picks[1])
    gain_ref[8:16] = add_rows(ffn_in_grad * mid_unit)
    middle_grad = out_grad + norm_backward(ffn_in_grad * ffn_gain, mid_unit, mid_inverse)
    middle_grad_ref[...] = middle_grad
    gain_ref[0:8] = add_rows(middle_grad * proj_unit)
    proj_grad = norm_backward(middle_grad * post_attn_gain, proj_unit, proj_inverse).astype(BF16)
    attended_grad_ref[...] = dot_nt(proj_grad, output_weight).astype(BF16)
    output_w[...] = dot_tn(all_attended, proj_grad).astype(BF16).reshape(64, 16, WIDTH)
    pad = jnp.zeros((16, 2 * OUT_COLS - WIDTH), BF16)

    def hand(i, carry):
        grad_a = output_w[table[4, i], :, :OUT_COLS]
        grad_b = jnp.concatenate([output_w[table[5, i], :, OUT_COLS:], pad], 1)
        keep_down_s[i, :, :OUT_COLS] = jnp.where(first_core, grad_a, grad_b)
        give_down_s[i, :, :OUT_COLS] = jnp.where(first_core, grad_b, grad_a)
        keep_down_s[i, :, OUT_COLS:] = grad_down[table[6, i]]
        give_down_s[i, :, OUT_COLS:] = grad_down[table[7, i]]
        return carry

    lax.fori_loop(0, 64, hand, 0, unroll=8)
    for source, target, k in (
        (keep_down_s, keep_down_ref, 8),
        (give_down_s, give_down_ref, 9),
    ):
        copy = pltpu.make_async_copy(source, target, leaving.at[k])
        copy.start()
        sent.append(copy)
    for copy in sent:
        copy.wait()


def feed_forward(
    meta, table, gains, mine, cotangents, attended, own, other, own_down, other_down
):
    return call(
        feed_kernel,
        "feed_forward",
        [
            ((4, BLOCK, WIDTH), BF16),
            ((TOKENS, WIDTH), F32),
            ((TOKENS, HEADS * HEAD), BF16),
            ((24, WIDTH), F32),
            ((WIDTH, HIDDEN), BF16),
            ((WIDTH, HIDDEN), BF16),
            ((64, 16, DOWN_PACK), BF16),
            ((64, 16, DOWN_PACK), BF16),
        ],
        [smem(), smem()] + [vmem()] * 8 + [anywhere()] * 2 + [vmem()] * 2,
        [meta, table, gains, mine, *cotangents, *attended, own, other, own_down, other_down],
        out_specs=[vmem()] * 4 + [anywhere()] * 4,
        scratch=[
            pltpu.VMEM((WIDTH, HIDDEN), BF16),
            pltpu.VMEM((WIDTH, HIDDEN), BF16),
            pltpu.VMEM((128, 16, WIDTH), BF16),
            pltpu.VMEM((64, 16, WIDTH), BF16),
            pltpu.VMEM((TOKENS, HIDDEN), F32),
            pltpu.VMEM((TOKENS, HIDDEN), F32),
            pltpu.VMEM((TOKENS, HIDDEN), BF16),
            pltpu.VMEM((2, TOKENS, WIDTH), BF16),
            pltpu.VMEM((2, TOKENS, CHUNK), BF16),
            pltpu.VMEM((WIDTH, HIDDEN), BF16),
            pltpu.VMEM((WIDTH, HIDDEN), BF16),
            pltpu.VMEM((128, 16, WIDTH), BF16),
            pltpu.VMEM((64, 16, DOWN_PACK), BF16),
            pltpu.VMEM((64, 16, DOWN_PACK), BF16),
            pltpu.SemaphoreType.DMA((8,)),
            pltpu.SemaphoreType.DMA((10,)),
            pltpu.VMEM((4, BLOCK, WIDTH), BF16),
        ],
        megabytes=60,
        flops=17 * 10**9,
        moved_bytes=30 * 10**6,
    )


def attention_back_kernel(starting, first, meta, attended_grad, probs, queries, keys, values, *refs):
    step = pl.program_id(0)
    if starting:
        key_sum, value_sum, query_sum = refs

        @pl.when(step == 0)
        def _():
            key_sum[...] = jnp.zeros_like(key_sum)
            value_sum[...] = jnp.zeros_like(value_sum)
    else:
        earlier, inputs, outs = refs[:3], refs[3:14], refs[14:18]
        key_sum, value_sum, query_sum, part_a, part_b = refs[18:]

        @pl.when(step == 0)
        def _():
            key_sum[...] = earlier[0][...]
            value_sum[...] = earlier[1][...]

    window = pl.ds(pl.multiple_of((step + first) * BLOCK, BLOCK), SPAN)
    mixed_grad = jnp.concatenate(
        [attended_grad[:, h * HEAD : (h + 1) * HEAD] for h in range(HEADS)], 0
    )
    prob_grad = dot_nt(mixed_grad, values[window])
    soft = probs[0].astype(F32)
    row_dot = jnp.sum(soft * prob_grad, -1, keepdims=True)
    score_grad = (soft * (prob_grad - row_dot)).astype(BF16)
    query_sum[step] = dot(score_grad, keys[window])
    key_sum[window] += dot_tn(score_grad, queries[0])
    value_sum[window] += dot_tn(probs[0], mixed_grad)
    if starting:
        return

    @pl.when(step == pl.num_programs(0) - 1)
    def _():
        finish_attention(
            meta, key_sum, value_sum, query_sum, earlier[2], part_a, part_b, *inputs, *outs
        )


def finish_attention(
    meta,
    key_sum,
    value_sum,
    query_sum,
    query_last,
    part_a,
    part_b,
    weights,
    gains,
    head_gains,
    cosine,
    sine,
    mine,
    before,
    normed,
    key_pre,
    query_pre,
    feed_gain,
    own_ref,
    before_ref,
    keep_ref,
    give_ref,
):
    query_gain, key_gain = head_gains[4:5] * SCALE, head_gains[5:6] * SCALE
    cosine_own, sine_own = cosine[TOKENS:], -sine[TOKENS:]
    query_total = jnp.zeros((8, HEAD), F32)
    pre_grads = []
    for h in range(HEADS):
        pre = query_pre[:, h * HEAD : (h + 1) * HEAD]
        inverse = inverse_rms(pre)
        unit = pre * inverse
        rows = slice(h * BLOCK, (h + 1) * BLOCK)
        grad = jnp.concatenate([part[j, rows] for part in (query_sum, query_last) for j in range(2)], 0)
        turned = rotate(grad, cosine_own, sine_own)
        query_total += add_rows(turned * unit)
        pre_grads.append(norm_backward(turned * query_gain, unit, inverse).astype(BF16))
    query_pre_grad = jnp.concatenate(pre_grads, 1)
    pre = key_pre[...]
    inverse = inverse_rms(pre)
    unit = pre * inverse
    turned = rotate(key_sum[...], cosine[...], -sine[...])
    key_total = add_rows(turned * unit)
    key_pre_grad = norm_backward(turned * key_gain, unit, inverse).astype(BF16)
    both = jnp.concatenate([key_pre_grad, value_sum[...].astype(BF16)], 1)
    normed_grad = dot_nt(both, weights[:, HEADS * HEAD :])
    own = normed_grad[TOKENS:] + dot_nt(query_pre_grad, weights[:, : HEADS * HEAD])
    own_ref[...] = own
    before_ref[...] = normed_grad[:TOKENS].astype(BF16)
    normed_grad = jnp.concatenate([normed_grad[:TOKENS], own], 0)
    tokens = jnp.concatenate(
        [part[j, :BLOCK] for part in (before, mine) for j in range(4)], 0
    ).astype(F32)
    attn_total = add_rows(tokens * inverse_rms(tokens) * normed_grad)
    pick_a, pick_b, gain_shard = line_picks(meta, SCATTER)
    query_weight_grad = dot_tn(normed[TOKENS:], query_pre_grad).astype(BF16)
    part_a[...] = dot_tn(pick_a, query_weight_grad[:, :ATT_COLS]).astype(BF16)
    both_grad = dot_tn(normed[...], both).astype(BF16)
    part_b[:, 256:] = dot_tn(pick_b, both_grad).astype(BF16)
    pick, pick_head = gain_picks(gain_shard)
    wide = jnp.zeros((128, WIDTH), F32)
    totals = (attn_total, feed_gain[0:8], feed_gain[8:16], feed_gain[16:24])
    for g in range(4):
        line = jnp.sum(totals[g], 0, keepdims=True)
        wide += jnp.where(gain_lanes(128, WIDTH, 5, 5 * g), line, 0.0)
    head = jnp.zeros((128, HEAD), F32)
    for g, total in enumerate((query_total, key_total)):
        line = jnp.sum(total, 0, keepdims=True) * SCALE
        head += jnp.where(gain_lanes(128, HEAD, 2, 20 + 2 * g), line, 0.0)
    contract = (((0,), (1,)), ((), ()))
    gain_block = lax.dot_general(
        pick, wide.astype(BF16), contract, preferred_element_type=F32
    ) + lax.dot_general(pick_head, head.astype(BF16), contract, preferred_element_type=F32)
    left = dot_tn(pick_b, query_weight_grad[:, ATT_COLS:])
    part_b[:, :128] = (left[:, :128] + gain_block).astype(BF16)
    part_b[:, 128:256] = left[:, 128:].astype(BF16)
    first_core = meta[3] == 0
    keep_ref[...] = jnp.where(first_core, part_a[...], part_b[...])
    give_ref[...] = jnp.where(first_core, part_b[...], part_a[...])


def attention_back(first, count, meta, attended_grad, probs, kept, earlier, inputs, after):
    starting = earlier is None
    sums = [((KEYS, HEAD), F32), ((KEYS, HEAD), F32), ((count, HEADS * BLOCK, HEAD), F32)]
    in_specs = [
        smem(),
        pl.BlockSpec((BLOCK, HEADS * HEAD), lambda r: (r + first, 0)),
        by_row((HEADS * BLOCK, SPAN)),
        from_row((HEADS * BLOCK, HEAD), first),
        whole((KEYS, HEAD)),
        whole((KEYS, HEAD)),
    ]
    args = [meta, attended_grad, probs, kept[5], kept[1], kept[2]]
    outs = sums
    if not starting:
        args += [*earlier, *inputs]
        in_specs += [whole(value.shape) for value in (*earlier, *inputs)]
        outs = [((TOKENS, WIDTH), F32), ((TOKENS, WIDTH), BF16)] + [((1024, ATT_COLS), BF16)] * 2
    return call(
        functools.partial(attention_back_kernel, starting, first),
        "attention_back",
        outs,
        in_specs,
        args,
        out_specs=[whole(s) for s, _ in outs],
        scratch=[]
        if starting
        else [pltpu.VMEM(s, d) for s, d in sums] + [pltpu.VMEM((1024, ATT_COLS), BF16)] * 2,
        after=after,
        grid=(count,),
        megabytes=60,
        flops=count * 5 * 10**9,
        moved_bytes=count * 12 * 10**6,
    )


def pack_kernel(meta, *refs):
    sources, keep_ref, give_ref, part = refs[:7], refs[7], refs[8], refs[9]
    held, arrivals = refs[10:17], refs[17]
    copies = [
        pltpu.make_async_copy(source, target, arrivals.at[j])
        for j, (source, target) in enumerate(zip(sources, held))
    ]
    for copy in copies:
        copy.start()
    for copy in copies:
        copy.wait()
    query, key, value, output, gate, up, gains = held
    for half in range(2):
        part[half] = jnp.zeros((8, PACK), F32)
    out_start = ATT_COLS
    feed_start = ATT_COLS + OUT_COLS
    left = HEADS * HEAD - ATT_COLS
    part[0, :5, :ATT_COLS] = query[:, :ATT_COLS].astype(F32)
    part[0, :, out_start:feed_start] = output[:, :OUT_COLS].astype(F32)
    part[0, :5, feed_start:] = gate[...].astype(F32)
    part[1, :5, :left] = query[:, ATT_COLS:].astype(F32)
    part[1, :5, left : left + HEAD] = key[...].astype(F32)
    part[1, :5, left + HEAD : ATT_COLS] = value[...].astype(F32)
    part[1, 5:6, :128] = gains[...].astype(F32)
    part[1, :, out_start : out_start + WIDTH - OUT_COLS] = output[:, OUT_COLS:].astype(F32)
    part[1, :5, feed_start:] = up[...].astype(F32)
    core = meta[3]
    keep_ref[...] = part[core].astype(BF16)
    give_ref[...] = part[1 - core].astype(BF16)


def pack_weights(meta, query, key, value, output, gate, up, gains):
    return call(
        pack_kernel,
        "pack_weights",
        [((8, PACK), BF16)] * 2,
        [smem()] + [anywhere()] * 7,
        [meta, query, key, value, output, gate, up, gains],
        scratch=[pltpu.VMEM((2, 8, PACK), F32)]
        + [
            pltpu.VMEM(held.shape, held.dtype)
            for held in (query, key, value, output, gate, up, gains)
        ]
        + [pltpu.SemaphoreType.DMA((7,))],
        megabytes=60,
        flops=10**6,
        moved_bytes=3 * 10**5,
    )


def pair_kernel(meta, kept, crossed, down, out_ref):
    first_core = meta[3] == 0
    mine, theirs = kept[...].astype(F32), crossed[...].astype(F32)
    upper = jnp.where(first_core, mine, theirs)
    lower = jnp.where(first_core, theirs, mine)
    out_ref[:, :PACK] = jnp.concatenate([upper, lower], 0).astype(BF16)
    out_ref[:, PACK:] = down[...]


def pair_up(meta, kept, crossed, down):
    return call(
        pair_kernel,
        "pair_up",
        [((16, PACK + WIDTH), BF16)],
        [smem()] + [vmem()] * 3,
        [meta, kept, crossed, down],
        megabytes=8,
        flops=10**6,
        moved_bytes=4 * 10**5,
    )[0]


def split_kernel(slot, meta, value, *refs):
    for j in range(4):
        refs[j][...] = value[meta[slot] ^ j]


def split_up(meta, slot, value, after):
    return call(
        functools.partial(split_kernel, slot),
        "split_up",
        [(value.shape[1:], value.dtype)] * 4,
        [smem(), vmem()],
        [meta, value],
        after=after,
        megabytes=16,
        flops=10**6,
        moved_bytes=10**6,
    )


def join_kernel(slot, meta, *refs):
    for j in range(4):
        refs[4][meta[slot] ^ j] = refs[j][...]


def join_up(meta, slot, pieces):
    return call(
        functools.partial(join_kernel, slot),
        "join_up",
        [((4,) + pieces[0].shape, pieces[0].dtype)],
        [smem()] + [vmem()] * 4,
        [meta, *pieces],
        megabytes=16,
        flops=10**6,
        moved_bytes=10**6,
    )[0]


def dealt(meta, value, slot_out, slot_in, after):
    own, one, two, three = split_up(meta, slot_out, value, after)
    pieces = [own, swap(one), exchange(two, False), exchange(three, True)]
    return join_up(meta, slot_in, pieces)


def hold_kernel(value, out):
    out[...] = value[...]


def hold(value, after):
    return call(
        hold_kernel,
        "hold",
        [(value.shape, value.dtype)],
        [vmem()],
        [value],
        after=after,
        megabytes=16,
        flops=10**6,
        moved_bytes=10**6,
    )[0]


def add_pieces_kernel(kept, crossed, *refs):
    rows = refs[0].shape[0]
    for j in range(4):
        here = slice(j * rows, (j + 1) * rows)
        refs[j][...] = (kept[here].astype(F32) + crossed[here].astype(F32)).astype(BF16)


def add_pieces(kept, crossed, after):
    shape = (kept.shape[0] // 4,) + kept.shape[1:]
    return call(
        add_pieces_kernel,
        "add_pieces",
        [(shape, BF16)] * 4,
        [vmem()] * 2,
        [kept, crossed],
        after=after,
        megabytes=60,
        flops=10**7,
        moved_bytes=8 * 10**6,
    )


def line_kernel(*refs):
    total = add_up(refs[0][...], [ref[...] for ref in refs[1:4]]).astype(BF16)
    for j in range(4):
        refs[4 + j][...] = total[j]


def line_up(own, others):
    return call(
        line_kernel,
        "line_up",
        [(own.shape[1:], BF16)] * 4,
        [vmem()] * 4,
        [own, *others],
        megabytes=16,
        flops=10**6,
        moved_bytes=2 * 10**6,
    )


def total_kernel(meta, *refs):
    total = add_up(refs[0][...], [ref[...] for ref in refs[1:4]])
    keep_ref, give_ref, down_ref = refs[4:]
    first_core = meta[3] == 0
    upper, lower = total[:8, :PACK], total[8:, :PACK]
    keep_ref[...] = jnp.where(first_core, upper, lower)
    give_ref[...] = jnp.where(first_core, lower, upper)
    down_ref[...] = total[:, PACK:]


def total_up(meta, own, others):
    return call(
        total_kernel,
        "total_up",
        [((8, PACK), F32)] * 2 + [((16, WIDTH), F32)],
        [smem()] + [vmem()] * 4,
        [meta, own, *others],
        megabytes=16,
        flops=10**6,
        moved_bytes=10**6,
    )


def output_kernel(slot, meta, gains, middle_grad, own, returned, mine, block_out, *refs):
    tokens = jnp.concatenate([mine[j, :BLOCK] for j in range(4)], 0).astype(F32)
    inverse = inverse_rms(tokens)
    normed_grad = own[...] + returned[...].astype(F32)
    grad = middle_grad[...] + norm_backward(normed_grad * gains[0:1], tokens * inverse, inverse)
    refs[4][...] = grad.astype(BF16).reshape(4, BLOCK, WIDTH)
    for j in range(4):
        refs[j][0] = block_out[meta[slot] ^ j]
        refs[j][1] = refs[4][meta[slot] ^ j]


def output_pieces(meta, slot, gains, middle_grad, own, returned, mine, block_out):
    return call(
        functools.partial(output_kernel, slot),
        "output_pieces",
        [((2, BLOCK, WIDTH), BF16)] * 4,
        [smem()] + [vmem()] * 6,
        [meta, gains, middle_grad, own, returned, mine, block_out],
        scratch=[pltpu.VMEM((4, BLOCK, WIDTH), BF16)],
        megabytes=24,
        flops=10**7,
        moved_bytes=5 * 10**6,
    )


def join_outputs_kernel(slot, meta, *refs):
    for j in range(4):
        for k in range(2):
            refs[4 + k][meta[slot] ^ j] = refs[j][k]


def join_outputs(meta, slot, pieces):
    return call(
        functools.partial(join_outputs_kernel, slot),
        "join_outputs",
        [((4, BLOCK, WIDTH), BF16)] * 2,
        [smem()] + [vmem()] * 4,
        [meta, *pieces],
        megabytes=60,
        flops=10**6,
        moved_bytes=2 * 10**6,
    )


def stack_kernel(*refs):
    for j in range(4):
        refs[4][j] = refs[j][...]


def stack_both_kernel(*refs):
    for j in range(8):
        refs[8 + j // 4][j % 4] = refs[j][...]


def stack_both(first, second, after):
    return call(
        stack_both_kernel,
        "stack_both",
        [((4,) + first[0].shape, BF16), ((4,) + second[0].shape, BF16)],
        [vmem()] * 8,
        [*first, *second],
        after=after,
        megabytes=60,
        flops=10**6,
        moved_bytes=10**7,
    )


def stack_up(pieces, shape):
    return call(
        stack_kernel,
        "stack_up",
        [((4,) + shape, BF16)],
        [vmem()] * 4,
        pieces,
        megabytes=16,
        flops=10**6,
        moved_bytes=4 * 10**6,
    )[0]


def att_slab_kernel(*refs):
    for j in range(4):
        refs[4][j * 64 : (j + 1) * 64] = refs[j][:, :, :ATT_COLS].reshape(64, ATT_COLS)


def attention_slab(pieces, after):
    return call(
        att_slab_kernel,
        "attention_slab",
        [((256, ATT_COLS), BF16)],
        [vmem()] * 4,
        pieces,
        after=after,
        megabytes=16,
        flops=10**6,
        moved_bytes=3 * 10**6,
    )[0]


def loose_rows():
    line = lax.broadcasted_iota(jnp.int32, (256, 160), 0)
    row = line & 7
    dense = lax.broadcasted_iota(jnp.int32, (256, 160), 1)
    same = ((line >> 3) * 5 + row == dense) & (row < 5)
    return jnp.where(same, 1.0, 0.0).astype(BF16)


def feed_slab_kernel(*refs):
    feed_ref, down_ref, loose = refs[4:]
    feed_start = ATT_COLS + OUT_COLS
    for j in range(4):
        here = slice(j * 4, (j + 1) * 4)
        down_ref[here, :, :OUT_COLS] = refs[j][:, :, ATT_COLS:feed_start]
        down_ref[here, :, OUT_COLS:] = refs[j][:, :, PACK:]
        loose[j * 64 : (j + 1) * 64] = refs[j][:, :, feed_start:PACK].reshape(64, HIDDEN)
    feed_ref[...] = dot_tn(loose_rows(), loose[...]).astype(BF16)


def feed_slabs(pieces, after):
    return call(
        feed_slab_kernel,
        "feed_slabs",
        [((160, HIDDEN), BF16), ((16, 16, DOWN_PACK), BF16)],
        [vmem()] * 4,
        pieces,
        scratch=[pltpu.VMEM((256, HIDDEN), BF16)],
        after=after,
        megabytes=16,
        flops=2 * 10**8,
        moved_bytes=4 * 10**6,
    )


def merge_kernel(*refs):
    att, feed, down, outs = refs[:4], refs[4:8], refs[8:12], refs[12:]

    def total(pieces):
        return add_up(pieces[0][...], [piece[...] for piece in pieces[1:]]).astype(BF16)

    att_total = total(att).reshape(16, 16, ATT_COLS)
    feed_total = dot(loose_rows(), total(feed)).astype(BF16).reshape(16, 16, HIDDEN)
    down_total = total(down)
    for j in range(4):
        here = slice(j * 4, (j + 1) * 4)
        outs[j][:, :, :ATT_COLS] = att_total[here]
        outs[j][:, :, ATT_COLS : ATT_COLS + HIDDEN] = feed_total[here]
        outs[j][:, :, ATT_COLS + HIDDEN :] = down_total[here]


def merge_grads(att, feed, down):
    return call(
        merge_kernel,
        "merge_grads",
        [((4, 16, PACK + WIDTH), BF16)] * 4,
        [vmem()] * 12,
        [*att, *feed, *down],
        megabytes=60,
        flops=2 * 10**8,
        moved_bytes=8 * 10**6,
    )


def unpack_kernel(meta, mine, theirs, query, key, value, output, gate, up, gains):
    first_core = meta[3] == 0
    part_a = jnp.where(first_core, mine[...], theirs[...])
    part_b = jnp.where(first_core, theirs[...], mine[...])
    left = HEADS * HEAD - ATT_COLS
    feed_end = ATT_COLS + HIDDEN
    query[:, :ATT_COLS] = part_a[:5, :ATT_COLS]
    query[:, ATT_COLS:] = part_b[:5, :left]
    key[...] = part_b[:5, left : left + HEAD]
    value[...] = part_b[:5, left + HEAD : ATT_COLS]
    gate[...] = part_a[:5, ATT_COLS:feed_end]
    up[...] = part_b[:5, ATT_COLS:feed_end]
    output[:, :OUT_COLS] = part_a[:, feed_end:]
    output[:, OUT_COLS:] = part_b[:, feed_end : feed_end + WIDTH - OUT_COLS]
    gains[...] = part_b[5:6, :128]


def unpack_grads(meta, mine, theirs):
    return call(
        unpack_kernel,
        "unpack_grads",
        [
            ((5, HEADS * HEAD), F32),
            ((5, HEAD), F32),
            ((5, HEAD), F32),
            ((8, WIDTH), F32),
            ((5, HIDDEN), F32),
            ((5, HIDDEN), F32),
            ((1, 128), F32),
        ],
        [smem()] + [vmem()] * 2,
        [meta, mine, theirs],
        megabytes=8,
        flops=10**6,
        moved_bytes=4 * 10**5,
    )


def on_device(
    hidden_in,
    segment_ids,
    cotangent,
    attn_gain,
    query_weight,
    key_weight,
    value_weight,
    query_gain,
    key_gain,
    output_weight,
    post_attn_gain,
    ffn_gain,
    gate_weight,
    up_weight,
    down_weight,
    post_ffn_gain,
):
    me = my_place()
    core = me["c"]
    first_core = core == 0
    row = 2 * ((me["x"] ^ (me["x"] >> 1)) & 1) + core
    member = 2 * (me["x"] & 1) + core
    place = (me["y"] >> 1) * 1024 + (me["x"] >> 1) * TOKENS
    meta = jnp.stack([me["z"], me["y"], me["x"], core, place, row, member]).astype(jnp.int32)
    row_slot, member_slot = 5, 6

    def pick(value_first, value_second):
        return jnp.where(first_core, value_first, value_second)

    positions = place + jnp.arange(-TOKENS, TOKENS, dtype=jnp.int32)
    frequency = jnp.exp(
        jnp.arange(HEAD // 2, dtype=F32) * (-2.0 * math.log(ROPE_BASE) / HEAD)
    )
    angles = positions.astype(F32)[:, None] * frequency[None]
    tables = (jnp.cos(angles), jnp.sin(angles))

    gains = jnp.zeros((128,), F32)
    start = 0
    for gain in (attn_gain, post_attn_gain, ffn_gain, post_ffn_gain, query_gain, key_gain):
        size = gain.shape[0]
        gains = gains + jnp.pad(gain.astype(F32), (start, 128 - start - size))
        start += size
    kept, given = pack_weights(
        meta,
        query_weight,
        key_weight,
        value_weight,
        output_weight,
        gate_weight,
        up_weight,
        gains.reshape(1, 128),
    )
    pair = pair_up(meta, kept, swap(given), down_weight)
    near_chips = arrived(pair, 0)

    hidden = hidden_in.reshape(4, BLOCK, WIDTH)
    segments = segment_ids.reshape(4, 1, BLOCK).astype(BF16)
    segments = jnp.pad(segments, ((0, 0), (0, TAGGED - BLOCK - 1), (0, WIDTH - BLOCK)))
    mine = dealt(meta, jnp.concatenate([hidden, segments], 1), row_slot, member_slot, [*near_chips, *tables])
    before = next_chunk(mine, False)

    line = stack_up([pair, *near_chips], pair.shape)
    plane = [line, *arrived(line, 1)]
    att_slab = attention_slab(plane, [])
    att_own = [att_slab, *arrived(att_slab, 2)]
    att_other = [swap(value) for value in att_own]
    feed_slab, down_slab = feed_slabs(plane, [*att_own[1:], before])

    grid = jnp.arange(64, dtype=jnp.int32)
    table = []
    for orders in (GATHER, SCATTER):
        chips = [chip_of([me["z"], me["y"], me["x"]], order, grid) for order in orders]
        held, crossed = pick(chips[0], chips[1]), pick(chips[1], chips[0])
        table += [*chips, held * 2 + core, crossed * 2 + 1 - core]
    table = jnp.stack(table).astype(jnp.int32)

    first = attention_blocks(
        0, 2, meta, mine, before, tables, att_own + att_other, None, [feed_slab]
    )
    made, kept_values, (attended_first, probs_first) = first[:3], first[3:9], first[9:]
    feed_own, down_own = stack_both(
        [feed_slab, *arrived(feed_slab, 2)], [down_slab, *arrived(down_slab, 2)], [attended_first]
    )
    own, one, two, three = split_up(
        meta, row_slot, cotangent.reshape(4, BLOCK, WIDTH), [attended_first]
    )
    cotangents = [own, swap(one), exchange(two, False), exchange(three, True)]
    attended_last, probs_last = attention_blocks(
        2, 2, meta, mine, before, None, None, kept_values, [down_own, feed_own]
    )
    (
        block_out,
        middle_grad,
        attended_grad,
        feed_gain,
        keep_feed,
        give_feed,
        keep_down,
        give_down,
    ) = feed_forward(
        meta,
        table,
        made[1],
        mine,
        cotangents,
        [attended_first, attended_last],
        feed_own,
        swap(feed_own),
        down_own,
        swap(down_own),
    )
    back = attention_back(2, 2, meta, attended_grad, probs_last, kept_values, None, None, [])
    feed_sum = add_pieces(keep_feed, swap(give_feed), [back[0]])
    down_sum = add_pieces(keep_down, swap(give_down), [back[0]])
    normed_grad, to_before, keep_att, give_att = attention_back(
        0,
        2,
        meta,
        attended_grad,
        probs_first,
        kept_values,
        back,
        (
            *made,
            *tables,
            mine,
            before,
            kept_values[0],
            kept_values[3],
            kept_values[4],
            feed_gain,
        ),
        [*feed_sum, *down_sum],
    )
    feed_in = received(feed_sum, 2)
    down_in = received(down_sum, 2)

    give_att = hold(give_att, [*feed_in, *down_in])
    att_sum = add_pieces(keep_att, swap(give_att), [])
    plane = merge_grads(
        [att_sum[0], *received(att_sum, 2)], [feed_sum[0], *feed_in], [down_sum[0], *down_in]
    )
    line = line_up(plane[0], received(plane, 1))
    kept_grads, given_grads, grad_down = total_up(meta, line[0], received(line, 0))
    grad_query, grad_key, grad_value, grad_output, grad_gate, grad_up, gain_grads = unpack_grads(
        meta, kept_grads, swap(given_grads)
    )
    gain_grads = gain_grads.reshape(128)

    returned = next_chunk(to_before, True)
    own, one, two, three = output_pieces(
        meta, member_slot, made[1], middle_grad, normed_grad, returned, mine, block_out
    )
    block_out, input_grad = join_outputs(
        meta, row_slot, [own, swap(one), exchange(two, False), exchange(three, True)]
    )
    return (
        block_out.reshape(hidden_in.shape),
        input_grad.reshape(hidden_in.shape),
        gain_grads[0:5],
        grad_query,
        grad_key,
        grad_value,
        gain_grads[20:22],
        gain_grads[22:24],
        grad_output,
        gain_grads[5:10],
        gain_grads[10:15],
        grad_gate,
        grad_up,
        grad_down,
        gain_grads[15:20],
    )


def solution(mesh):
    rows = P(None, "dp", "seq", None)
    shard = P(("dp", "seq"), None)
    vector = P(("dp", "seq"))
    return jax.shard_map(
        on_device,
        mesh=mesh,
        in_specs=(rows, P(None, "dp", "seq"), rows)
        + (vector, shard, shard, shard, vector, vector, shard, vector)
        + (vector, shard, shard, shard, vector),
        out_specs=(rows, rows)
        + (vector, shard, shard, shard, vector, vector, shard, vector)
        + (vector, shard, shard, shard, vector),
        check_vma=False,
    )
```

```python
import functools
import math

import jax
import jax.numpy as jnp
from jax import lax
from jax.experimental import pallas as pl
from jax.experimental.pallas import tpu as pltpu
from jax.sharding import PartitionSpec as P

WINDOW = 512
HALO = 4
BLOCK = 128
TOKENS = 512
KEYS = 1024
WIDTH = 640
HEADS = 4
HEAD = 256
HIDDEN = 2048
SPAN = (HALO + 1) * BLOCK
CHUNK = 512
TAGGED = BLOCK + 16
EPSILON = 1e-06
ROPE_BASE = 10000.0
MASKED = -1e30
SCALE = HEAD ** (-0.5)
F32 = jnp.float32
BF16 = jnp.bfloat16

AXES = ("dp", "seq")
SIZE = {"x": 4, "y": 4, "z": 4, "c": 2}
ORDERS = (("y", "x", "z"), ("y", "z", "x"))
ATT_COLS = 768
OUT_COLS = 384
DOWN_PACK = OUT_COLS + WIDTH
PACK = ATT_COLS + OUT_COLS + HIDDEN
FIRST_PACK = ATT_COLS + DOWN_PACK


def shard_of(z, y, x, c):
    return z * 32 + (y % 2) * 16 + (y // 2) * 8 + x * 2 + c


def moved(axis_of_core, by):
    pairs = []
    for z in range(4):
        for y in range(4):
            for x in range(4):
                for c in range(2):
                    place = {"z": z, "y": y, "x": x, "c": c}
                    axis = axis_of_core[c]
                    place[axis] = (place[axis] + by) % SIZE[axis]
                    pairs.append((shard_of(z, y, x, c), shard_of(**place)))
    return pairs


def send(value, phase, by):
    axes = (ORDERS[0][phase], ORDERS[1][phase])
    return lax.ppermute(value, AXES, moved(axes, by))


def swap(value):
    return lax.ppermute(value, AXES, moved(("c", "c"), 1))


def exchange(value, flip):
    pairs = []
    for i in range(128):
        pairs.append((i, i ^ (3 if flip else 2)))
    return lax.ppermute(value, AXES, pairs)


def next_chunk(value, first_half):
    along, across = [], []
    for dp in range(8):
        for c in range(2):
            for x in range(4):
                for yh in range(2):
                    if x >= 2 and yh == 1:
                        continue
                    here = dp * 16 + yh * 8 + x * 2 + c
                    along.append((here, here + (3 - 2 * x) * 2))
            for x in range(2):
                here = dp * 16 + x * 2 + c
                across.append((here, here + 8))
    near = lax.ppermute(value, AXES, along)
    return near, jnp.where(first_half, lax.ppermute(near, AXES, across), near)


def chunk_before(value):
    pairs = []
    for dp in range(8):
        for yh in range(2):
            for x in range(4):
                for c in range(2):
                    if x >= 2 and yh == 1:
                        continue
                    here = dp * 16 + yh * 8 + x * 2 + c
                    there = dp * 16 + (yh + (x >= 2)) * 8 + (3 - x) * 2 + c
                    pairs.append((there, here))
    return lax.ppermute(value, AXES, pairs)


def my_place():
    dp, seq = lax.axis_index("dp"), lax.axis_index("seq")
    return {"z": dp // 2, "y": (seq // 8) * 2 + dp % 2, "x": (seq // 2) % 4, "c": seq % 2}


def arrived(value, phase):
    two, one, three = [send(value, phase, -by) for by in (2, 1, 3)]
    return [one, two, three]


def received(pieces, phase):
    return [send(pieces[by], phase, by) for by in (2, 1, 3)]


def add_up(own, others):
    total = own.astype(F32)
    for other in others:
        total = total + other.astype(F32)
    return total


def chip_at(meta, order, j3, j2, j1):
    place = {
        order[2]: (meta["zyx".index(order[2])] + j3) & 3,
        order[1]: (meta["zyx".index(order[1])] + j2) & 3,
        order[0]: (meta["zyx".index(order[0])] + j1) & 3,
    }
    z, y, x = place["z"], place["y"], place["x"]
    return z * 16 + (y & 1) * 8 + (y >> 1) * 4 + x


def chip_of(meta, order, i):
    return chip_at(meta, order, i >> 4, (i >> 2) & 3, i & 3)


def slab_rows(meta, order, rows_held):
    line = lax.broadcasted_iota(jnp.int32, (1, 128 * rows_held), 1)
    if rows_held == 8:
        both, row = line >> 3, line & 7
    else:
        both = lax.shift_right_logical(line * 52429, 18)
        row = line - both * 5
    return chip_of(meta, order, both >> 1) * 2 + (both & 1), row


def dot(a, b):
    return jnp.dot(a, b, preferred_element_type=F32)


def dot_nt(a, b):
    return lax.dot_general(a, b, (((1,), (1,)), ((), ())), preferred_element_type=F32)


def dot_tn(a, b):
    return lax.dot_general(a, b, (((0,), (0,)), ((), ())), preferred_element_type=F32)


def add_rows(values):
    total = values[:8]
    for first in range(8, values.shape[0], 8):
        total = total + values[first : first + 8]
    return total


def one_hot(index_row, count):
    places = lax.broadcasted_iota(jnp.int32, (count, index_row.shape[1]), 0)
    return jnp.where(places == index_row, 1.0, 0.0).astype(BF16)


def inverse_rms(values):
    return lax.rsqrt(jnp.mean(values * values, -1, keepdims=True) + EPSILON)


def norm_backward(grad_hat, unit_value, inverse):
    return inverse * (grad_hat - unit_value * jnp.mean(grad_hat * unit_value, -1, keepdims=True))


def rotate(values, cosine, sine):
    first, second = values[:, : HEAD // 2], values[:, HEAD // 2 :]
    return jnp.concatenate(
        [first * cosine - second * sine, second * cosine + first * sine], axis=-1
    )


def vmem():
    return pl.BlockSpec(memory_space=pltpu.VMEM)


def smem():
    return pl.BlockSpec(memory_space=pltpu.SMEM)


def anywhere():
    return pl.BlockSpec(memory_space=pl.ANY)


def whole(shape):
    return pl.BlockSpec(shape, lambda r: (0,) * len(shape))


def by_row(shape):
    return pl.BlockSpec((1,) + shape, lambda r: (r,) + (0,) * len(shape))


def from_row(shape, first):
    return pl.BlockSpec((1,) + shape, lambda r: (r + first,) + (0,) * len(shape))


def call(
    kernel,
    name,
    outs,
    in_specs,
    args,
    out_specs=None,
    scratch=(),
    after=(),
    aliases=None,
    grid=(),
    megabytes=58,
    flops=0,
    moved_bytes=0,
):
    after = list(after)
    count = len(in_specs)

    def body(*refs):
        kernel(*refs[:count], *refs[count + len(after) :])

    return pl.pallas_call(
        body,
        grid=grid,
        out_shape=[jax.ShapeDtypeStruct(s, d) for s, d in outs],
        in_specs=list(in_specs) + [anywhere()] * len(after),
        out_specs=[vmem()] * len(outs) if out_specs is None else out_specs,
        scratch_shapes=list(scratch),
        input_output_aliases=aliases or {},
        compiler_params=pltpu.CompilerParams(vmem_limit_bytes=megabytes * 2**20),
        cost_estimate=pl.CostEstimate(
            flops=flops, bytes_accessed=moved_bytes, transcendentals=0
        ),
        name=name,
    )(*args, *after)


def line_picks(meta):
    shard_a, row_a = slab_rows(meta, ORDERS[0], 8)
    shard_b, row_b = slab_rows(meta, ORDERS[1], 8)
    pick_a = one_hot(jnp.where(row_a < 5, shard_a * 5 + row_a, -1), WIDTH)
    pick_b = one_hot(jnp.where(row_b < 5, shard_b * 5 + row_b, -1), WIDTH)
    return pick_a, pick_b, jnp.where(row_b == 5, shard_b, -1)


def gain_picks(shard_line):
    wide = lax.broadcasted_iota(jnp.int32, (WIDTH, shard_line.shape[1]), 0)
    first = shard_line * 5
    pick = jnp.where((wide >= first) & (wide < first + 5) & (first >= 0), 1.0, 0.0).astype(BF16)
    head = lax.broadcasted_iota(jnp.int32, (HEAD, shard_line.shape[1]), 0)
    pick_head = jnp.where((head >> 1) == shard_line, 1.0, 0.0).astype(BF16)
    return pick, pick_head


def gain_lanes(count, width, per_shard, first):
    lane = lax.broadcasted_iota(jnp.int32, (count, width), 0)
    entry = lax.broadcasted_iota(jnp.int32, (count, width), 1)
    if per_shard == 5:
        place = entry - lax.shift_right_logical(entry * 52429, 18) * 5
    else:
        place = entry & 1
    return lane == place + first


def both_parts(meta, own, other, part_a, part_b, rows):
    @pl.when(meta[3] == 0)
    def _():
        for j in range(4):
            part_a[j * rows : (j + 1) * rows] = own[j][...]
            part_b[j * rows : (j + 1) * rows] = other[j][...]

    @pl.when(meta[3] != 0)
    def _():
        for j in range(4):
            part_a[j * rows : (j + 1) * rows] = other[j][...]
            part_b[j * rows : (j + 1) * rows] = own[j][...]


def weights_kernel(meta, *refs):
    own, other = refs[:4], refs[4:8]
    weights_ref, gains_ref, head_gains_ref, part_a, part_b = refs[8:]
    both_parts(meta, own, other, part_a, part_b, 256)
    pick_a, pick_b, gain_shard = line_picks(meta)
    weights_ref[:, :ATT_COLS] = dot(pick_a, part_a[...]).astype(BF16)
    weights_ref[:, ATT_COLS:] = dot(pick_b, part_b[...]).astype(BF16)
    pick, pick_head = gain_picks(gain_shard)
    block = part_b[:, :128]
    contract = (((0,), (1,)), ((), ()))
    wide = lax.dot_general(block, pick, contract, preferred_element_type=F32)[:24]
    head = lax.dot_general(block, pick_head, contract, preferred_element_type=F32)[:24]
    gains_ref[...] = jnp.zeros_like(gains_ref)
    head_gains_ref[...] = jnp.zeros_like(head_gains_ref)
    for g in range(4):
        chosen = jnp.where(gain_lanes(24, WIDTH, 5, 5 * g), wide, 0.0)
        gains_ref[g : g + 1] = jnp.sum(chosen, 0, keepdims=True)
    for g in range(2):
        chosen = jnp.where(gain_lanes(24, HEAD, 2, 20 + 2 * g), head, 0.0)
        head_gains_ref[4 + g : 5 + g] = jnp.sum(chosen, 0, keepdims=True)


def prepare_kernel(weights, gains, head_gains, cosine, sine, mine, before, *refs):
    normed_ref, keys_ref, values_ref, key_pre_ref, query_pre_ref, queries_ref = refs
    tokens = jnp.concatenate(
        [part[j, :BLOCK] for part in (before, mine) for j in range(4)], 0
    ).astype(F32)
    normed = (tokens * inverse_rms(tokens) * gains[0:1]).astype(BF16)
    normed_ref[...] = normed
    key_value = dot(normed, weights[:, HEADS * HEAD :])
    key_pre = key_value[:, :HEAD]
    key_pre_ref[...] = key_pre
    values_ref[...] = key_value[:, HEAD:].astype(BF16)
    query_pre = dot(normed[TOKENS:], weights[:, : HEADS * HEAD])
    query_pre_ref[...] = query_pre
    query_gain, key_gain = head_gains[4:5], head_gains[5:6]
    keys = rotate(key_pre * inverse_rms(key_pre) * key_gain, cosine[...], sine[...])
    keys_ref[...] = keys.astype(BF16)
    for h in range(HEADS):
        pre = query_pre[:, h * HEAD : (h + 1) * HEAD]
        turned = rotate(
            pre * inverse_rms(pre) * query_gain, cosine[TOKENS:], sine[TOKENS:]
        ).astype(BF16)
        for j in range(4):
            queries_ref[j, h * BLOCK : (h + 1) * BLOCK] = turned[j * BLOCK : (j + 1) * BLOCK]


def attention_kernel(first, meta, mine, before, *refs):
    step = pl.program_id(0)
    if first == 0:
        cosine, sine, slabs, refs = refs[0], refs[1], refs[2:10], refs[10:]
        made, kept, refs = refs[:3], refs[3:9], refs[9:]

        @pl.when(step == 0)
        def _():
            weights_kernel(meta, *slabs, *made, refs[-2], refs[-1])
            prepare_kernel(*made, cosine, sine, mine, before, *kept)

        _, keys_ref, values_ref, _, _, queries_ref = kept
    else:
        keys_ref, values_ref, queries_ref = refs[:3]
        refs = refs[3:]
    attended_ref, probs_ref, line_s = refs[:3]
    place = step + first
    lines = [
        part[j, BLOCK:].astype(F32)[0:1, :BLOCK] for part in (before, mine) for j in range(4)
    ]
    line_s[...] = jnp.broadcast_to(jnp.concatenate(lines, 1), line_s.shape)
    start = pl.multiple_of(place * BLOCK, BLOCK)
    window = pl.ds(start, SPAN)
    square = (BLOCK, BLOCK)
    diagonal = lax.broadcasted_iota(jnp.int32, square, 0) == lax.broadcasted_iota(
        jnp.int32, square, 1
    )
    own_line = line_s[0:1, pl.ds(pl.multiple_of(start + TOKENS, BLOCK), BLOCK)]
    own_column = jnp.sum(jnp.where(diagonal, own_line, 0.0), 1, keepdims=True)
    query_place = lax.broadcasted_iota(jnp.int32, (BLOCK, SPAN), 0)
    key_place = lax.broadcasted_iota(jnp.int32, (BLOCK, SPAN), 1) - HALO * BLOCK
    visible = (
        (key_place <= query_place)
        & (query_place - key_place < WINDOW)
        & (key_place + meta[4] + start >= 0)
        & (own_column == line_s[0:1, window])
    )
    bias = jnp.where(visible, 0.0, MASKED)
    queries = queries_ref[place if first == 0 else 0]
    scores = dot_nt(queries, keys_ref[window]) * SCALE + jnp.concatenate([bias] * HEADS, 0)
    terms = jnp.exp(scores - jnp.max(scores, -1, keepdims=True))
    probs = (terms * (1.0 / jnp.sum(terms, -1, keepdims=True))).astype(BF16)
    probs_ref[0] = probs
    mixed = dot(probs, values_ref[window]).astype(BF16)
    for h in range(HEADS):
        attended_ref[0, :, h * HEAD : (h + 1) * HEAD] = mixed[h * BLOCK : (h + 1) * BLOCK]


MADE = [((WIDTH, 1536), BF16), ((8, WIDTH), F32), ((8, HEAD), F32)]
KEPT = [
    ((KEYS, WIDTH), BF16),
    ((KEYS, HEAD), BF16),
    ((KEYS, HEAD), BF16),
    ((KEYS, HEAD), F32),
    ((TOKENS, HEADS * HEAD), F32),
    ((4, HEADS * BLOCK, HEAD), BF16),
]


def attention_blocks(first, count, meta, mine, before, tables, slabs, kept, after):
    outs = [((count, BLOCK, HEADS * HEAD), BF16), ((count, HEADS * BLOCK, SPAN), BF16)]
    making = first == 0
    fixed = MADE + KEPT if making else []
    if making:
        more = [*tables, *slabs]
        more_specs = [whole((KEYS, HEAD // 2))] * 2 + [whole((256, ATT_COLS))] * 8
    else:
        more = [kept[1], kept[2], kept[5]]
        more_specs = [whole((KEYS, HEAD))] * 2 + [from_row((HEADS * BLOCK, HEAD), first)]
    return call(
        functools.partial(attention_kernel, first),
        "attention_blocks",
        fixed + outs,
        [smem()] + [whole((4, TAGGED, WIDTH))] * 2 + more_specs,
        [meta, mine, before, *more],
        out_specs=[whole(s) for s, _ in fixed] + [by_row(s[1:]) for s, _ in outs],
        scratch=[pltpu.VMEM((8, KEYS), F32)]
        + [pltpu.VMEM((1024, ATT_COLS), BF16)] * (2 if making else 0),
        after=after,
        grid=(count,),
        megabytes=60,
        flops=count * 4 * 10**9,
        moved_bytes=count * 10**7,
    )


def gelu_parts(gate):
    square = gate * gate
    bent = jnp.tanh(gate * (0.7978845608 + (0.7978845608 * 0.044715) * square))
    half = 0.5 + 0.5 * bent
    slope = half + gate * (1.0 - bent * bent) * (
        (0.5 * 0.7978845608) + (0.5 * 0.7978845608 * 3 * 0.044715) * square
    )
    return gate * half, slope


def feed_kernel(meta, table, gains, mine, cotangent, *refs):
    attended, refs = refs[0], refs[1:]
    own, other, own_down, other_down = refs[:4], refs[4:8], refs[8:12], refs[12:16]
    refs = refs[16:]
    block_out_ref, middle_grad_ref, attended_grad_ref, gain_ref = refs[:4]
    keep_ref, give_ref, keep_down_ref, give_down_ref = refs[4:8]
    (
        gate_w,
        up_w,
        down_w,
        output_w,
        active_s,
        slope_s,
        inner_s,
        inputs_s,
        grads_s,
        keep_s,
        give_s,
        grad_down,
        keep_down_s,
        give_down_s,
        arrivals,
        leaving,
    ) = refs[8:]
    core = meta[3]
    first_core = core == 0

    def fetch(sources, target, first):
        return [
            pltpu.make_async_copy(
                sources[j], target.at[j * 160 : (j + 1) * 160], arrivals.at[first + j]
            )
            for j in range(4)
        ]

    @pl.when(first_core)
    def _():
        for copy in fetch(own, gate_w, 0) + fetch(other, up_w, 4):
            copy.start()

    @pl.when(jnp.logical_not(first_core))
    def _():
        for copy in fetch(other, gate_w, 0) + fetch(own, up_w, 4):
            copy.start()

    for j in range(4):

        def place(i, carry, j=j):
            here = pl.ds(pl.multiple_of(i * 16, 16), 16)
            mine, theirs = own_down[j][here, ATT_COLS:], other_down[j][here, ATT_COLS:]
            down_w[table[2, j * 16 + i]] = mine[:, OUT_COLS:]
            down_w[table[3, j * 16 + i]] = theirs[:, OUT_COLS:]
            mine, theirs = mine[:, :OUT_COLS], theirs[:, :OUT_COLS]
            output_w[table[0, j * 16 + i], :, :OUT_COLS] = jnp.where(first_core, mine, theirs)
            output_w[table[1, j * 16 + i], :, OUT_COLS:] = jnp.where(first_core, theirs, mine)[
                :, : WIDTH - OUT_COLS
            ]
            return carry

        lax.fori_loop(0, 16, place, 0, unroll=8)

    picks = []
    for order in ORDERS:
        shard, row = slab_rows(meta, order, 5)
        picks.append(one_hot(shard * 5 + row, WIDTH))
    post_attn_gain, ffn_gain, post_ffn_gain = gains[1:2], gains[2:3], gains[3:4]
    output_weight = output_w[...].reshape(HEADS * HEAD, WIDTH)
    all_attended = attended[...].reshape(TOKENS, HEADS * HEAD)
    projected = dot(all_attended, output_weight)
    proj_inverse = inverse_rms(projected)
    proj_unit = projected * proj_inverse
    tokens = jnp.concatenate([mine[j, :BLOCK] for j in range(4)], 0)
    middle = tokens.astype(F32) + proj_unit * post_attn_gain
    mid_inverse = inverse_rms(middle)
    mid_unit = middle * mid_inverse
    ffn_in = (mid_unit * ffn_gain).astype(BF16)
    input_a = dot(ffn_in, picks[0]).astype(BF16)
    input_b = dot(ffn_in, picks[1]).astype(BF16)
    inputs_s[core] = input_a
    inputs_s[1 - core] = input_b
    for copy in fetch(own, gate_w, 0) + fetch(own, up_w, 4):
        copy.wait()
    down = jnp.zeros((TOKENS, WIDTH), F32)
    for n in range(HIDDEN // CHUNK):
        columns = slice(n * CHUNK, (n + 1) * CHUNK)
        gate = dot(input_a, gate_w[:, columns])
        up = dot(input_b, up_w[:, columns])
        active, slope = gelu_parts(gate)
        active_s[:, columns] = active
        slope_s[:, columns] = slope * up
        inner = (active * up).astype(BF16)
        inner_s[:, columns] = inner
        blocks = slice(n * (CHUNK // 16), (n + 1) * (CHUNK // 16))
        down += dot(inner, down_w[blocks].reshape(CHUNK, WIDTH))
    down_inverse = inverse_rms(down)
    down_unit = down * down_inverse
    block_out = (middle + down_unit * post_ffn_gain).astype(BF16)
    block_out_ref[...] = block_out.reshape(4, BLOCK, WIDTH)
    out_grad = cotangent[...].reshape(TOKENS, WIDTH).astype(F32)
    gain_ref[16:24] = add_rows(out_grad * down_unit)
    down_grad = norm_backward(out_grad * post_ffn_gain, down_unit, down_inverse).astype(BF16)
    sum_a = jnp.zeros((TOKENS, WIDTH), F32)
    sum_b = jnp.zeros((TOKENS, WIDTH), F32)
    sent = []
    for n in range(HIDDEN // CHUNK):
        columns = slice(n * CHUNK, (n + 1) * CHUNK)
        blocks = slice(n * (CHUNK // 16), (n + 1) * (CHUNK // 16))
        inner_grad = dot_nt(down_grad, down_w[blocks].reshape(CHUNK, WIDTH))
        gate_grad = (inner_grad * slope_s[:, columns]).astype(BF16)
        up_grad = (inner_grad * active_s[:, columns]).astype(BF16)
        grads_s[core] = gate_grad
        grads_s[1 - core] = up_grad
        grad_down[blocks] = (
            dot_tn(inner_s[:, columns], down_grad).astype(BF16).reshape(CHUNK // 16, 16, WIDTH)
        )
        keep_s[:, columns] = dot_tn(inputs_s[0], grads_s[0]).astype(BF16)
        give_s[:, columns] = dot_tn(inputs_s[1], grads_s[1]).astype(BF16)
        for source, target, k in ((keep_s, keep_ref, n), (give_s, give_ref, 4 + n)):
            copy = pltpu.make_async_copy(
                source.at[:, columns], target.at[:, columns], leaving.at[k]
            )
            copy.start()
            sent.append(copy)
        sum_a += dot_nt(gate_grad, gate_w[:, columns])
        sum_b += dot_nt(up_grad, up_w[:, columns])
    ffn_in_grad = dot_nt(sum_a.astype(BF16), picks[0]) + dot_nt(sum_b.astype(BF16), picks[1])
    gain_ref[8:16] = add_rows(ffn_in_grad * mid_unit)
    middle_grad = out_grad + norm_backward(ffn_in_grad * ffn_gain, mid_unit, mid_inverse)
    middle_grad_ref[...] = middle_grad
    gain_ref[0:8] = add_rows(middle_grad * proj_unit)
    proj_grad = norm_backward(middle_grad * post_attn_gain, proj_unit, proj_inverse).astype(BF16)
    attended_grad_ref[...] = dot_nt(proj_grad, output_weight).astype(BF16)
    output_w[...] = dot_tn(all_attended, proj_grad).astype(BF16).reshape(64, 16, WIDTH)
    pad = jnp.zeros((16, 2 * OUT_COLS - WIDTH), BF16)

    def hand(i, carry):
        grad_a = output_w[table[0, i], :, :OUT_COLS]
        grad_b = jnp.concatenate([output_w[table[1, i], :, OUT_COLS:], pad], 1)
        keep_down_s[i, :, :OUT_COLS] = jnp.where(first_core, grad_a, grad_b)
        give_down_s[i, :, :OUT_COLS] = jnp.where(first_core, grad_b, grad_a)
        keep_down_s[i, :, OUT_COLS:] = grad_down[table[2, i]]
        give_down_s[i, :, OUT_COLS:] = grad_down[table[3, i]]
        return carry

    lax.fori_loop(0, 64, hand, 0, unroll=8)
    for source, target, k in (
        (keep_down_s, keep_down_ref, 8),
        (give_down_s, give_down_ref, 9),
    ):
        copy = pltpu.make_async_copy(source, target, leaving.at[k])
        copy.start()
        sent.append(copy)
    for copy in sent:
        copy.wait()


def feed_forward(
    meta, table, gains, mine, cotangent, attended, own, other, own_down, other_down
):
    return call(
        feed_kernel,
        "feed_forward",
        [
            ((4, BLOCK, WIDTH), BF16),
            ((TOKENS, WIDTH), F32),
            ((TOKENS, HEADS * HEAD), BF16),
            ((24, WIDTH), F32),
            ((WIDTH, HIDDEN), BF16),
            ((WIDTH, HIDDEN), BF16),
            ((64, 16, DOWN_PACK), BF16),
            ((64, 16, DOWN_PACK), BF16),
        ],
        [smem(), smem()] + [vmem()] * 4 + [anywhere()] * 8 + [vmem()] * 8,
        [meta, table, gains, mine, cotangent, attended, *own, *other, *own_down, *other_down],
        out_specs=[vmem()] * 4 + [anywhere()] * 4,
        scratch=[
            pltpu.VMEM((WIDTH, HIDDEN), BF16),
            pltpu.VMEM((WIDTH, HIDDEN), BF16),
            pltpu.VMEM((128, 16, WIDTH), BF16),
            pltpu.VMEM((64, 16, WIDTH), BF16),
            pltpu.VMEM((TOKENS, HIDDEN), F32),
            pltpu.VMEM((TOKENS, HIDDEN), F32),
            pltpu.VMEM((TOKENS, HIDDEN), BF16),
            pltpu.VMEM((2, TOKENS, WIDTH), BF16),
            pltpu.VMEM((2, TOKENS, CHUNK), BF16),
            pltpu.VMEM((WIDTH, HIDDEN), BF16),
            pltpu.VMEM((WIDTH, HIDDEN), BF16),
            pltpu.VMEM((128, 16, WIDTH), BF16),
            pltpu.VMEM((64, 16, DOWN_PACK), BF16),
            pltpu.VMEM((64, 16, DOWN_PACK), BF16),
            pltpu.SemaphoreType.DMA((8,)),
            pltpu.SemaphoreType.DMA((10,)),
        ],
        megabytes=60,
        flops=17 * 10**9,
        moved_bytes=30 * 10**6,
    )


def attention_back_kernel(starting, first, meta, attended_grad, probs, queries, keys, values, *refs):
    step = pl.program_id(0)
    if starting:
        key_sum, value_sum, query_sum = refs

        @pl.when(step == 0)
        def _():
            key_sum[...] = jnp.zeros_like(key_sum)
            value_sum[...] = jnp.zeros_like(value_sum)
    else:
        earlier, inputs, outs = refs[:3], refs[3:14], refs[14:18]
        key_sum, value_sum, query_sum, part_a, part_b = refs[18:]

        @pl.when(step == 0)
        def _():
            key_sum[...] = earlier[0][...]
            value_sum[...] = earlier[1][...]

    window = pl.ds(pl.multiple_of((step + first) * BLOCK, BLOCK), SPAN)
    mixed_grad = jnp.concatenate(
        [attended_grad[:, h * HEAD : (h + 1) * HEAD] for h in range(HEADS)], 0
    )
    prob_grad = dot_nt(mixed_grad, values[window])
    soft = probs[0].astype(F32)
    row_dot = jnp.sum(soft * prob_grad, -1, keepdims=True)
    score_grad = (soft * (prob_grad - row_dot)).astype(BF16)
    query_sum[step] = dot(score_grad, keys[window])
    key_sum[window] += dot_tn(score_grad, queries[0])
    value_sum[window] += dot_tn(probs[0], mixed_grad)
    if starting:
        return

    @pl.when(step == pl.num_programs(0) - 1)
    def _():
        finish_attention(
            meta, key_sum, value_sum, query_sum, earlier[2], part_a, part_b, *inputs, *outs
        )


def finish_attention(
    meta,
    key_sum,
    value_sum,
    query_sum,
    query_last,
    part_a,
    part_b,
    weights,
    gains,
    head_gains,
    cosine,
    sine,
    mine,
    before,
    normed,
    key_pre,
    query_pre,
    feed_gain,
    own_ref,
    before_ref,
    keep_ref,
    give_ref,
):
    query_gain, key_gain = head_gains[4:5] * SCALE, head_gains[5:6] * SCALE
    cosine_own, sine_own = cosine[TOKENS:], -sine[TOKENS:]
    query_total = jnp.zeros((8, HEAD), F32)
    pre_grads = []
    for h in range(HEADS):
        pre = query_pre[:, h * HEAD : (h + 1) * HEAD]
        inverse = inverse_rms(pre)
        unit = pre * inverse
        rows = slice(h * BLOCK, (h + 1) * BLOCK)
        grad = jnp.concatenate([part[j, rows] for part in (query_sum, query_last) for j in range(2)], 0)
        turned = rotate(grad, cosine_own, sine_own)
        query_total += add_rows(turned * unit)
        pre_grads.append(norm_backward(turned * query_gain, unit, inverse).astype(BF16))
    query_pre_grad = jnp.concatenate(pre_grads, 1)
    pre = key_pre[...]
    inverse = inverse_rms(pre)
    unit = pre * inverse
    turned = rotate(key_sum[...], cosine[...], -sine[...])
    key_total = add_rows(turned * unit)
    key_pre_grad = norm_backward(turned * key_gain, unit, inverse).astype(BF16)
    both = jnp.concatenate([key_pre_grad, value_sum[...].astype(BF16)], 1)
    normed_grad = dot_nt(both, weights[:, HEADS * HEAD :])
    own = normed_grad[TOKENS:] + dot_nt(query_pre_grad, weights[:, : HEADS * HEAD])
    own_ref[...] = own
    before_ref[...] = normed_grad[:TOKENS].astype(BF16)
    normed_grad = jnp.concatenate([normed_grad[:TOKENS], own], 0)
    tokens = jnp.concatenate(
        [part[j, :BLOCK] for part in (before, mine) for j in range(4)], 0
    ).astype(F32)
    attn_total = add_rows(tokens * inverse_rms(tokens) * normed_grad)
    pick_a, pick_b, gain_shard = line_picks(meta)
    query_weight_grad = dot_tn(normed[TOKENS:], query_pre_grad).astype(BF16)
    part_a[...] = dot_tn(pick_a, query_weight_grad[:, :ATT_COLS]).astype(BF16)
    both_grad = dot_tn(normed[...], both).astype(BF16)
    part_b[:, 256:] = dot_tn(pick_b, both_grad).astype(BF16)
    pick, pick_head = gain_picks(gain_shard)
    wide = jnp.zeros((128, WIDTH), F32)
    totals = (attn_total, feed_gain[0:8], feed_gain[8:16], feed_gain[16:24])
    for g in range(4):
        line = jnp.sum(totals[g], 0, keepdims=True)
        wide += jnp.where(gain_lanes(128, WIDTH, 5, 5 * g), line, 0.0)
    head = jnp.zeros((128, HEAD), F32)
    for g, total in enumerate((query_total, key_total)):
        line = jnp.sum(total, 0, keepdims=True) * SCALE
        head += jnp.where(gain_lanes(128, HEAD, 2, 20 + 2 * g), line, 0.0)
    contract = (((0,), (1,)), ((), ()))
    gain_block = lax.dot_general(
        pick, wide.astype(BF16), contract, preferred_element_type=F32
    ) + lax.dot_general(pick_head, head.astype(BF16), contract, preferred_element_type=F32)
    left = dot_tn(pick_b, query_weight_grad[:, ATT_COLS:])
    part_b[:, :128] = (left[:, :128] + gain_block).astype(BF16)
    part_b[:, 128:256] = left[:, 128:].astype(BF16)
    first_core = meta[3] == 0
    keep_ref[...] = jnp.where(first_core, part_a[...], part_b[...])
    give_ref[...] = jnp.where(first_core, part_b[...], part_a[...])


def attention_back(first, count, meta, attended_grad, probs, kept, earlier, inputs, after):
    starting = earlier is None
    sums = [((KEYS, HEAD), F32), ((KEYS, HEAD), F32), ((count, HEADS * BLOCK, HEAD), F32)]
    in_specs = [
        smem(),
        pl.BlockSpec((BLOCK, HEADS * HEAD), lambda r: (r + first, 0)),
        from_row((HEADS * BLOCK, SPAN), first),
        from_row((HEADS * BLOCK, HEAD), first),
        whole((KEYS, HEAD)),
        whole((KEYS, HEAD)),
    ]
    args = [meta, attended_grad, probs, kept[5], kept[1], kept[2]]
    outs = sums
    if not starting:
        args += [*earlier, *inputs]
        in_specs += [whole(value.shape) for value in (*earlier, *inputs)]
        outs = [((TOKENS, WIDTH), F32), ((TOKENS, WIDTH), BF16)] + [((1024, ATT_COLS), BF16)] * 2
    return call(
        functools.partial(attention_back_kernel, starting, first),
        "attention_back",
        outs,
        in_specs,
        args,
        out_specs=[whole(s) for s, _ in outs],
        scratch=[]
        if starting
        else [pltpu.VMEM(s, d) for s, d in sums] + [pltpu.VMEM((1024, ATT_COLS), BF16)] * 2,
        after=after,
        grid=(count,),
        megabytes=60,
        flops=count * 5 * 10**9,
        moved_bytes=count * 12 * 10**6,
    )


def pack_kernel(meta, *refs):
    sources, keep_ref, give_ref, part = refs[:7], refs[7], refs[8], refs[9]
    held, arrivals = refs[10:17], refs[17]
    copies = [
        pltpu.make_async_copy(source, target, arrivals.at[j])
        for j, (source, target) in enumerate(zip(sources, held))
    ]
    for copy in copies:
        copy.start()
    for copy in copies:
        copy.wait()
    query, key, value, output, gate, up, gains = held
    for half in range(2):
        part[half] = jnp.zeros((8, PACK), F32)
    out_start = ATT_COLS
    feed_start = ATT_COLS + OUT_COLS
    left = HEADS * HEAD - ATT_COLS
    part[0, :5, :ATT_COLS] = query[:, :ATT_COLS].astype(F32)
    part[0, :, out_start:feed_start] = output[:, :OUT_COLS].astype(F32)
    part[0, :5, feed_start:] = gate[...].astype(F32)
    part[1, :5, :left] = query[:, ATT_COLS:].astype(F32)
    part[1, :5, left : left + HEAD] = key[...].astype(F32)
    part[1, :5, left + HEAD : ATT_COLS] = value[...].astype(F32)
    part[1, 5:6, :128] = gains[...].astype(F32)
    part[1, :, out_start : out_start + WIDTH - OUT_COLS] = output[:, OUT_COLS:].astype(F32)
    part[1, :5, feed_start:] = up[...].astype(F32)
    core = meta[3]
    keep_ref[...] = part[core].astype(BF16)
    give_ref[...] = part[1 - core].astype(BF16)


def pack_weights(meta, query, key, value, output, gate, up, gains):
    return call(
        pack_kernel,
        "pack_weights",
        [((8, PACK), BF16)] * 2,
        [smem()] + [anywhere()] * 7,
        [meta, query, key, value, output, gate, up, gains],
        scratch=[pltpu.VMEM((2, 8, PACK), F32)]
        + [
            pltpu.VMEM(held.shape, held.dtype)
            for held in (query, key, value, output, gate, up, gains)
        ]
        + [pltpu.SemaphoreType.DMA((7,))],
        megabytes=60,
        flops=10**6,
        moved_bytes=3 * 10**5,
    )


def pair_kernel(meta, kept, crossed, down, out_ref):
    first_core = meta[3] == 0
    mine, theirs = kept[...].astype(F32), crossed[...].astype(F32)
    upper = jnp.where(first_core, mine, theirs)
    lower = jnp.where(first_core, theirs, mine)
    out_ref[:, :PACK] = jnp.concatenate([upper, lower], 0).astype(BF16)
    out_ref[:, PACK:] = down[...]


def pair_up(meta, kept, crossed, down):
    return call(
        pair_kernel,
        "pair_up",
        [((16, PACK + WIDTH), BF16)],
        [smem()] + [vmem()] * 3,
        [meta, kept, crossed, down],
        megabytes=16,
        flops=10**6,
        moved_bytes=4 * 10**5,
    )[0]


def split_kernel(slot, meta, value, *refs):
    for j in range(4):
        refs[j][...] = value[meta[slot] ^ j]


def split_up(meta, slot, value, after):
    return call(
        functools.partial(split_kernel, slot),
        "split_up",
        [(value.shape[1:], value.dtype)] * 4,
        [smem(), vmem()],
        [meta, value],
        after=after,
        megabytes=16,
        flops=10**6,
        moved_bytes=10**6,
    )


def join_tokens_kernel(slot, meta, *refs):
    for j in range(4):
        refs[4][meta[slot] ^ j] = refs[j][:TAGGED]
        refs[5][meta[slot] ^ j] = refs[j][TAGGED:]


def join_tokens(meta, slot, pieces, after):
    return call(
        functools.partial(join_tokens_kernel, slot),
        "join_tokens",
        [((4, TAGGED, WIDTH), BF16), ((4, BLOCK, WIDTH), BF16)],
        [smem()] + [vmem()] * 4,
        [meta, *pieces],
        after=after,
        megabytes=16,
        flops=10**6,
        moved_bytes=10**6,
    )


def hold_kernel(*refs):
    pass


def hold(values, after):
    return call(
        hold_kernel,
        "hold",
        [(value.shape, value.dtype) for value in values],
        [anywhere()] * len(values),
        values,
        out_specs=[anywhere()] * len(values),
        after=after,
        aliases={j: j for j in range(len(values))},
        megabytes=16,
        flops=10**4,
        moved_bytes=10**4,
    )


def add_pieces_kernel(kept, crossed, *refs):
    rows = refs[0].shape[0]
    for j in range(4):
        here = slice(j * rows, (j + 1) * rows)
        refs[j][...] = (kept[here].astype(F32) + crossed[here].astype(F32)).astype(BF16)


def add_pieces(kept, crossed, after):
    shape = (kept.shape[0] // 4,) + kept.shape[1:]
    return call(
        add_pieces_kernel,
        "add_pieces",
        [(shape, BF16)] * 4,
        [vmem()] * 2,
        [kept, crossed],
        after=after,
        megabytes=60,
        flops=10**7,
        moved_bytes=8 * 10**6,
    )


def line_kernel(*refs):
    total = add_up(refs[0][...], [ref[...] for ref in refs[1:4]]).astype(BF16)
    for j in range(4):
        refs[4 + j][...] = total[j]


def line_up(own, others, after):
    return call(
        line_kernel,
        "line_up",
        [(own.shape[1:], BF16)] * 4,
        [vmem()] * 4,
        [own, *others],
        after=after,
        megabytes=16,
        flops=10**6,
        moved_bytes=2 * 10**6,
    )


def total_kernel(meta, *refs):
    total = add_up(refs[0][...], [ref[...] for ref in refs[1:4]])
    keep_ref, give_ref, down_ref = refs[4:]
    first_core = meta[3] == 0
    upper, lower = total[:8, :PACK], total[8:, :PACK]
    keep_ref[...] = jnp.where(first_core, upper, lower)
    give_ref[...] = jnp.where(first_core, lower, upper)
    down_ref[...] = total[:, PACK:]


def total_up(meta, own, others):
    return call(
        total_kernel,
        "total_up",
        [((8, PACK), F32)] * 2 + [((16, WIDTH), F32)],
        [smem()] + [vmem()] * 4,
        [meta, own, *others],
        megabytes=16,
        flops=10**6,
        moved_bytes=10**6,
    )


def output_kernel(slot, meta, gains, middle_grad, own, returned, mine, block_out, *refs):
    tokens = jnp.concatenate([mine[j, :BLOCK] for j in range(4)], 0).astype(F32)
    inverse = inverse_rms(tokens)
    normed_grad = own[...] + returned[...].astype(F32)
    grad = middle_grad[...] + norm_backward(normed_grad * gains[0:1], tokens * inverse, inverse)
    refs[4][...] = grad.astype(BF16).reshape(4, BLOCK, WIDTH)
    for j in range(4):
        refs[j][0] = block_out[meta[slot] ^ j]
        refs[j][1] = refs[4][meta[slot] ^ j]


def output_pieces(meta, slot, gains, middle_grad, own, returned, mine, block_out):
    return call(
        functools.partial(output_kernel, slot),
        "output_pieces",
        [((2, BLOCK, WIDTH), BF16)] * 4,
        [smem()] + [vmem()] * 6,
        [meta, gains, middle_grad, own, returned, mine, block_out],
        scratch=[pltpu.VMEM((4, BLOCK, WIDTH), BF16)],
        megabytes=16,
        flops=10**7,
        moved_bytes=5 * 10**6,
    )


def join_outputs_kernel(slot, meta, *refs):
    for j in range(4):
        for k in range(2):
            refs[4 + k][meta[slot] ^ j] = refs[j][k]


def join_outputs(meta, slot, pieces):
    return call(
        functools.partial(join_outputs_kernel, slot),
        "join_outputs",
        [((4, BLOCK, WIDTH), BF16)] * 2,
        [smem()] + [vmem()] * 4,
        [meta, *pieces],
        megabytes=16,
        flops=10**6,
        moved_bytes=2 * 10**6,
    )


def stack_kernel(*refs):
    for j in range(4):
        refs[4][j] = refs[j][...]


def stack_kernel(*refs):
    for j in range(4):
        refs[4][j] = refs[j][...]


def stack_both_kernel(*refs):
    for j in range(8):
        refs[8 + j // 4][j % 4] = refs[j][...]


def stack_both(first, second, after):
    return call(
        stack_both_kernel,
        "stack_both",
        [((4,) + first[0].shape, BF16), ((4,) + second[0].shape, BF16)],
        [vmem()] * 8,
        [*first, *second],
        after=after,
        megabytes=16,
        flops=10**6,
        moved_bytes=10**7,
    )


def stack_up(pieces, shape, after):
    return call(
        stack_kernel,
        "stack_up",
        [((4,) + shape, BF16)],
        [vmem()] * 4,
        pieces,
        after=after,
        megabytes=16,
        flops=10**6,
        moved_bytes=4 * 10**6,
    )[0]


def first_slab_kernel(*refs):
    for j in range(4):
        here = slice(j * 64, (j + 1) * 64)
        refs[4][here, :ATT_COLS] = refs[j][:, :, :ATT_COLS].reshape(64, ATT_COLS)
        refs[4][here, ATT_COLS : ATT_COLS + OUT_COLS] = refs[j][
            :, :, ATT_COLS : ATT_COLS + OUT_COLS
        ].reshape(64, OUT_COLS)
        refs[4][here, ATT_COLS + OUT_COLS :] = refs[j][:, :, PACK:].reshape(64, WIDTH)


def first_slab(pieces, after):
    return call(
        first_slab_kernel,
        "first_slab",
        [((256, FIRST_PACK), BF16)],
        [vmem()] * 4,
        pieces,
        after=after,
        megabytes=16,
        flops=10**6,
        moved_bytes=3 * 10**6,
    )[0]


def loose_rows():
    line = lax.broadcasted_iota(jnp.int32, (256, 160), 0)
    row = line & 7
    dense = lax.broadcasted_iota(jnp.int32, (256, 160), 1)
    same = ((line >> 3) * 5 + row == dense) & (row < 5)
    return jnp.where(same, 1.0, 0.0).astype(BF16)


def feed_slab_kernel(*refs):
    feed_ref, loose = refs[4:]
    for j in range(4):
        loose[j * 64 : (j + 1) * 64] = refs[j][:, :, ATT_COLS + OUT_COLS : PACK].reshape(
            64, HIDDEN
        )
    feed_ref[...] = dot_tn(loose_rows(), loose[...]).astype(BF16)


def feed_slab_of(pieces, after):
    return call(
        feed_slab_kernel,
        "feed_slab",
        [((160, HIDDEN), BF16)],
        [vmem()] * 4,
        pieces,
        scratch=[pltpu.VMEM((256, HIDDEN), BF16)],
        after=after,
        megabytes=16,
        flops=2 * 10**8,
        moved_bytes=4 * 10**6,
    )[0]


def merge_kernel(*refs):
    att, feed, down, outs = refs[:4], refs[4:8], refs[8:12], refs[12:]

    def total(pieces):
        return add_up(pieces[0][...], [piece[...] for piece in pieces[1:]]).astype(BF16)

    att_total = total(att).reshape(16, 16, ATT_COLS)
    feed_total = dot(loose_rows(), total(feed)).astype(BF16).reshape(16, 16, HIDDEN)
    down_total = total(down)
    for j in range(4):
        here = slice(j * 4, (j + 1) * 4)
        outs[j][:, :, :ATT_COLS] = att_total[here]
        outs[j][:, :, ATT_COLS : ATT_COLS + HIDDEN] = feed_total[here]
        outs[j][:, :, ATT_COLS + HIDDEN :] = down_total[here]


def merge_grads(att, feed, down):
    return call(
        merge_kernel,
        "merge_grads",
        [((4, 16, PACK + WIDTH), BF16)] * 4,
        [vmem()] * 12,
        [*att, *feed, *down],
        megabytes=60,
        flops=2 * 10**8,
        moved_bytes=8 * 10**6,
    )


def unpack_kernel(meta, mine, theirs, query, key, value, output, gate, up, gains):
    first_core = meta[3] == 0
    part_a = jnp.where(first_core, mine[...], theirs[...])
    part_b = jnp.where(first_core, theirs[...], mine[...])
    left = HEADS * HEAD - ATT_COLS
    feed_end = ATT_COLS + HIDDEN
    query[:, :ATT_COLS] = part_a[:5, :ATT_COLS]
    query[:, ATT_COLS:] = part_b[:5, :left]
    key[...] = part_b[:5, left : left + HEAD]
    value[...] = part_b[:5, left + HEAD : ATT_COLS]
    gate[...] = part_a[:5, ATT_COLS:feed_end]
    up[...] = part_b[:5, ATT_COLS:feed_end]
    output[:, :OUT_COLS] = part_a[:, feed_end:]
    output[:, OUT_COLS:] = part_b[:, feed_end : feed_end + WIDTH - OUT_COLS]
    gains[...] = part_b[5:6, :128]


def unpack_grads(meta, mine, theirs):
    return call(
        unpack_kernel,
        "unpack_grads",
        [
            ((5, HEADS * HEAD), F32),
            ((5, HEAD), F32),
            ((5, HEAD), F32),
            ((8, WIDTH), F32),
            ((5, HIDDEN), F32),
            ((5, HIDDEN), F32),
            ((1, 128), F32),
        ],
        [smem()] + [vmem()] * 2,
        [meta, mine, theirs],
        megabytes=16,
        flops=10**6,
        moved_bytes=4 * 10**5,
    )


def on_device(
    hidden_in,
    segment_ids,
    cotangent,
    attn_gain,
    query_weight,
    key_weight,
    value_weight,
    query_gain,
    key_gain,
    output_weight,
    post_attn_gain,
    ffn_gain,
    gate_weight,
    up_weight,
    down_weight,
    post_ffn_gain,
):
    me = my_place()
    core = me["c"]
    first_core = core == 0
    row = 2 * ((me["x"] ^ (me["x"] >> 1)) & 1) + core
    member = 2 * (me["x"] & 1) + core
    place = (me["y"] >> 1) * 1024 + (me["x"] >> 1) * TOKENS
    meta = jnp.stack([me["z"], me["y"], me["x"], core, place, row, member]).astype(jnp.int32)
    row_slot, member_slot = 5, 6

    def pick(value_first, value_second):
        return jnp.where(first_core, value_first, value_second)

    positions = place + jnp.arange(-TOKENS, TOKENS, dtype=jnp.int32)
    frequency = jnp.exp(
        jnp.arange(HEAD // 2, dtype=F32) * (-2.0 * math.log(ROPE_BASE) / HEAD)
    )
    angles = positions.astype(F32)[:, None] * frequency[None]
    tables = (jnp.cos(angles), jnp.sin(angles))

    gains = jnp.zeros((128,), F32)
    start = 0
    for gain in (attn_gain, post_attn_gain, ffn_gain, post_ffn_gain, query_gain, key_gain):
        size = gain.shape[0]
        gains = gains + jnp.pad(gain.astype(F32), (start, 128 - start - size))
        start += size
    kept, given = pack_weights(
        meta,
        query_weight,
        key_weight,
        value_weight,
        output_weight,
        gate_weight,
        up_weight,
        gains.reshape(1, 128),
    )
    pair = pair_up(meta, kept, swap(given), down_weight)
    near_chips = arrived(pair, 0)

    segments = segment_ids.reshape(4, 1, BLOCK).astype(BF16)
    segments = jnp.pad(segments, ((0, 0), (0, TAGGED - BLOCK - 1), (0, WIDTH - BLOCK)))
    dealing = jnp.concatenate(
        [
            hidden_in.reshape(4, BLOCK, WIDTH),
            segments,
            cotangent.reshape(4, BLOCK, WIDTH),
        ],
        1,
    )
    own, one, two, three = split_up(meta, row_slot, dealing, [])
    pieces = [own, swap(one), exchange(two, False), exchange(three, True)]
    mine, cotangent_mine = join_tokens(meta, member_slot, pieces, [pair])
    near, before = next_chunk(mine, me["x"] < 2)

    line = stack_up([pair, *near_chips], pair.shape, [mine])
    plane = [line, *arrived(line, 1)]
    plane = [line, *arrived(line, 1)]
    slab = first_slab(plane, [*tables, near])
    first_own = [slab, *arrived(slab, 2)]
    first_other = [swap(value) for value in first_own]
    feed_slab = feed_slab_of(plane, first_own[1:])

    grid = jnp.arange(64, dtype=jnp.int32)
    chips = [chip_of([me["z"], me["y"], me["x"]], order, grid) for order in ORDERS]
    held, crossed = pick(chips[0], chips[1]), pick(chips[1], chips[0])
    table = jnp.stack([*chips, held * 2 + core, crossed * 2 + 1 - core]).astype(jnp.int32)

    forward = attention_blocks(0, 4, meta, mine, before, tables, first_own + first_other, None, [])
    made, kept_values, (attended, probs) = forward[:3], forward[3:9], forward[9:]
    feed_own = [feed_slab, *hold(arrived(feed_slab, 2), [attended])]
    (
        block_out,
        middle_grad,
        attended_grad,
        feed_gain,
        keep_feed,
        give_feed,
        keep_down,
        give_down,
    ) = feed_forward(
        meta,
        table,
        made[1],
        mine,
        cotangent_mine,
        attended,
        feed_own,
        [swap(value) for value in feed_own],
        first_own,
        first_other,
    )
    back = attention_back(2, 2, meta, attended_grad, probs, kept_values, None, None, [])
    feed_sum = add_pieces(keep_feed, swap(give_feed), [back[0]])
    down_sum = add_pieces(keep_down, swap(give_down), [back[0]])
    normed_grad, to_before, keep_att, give_att = attention_back(
        0,
        2,
        meta,
        attended_grad,
        probs,
        kept_values,
        back,
        (
            *made,
            *tables,
            mine,
            before,
            kept_values[0],
            kept_values[3],
            kept_values[4],
            feed_gain,
        ),
        [*feed_sum, *down_sum],
    )
    feed_in = received(feed_sum, 2)
    down_in = received(down_sum, 2)

    give_att = hold([give_att], [*feed_in, *down_in[:2]])[0]
    att_sum = add_pieces(keep_att, swap(give_att), [])
    plane = merge_grads(
        [att_sum[0], *received(att_sum, 2)], [feed_sum[0], *feed_in], [down_sum[0], *down_in]
    )
    returned = chunk_before(to_before)
    own, one, two, three = output_pieces(
        meta, member_slot, made[1], middle_grad, normed_grad, returned, mine, block_out
    )
    line = line_up(plane[0], received(plane, 1), [own])
    kept_grads, given_grads, grad_down = total_up(meta, line[0], received(line, 0))
    grad_query, grad_key, grad_value, grad_output, grad_gate, grad_up, gain_grads = unpack_grads(
        meta, kept_grads, swap(given_grads)
    )
    gain_grads = gain_grads.reshape(128)

    block_out, input_grad = join_outputs(
        meta, row_slot, [own, swap(one), exchange(two, False), exchange(three, True)]
    )
    return (
        block_out.reshape(hidden_in.shape),
        input_grad.reshape(hidden_in.shape),
        gain_grads[0:5],
        grad_query,
        grad_key,
        grad_value,
        gain_grads[20:22],
        gain_grads[22:24],
        grad_output,
        gain_grads[5:10],
        gain_grads[10:15],
        grad_gate,
        grad_up,
        grad_down,
        gain_grads[15:20],
    )


def solution(mesh):
    rows = P(None, "dp", "seq", None)
    shard = P(("dp", "seq"), None)
    vector = P(("dp", "seq"))
    return jax.shard_map(
        on_device,
        mesh=mesh,
        in_specs=(rows, P(None, "dp", "seq"), rows)
        + (vector, shard, shard, shard, vector, vector, shard, vector)
        + (vector, shard, shard, shard, vector),
        out_specs=(rows, rows)
        + (vector, shard, shard, shard, vector, vector, shard, vector)
        + (vector, shard, shard, shard, vector),
        check_vma=False,
    )
```

```python
import functools
import math

import jax
import jax.numpy as jnp
from jax import lax
from jax.experimental import pallas as pl
from jax.experimental.pallas import tpu as pltpu
from jax.sharding import PartitionSpec as P

WINDOW = 512
HALO = 4
BLOCK = 128
TOKENS = 512
KEYS = 1024
WIDTH = 640
HEADS = 4
HEAD = 256
HIDDEN = 2048
SPAN = (HALO + 1) * BLOCK
CHUNK = 512
TAGGED = BLOCK + 16
EPSILON = 1e-06
ROPE_BASE = 10000.0
MASKED = -1e30
SCALE = HEAD ** (-0.5)
F32 = jnp.float32
BF16 = jnp.bfloat16

AXES = ("dp", "seq")
SIZE = {"x": 4, "y": 4, "z": 4, "c": 2}
GATHER = (("x", "y", "z"), ("y", "z", "x"))
SCATTER = (("y", "x", "z"), ("y", "z", "x"))
ATT_COLS = 768
OUT_COLS = 384
DOWN_PACK = OUT_COLS + WIDTH
PACK = ATT_COLS + OUT_COLS + HIDDEN
FIRST_PACK = ATT_COLS + DOWN_PACK


def shard_of(z, y, x, c):
    return z * 32 + (y % 2) * 16 + (y // 2) * 8 + x * 2 + c


def moved(axis_of_core, by):
    pairs = []
    for z in range(4):
        for y in range(4):
            for x in range(4):
                for c in range(2):
                    place = {"z": z, "y": y, "x": x, "c": c}
                    axis = axis_of_core[c]
                    place[axis] = (place[axis] + by) % SIZE[axis]
                    pairs.append((shard_of(z, y, x, c), shard_of(**place)))
    return pairs


def send(value, orders, phase, by):
    axes = (orders[0][phase], orders[1][phase])
    return lax.ppermute(value, AXES, moved(axes, by))


def swap(value):
    return lax.ppermute(value, AXES, moved(("c", "c"), 1))


def exchange(value, flip):
    pairs = []
    for i in range(128):
        pairs.append((i, i ^ (3 if flip else 2)))
    return lax.ppermute(value, AXES, pairs)


def next_chunk(value, first_half):
    along, across = [], []
    for dp in range(8):
        for c in range(2):
            for x in range(4):
                for yh in range(2):
                    if x >= 2 and yh == 1:
                        continue
                    here = dp * 16 + yh * 8 + x * 2 + c
                    along.append((here, here + (3 - 2 * x) * 2))
            for x in range(2):
                here = dp * 16 + x * 2 + c
                across.append((here, here + 8))
    near = lax.ppermute(value, AXES, along)
    return near, jnp.where(first_half, lax.ppermute(near, AXES, across), near)


def chunk_before(value):
    pairs = []
    for dp in range(8):
        for yh in range(2):
            for x in range(4):
                for c in range(2):
                    if x >= 2 and yh == 1:
                        continue
                    here = dp * 16 + yh * 8 + x * 2 + c
                    there = dp * 16 + (yh + (x >= 2)) * 8 + (3 - x) * 2 + c
                    pairs.append((there, here))
    return lax.ppermute(value, AXES, pairs)


def my_place():
    dp, seq = lax.axis_index("dp"), lax.axis_index("seq")
    return {"z": dp // 2, "y": (seq // 8) * 2 + dp % 2, "x": (seq // 2) % 4, "c": seq % 2}


def arrived(value, phase):
    two, one, three = [send(value, GATHER, phase, -by) for by in (2, 1, 3)]
    return [one, two, three]


def received(pieces, phase):
    return [send(pieces[by], SCATTER, phase, by) for by in (2, 1, 3)]


def add_up(own, others):
    total = own.astype(F32)
    for other in others:
        total = total + other.astype(F32)
    return total


def chip_at(meta, order, j3, j2, j1):
    place = {
        order[2]: (meta["zyx".index(order[2])] + j3) & 3,
        order[1]: (meta["zyx".index(order[1])] + j2) & 3,
        order[0]: (meta["zyx".index(order[0])] + j1) & 3,
    }
    z, y, x = place["z"], place["y"], place["x"]
    return z * 16 + (y & 1) * 8 + (y >> 1) * 4 + x


def chip_of(meta, order, i):
    return chip_at(meta, order, i >> 4, (i >> 2) & 3, i & 3)


def slab_rows(meta, order, rows_held):
    line = lax.broadcasted_iota(jnp.int32, (1, 128 * rows_held), 1)
    if rows_held == 8:
        both, row = line >> 3, line & 7
    else:
        both = lax.shift_right_logical(line * 52429, 18)
        row = line - both * 5
    return chip_of(meta, order, both >> 1) * 2 + (both & 1), row


def dot(a, b):
    return jnp.dot(a, b, preferred_element_type=F32)


def dot_nt(a, b):
    return lax.dot_general(a, b, (((1,), (1,)), ((), ())), preferred_element_type=F32)


def dot_tn(a, b):
    return lax.dot_general(a, b, (((0,), (0,)), ((), ())), preferred_element_type=F32)


def add_rows(values):
    total = values[:8]
    for first in range(8, values.shape[0], 8):
        total = total + values[first : first + 8]
    return total


def one_hot(index_row, count):
    places = lax.broadcasted_iota(jnp.int32, (count, index_row.shape[1]), 0)
    return jnp.where(places == index_row, 1.0, 0.0).astype(BF16)


def inverse_rms(values):
    return lax.rsqrt(jnp.mean(values * values, -1, keepdims=True) + EPSILON)


def norm_backward(grad_hat, unit_value, inverse):
    return inverse * (grad_hat - unit_value * jnp.mean(grad_hat * unit_value, -1, keepdims=True))


def rotate(values, cosine, sine):
    first, second = values[:, : HEAD // 2], values[:, HEAD // 2 :]
    return jnp.concatenate(
        [first * cosine - second * sine, second * cosine + first * sine], axis=-1
    )


def vmem():
    return pl.BlockSpec(memory_space=pltpu.VMEM)


def smem():
    return pl.BlockSpec(memory_space=pltpu.SMEM)


def anywhere():
    return pl.BlockSpec(memory_space=pl.ANY)


def whole(shape):
    return pl.BlockSpec(shape, lambda r: (0,) * len(shape))


def by_row(shape):
    return pl.BlockSpec((1,) + shape, lambda r: (r,) + (0,) * len(shape))


def from_row(shape, first):
    return pl.BlockSpec((1,) + shape, lambda r: (r + first,) + (0,) * len(shape))


def call(
    kernel,
    name,
    outs,
    in_specs,
    args,
    out_specs=None,
    scratch=(),
    after=(),
    aliases=None,
    grid=(),
    megabytes=58,
    flops=0,
    moved_bytes=0,
):
    after = list(after)
    count = len(in_specs)

    def body(*refs):
        kernel(*refs[:count], *refs[count + len(after) :])

    return pl.pallas_call(
        body,
        grid=grid,
        out_shape=[jax.ShapeDtypeStruct(s, d) for s, d in outs],
        in_specs=list(in_specs) + [anywhere()] * len(after),
        out_specs=[vmem()] * len(outs) if out_specs is None else out_specs,
        scratch_shapes=list(scratch),
        input_output_aliases=aliases or {},
        compiler_params=pltpu.CompilerParams(vmem_limit_bytes=megabytes * 2**20),
        cost_estimate=pl.CostEstimate(
            flops=flops, bytes_accessed=moved_bytes, transcendentals=0
        ),
        name=name,
    )(*args, *after)


def line_picks(meta, orders):
    shard_a, row_a = slab_rows(meta, orders[0], 8)
    shard_b, row_b = slab_rows(meta, orders[1], 8)
    pick_a = one_hot(jnp.where(row_a < 5, shard_a * 5 + row_a, -1), WIDTH)
    pick_b = one_hot(jnp.where(row_b < 5, shard_b * 5 + row_b, -1), WIDTH)
    return pick_a, pick_b, jnp.where(row_b == 5, shard_b, -1)


def gain_picks(shard_line):
    wide = lax.broadcasted_iota(jnp.int32, (WIDTH, shard_line.shape[1]), 0)
    first = shard_line * 5
    pick = jnp.where((wide >= first) & (wide < first + 5) & (first >= 0), 1.0, 0.0).astype(BF16)
    head = lax.broadcasted_iota(jnp.int32, (HEAD, shard_line.shape[1]), 0)
    pick_head = jnp.where((head >> 1) == shard_line, 1.0, 0.0).astype(BF16)
    return pick, pick_head


def gain_lanes(count, width, per_shard, first):
    lane = lax.broadcasted_iota(jnp.int32, (count, width), 0)
    entry = lax.broadcasted_iota(jnp.int32, (count, width), 1)
    if per_shard == 5:
        place = entry - lax.shift_right_logical(entry * 52429, 18) * 5
    else:
        place = entry & 1
    return lane == place + first


def both_parts(meta, own, other, part_a, part_b, rows):
    @pl.when(meta[3] == 0)
    def _():
        for j in range(4):
            part_a[j * rows : (j + 1) * rows] = own[j][...]
            part_b[j * rows : (j + 1) * rows] = other[j][...]

    @pl.when(meta[3] != 0)
    def _():
        for j in range(4):
            part_a[j * rows : (j + 1) * rows] = other[j][...]
            part_b[j * rows : (j + 1) * rows] = own[j][...]


def weights_kernel(meta, *refs):
    own, other = refs[:4], refs[4:8]
    weights_ref, gains_ref, head_gains_ref, part_a, part_b = refs[8:]
    both_parts(meta, own, other, part_a, part_b, 256)
    pick_a, pick_b, gain_shard = line_picks(meta, GATHER)
    weights_ref[:, :ATT_COLS] = dot(pick_a, part_a[...]).astype(BF16)
    weights_ref[:, ATT_COLS:] = dot(pick_b, part_b[...]).astype(BF16)
    pick, pick_head = gain_picks(gain_shard)
    block = part_b[:, :128]
    contract = (((0,), (1,)), ((), ()))
    wide = lax.dot_general(block, pick, contract, preferred_element_type=F32)[:24]
    head = lax.dot_general(block, pick_head, contract, preferred_element_type=F32)[:24]
    gains_ref[...] = jnp.zeros_like(gains_ref)
    head_gains_ref[...] = jnp.zeros_like(head_gains_ref)
    for g in range(4):
        chosen = jnp.where(gain_lanes(24, WIDTH, 5, 5 * g), wide, 0.0)
        gains_ref[g : g + 1] = jnp.sum(chosen, 0, keepdims=True)
    for g in range(2):
        chosen = jnp.where(gain_lanes(24, HEAD, 2, 20 + 2 * g), head, 0.0)
        head_gains_ref[4 + g : 5 + g] = jnp.sum(chosen, 0, keepdims=True)


def prepare_kernel(weights, gains, head_gains, cosine, sine, mine, before, *refs):
    normed_ref, keys_ref, values_ref, key_pre_ref, query_pre_ref, queries_ref = refs
    tokens = jnp.concatenate(
        [part[j, :BLOCK] for part in (before, mine) for j in range(4)], 0
    ).astype(F32)
    normed = (tokens * inverse_rms(tokens) * gains[0:1]).astype(BF16)
    normed_ref[...] = normed
    key_value = dot(normed, weights[:, HEADS * HEAD :])
    key_pre = key_value[:, :HEAD]
    key_pre_ref[...] = key_pre.astype(BF16)
    values_ref[...] = key_value[:, HEAD:].astype(BF16)
    query_pre = dot(normed[TOKENS:], weights[:, : HEADS * HEAD])
    query_pre_ref[...] = query_pre.astype(BF16)
    query_gain, key_gain = head_gains[4:5], head_gains[5:6]
    keys = rotate(key_pre * inverse_rms(key_pre) * key_gain, cosine[...], sine[...])
    keys_ref[...] = keys.astype(BF16)
    for h in range(HEADS):
        pre = query_pre[:, h * HEAD : (h + 1) * HEAD]
        turned = rotate(
            pre * inverse_rms(pre) * query_gain, cosine[TOKENS:], sine[TOKENS:]
        ).astype(BF16)
        for j in range(4):
            queries_ref[j, h * BLOCK : (h + 1) * BLOCK] = turned[j * BLOCK : (j + 1) * BLOCK]


def attention_kernel(first, meta, mine, before, *refs):
    step = pl.program_id(0)
    if first == 0:
        cosine, sine, slabs, refs = refs[0], refs[1], refs[2:10], refs[10:]
        results, refs = refs[:9], refs[9:]
        held, leaving = refs[5:14], refs[14]
        made, kept = held[:3], held[3:]
        copies = [
            pltpu.make_async_copy(source, target, leaving.at[j])
            for j, (source, target) in enumerate(zip(held, results))
        ]

        @pl.when(step == 0)
        def _():
            weights_kernel(meta, *slabs, *made, refs[3], refs[4])
            prepare_kernel(*made, cosine, sine, mine, before, *kept)
            for copy in copies:
                copy.start()

        @pl.when(step == pl.num_programs(0) - 1)
        def _():
            for copy in copies:
                copy.wait()

        _, keys_ref, values_ref, _, _, queries_ref = kept
    else:
        keys_ref, values_ref, queries_ref = refs[:3]
        refs = refs[3:]
    attended_ref, probs_ref, line_s = refs[:3]
    place = step + first
    lines = [
        part[j, BLOCK:].astype(F32)[0:1, :BLOCK] for part in (before, mine) for j in range(4)
    ]
    line_s[...] = jnp.broadcast_to(jnp.concatenate(lines, 1), line_s.shape)
    start = pl.multiple_of(place * BLOCK, BLOCK)
    window = pl.ds(start, SPAN)
    square = (BLOCK, BLOCK)
    diagonal = lax.broadcasted_iota(jnp.int32, square, 0) == lax.broadcasted_iota(
        jnp.int32, square, 1
    )
    own_line = line_s[0:1, pl.ds(pl.multiple_of(start + TOKENS, BLOCK), BLOCK)]
    own_column = jnp.sum(jnp.where(diagonal, own_line, 0.0), 1, keepdims=True)
    query_place = lax.broadcasted_iota(jnp.int32, (BLOCK, SPAN), 0)
    key_place = lax.broadcasted_iota(jnp.int32, (BLOCK, SPAN), 1) - HALO * BLOCK
    visible = (
        (key_place <= query_place)
        & (query_place - key_place < WINDOW)
        & (key_place + meta[4] + start >= 0)
        & (own_column == line_s[0:1, window])
    )
    bias = jnp.where(visible, 0.0, MASKED)
    queries = queries_ref[place if first == 0 else 0]
    scores = dot_nt(queries, keys_ref[window]) * SCALE + jnp.concatenate([bias] * HEADS, 0)
    terms = jnp.exp(scores - jnp.max(scores, -1, keepdims=True))
    probs = (terms * (1.0 / jnp.sum(terms, -1, keepdims=True))).astype(BF16)
    probs_ref[0] = probs
    mixed = dot(probs, values_ref[window]).astype(BF16)
    for h in range(HEADS):
        attended_ref[0, :, h * HEAD : (h + 1) * HEAD] = mixed[h * BLOCK : (h + 1) * BLOCK]


MADE = [((WIDTH, 1536), BF16), ((8, WIDTH), F32), ((8, HEAD), F32)]
KEPT = [
    ((KEYS, WIDTH), BF16),
    ((KEYS, HEAD), BF16),
    ((KEYS, HEAD), BF16),
    ((KEYS, HEAD), BF16),
    ((TOKENS, HEADS * HEAD), BF16),
    ((4, HEADS * BLOCK, HEAD), BF16),
]


def attention_blocks(first, count, meta, mine, before, tables, slabs, kept, after):
    outs = [((count, BLOCK, HEADS * HEAD), BF16), ((count, HEADS * BLOCK, SPAN), BF16)]
    making = first == 0
    fixed = MADE + KEPT if making else []
    if making:
        more = [*tables, *slabs]
        more_specs = [whole((KEYS, HEAD // 2))] * 2 + [whole((256, ATT_COLS))] * 8
    else:
        more = [kept[1], kept[2], kept[5]]
        more_specs = [whole((KEYS, HEAD))] * 2 + [from_row((HEADS * BLOCK, HEAD), first)]
    return call(
        functools.partial(attention_kernel, first),
        "attention_blocks",
        fixed + outs,
        [smem()] + [whole((4, TAGGED, WIDTH))] * 2 + more_specs,
        [meta, mine, before, *more],
        out_specs=[anywhere()] * len(fixed) + [by_row(s[1:]) for s, _ in outs],
        scratch=[pltpu.VMEM((8, KEYS), F32)]
        + [pltpu.VMEM((1024, ATT_COLS), BF16)] * 2
        + [pltpu.VMEM(s, d) for s, d in fixed]
        + [pltpu.SemaphoreType.DMA((9,))],
        after=after,
        grid=(count,),
        megabytes=60,
        flops=count * 4 * 10**9,
        moved_bytes=count * 10**7,
    )


def gelu_parts(gate):
    square = gate * gate
    bent = jnp.tanh(gate * (0.7978845608 + (0.7978845608 * 0.044715) * square))
    half = 0.5 + 0.5 * bent
    slope = half + gate * (1.0 - bent * bent) * (
        (0.5 * 0.7978845608) + (0.5 * 0.7978845608 * 3 * 0.044715) * square
    )
    return gate * half, slope


def feed_kernel(meta, table, gains, mine, cotangent, *refs):
    attended, refs = refs[0], refs[1:]
    own, other, own_down, other_down = refs[:4], refs[4:8], refs[8:12], refs[12:16]
    refs = refs[16:]
    block_out_ref, middle_grad_ref, attended_grad_ref, gain_ref = refs[:4]
    keep_ref, give_ref, keep_down_ref, give_down_ref = refs[4:8]
    (
        gate_w,
        up_w,
        down_w,
        output_w,
        active_s,
        slope_s,
        inner_s,
        inputs_s,
        grads_s,
        keep_s,
        give_s,
        grad_down,
        keep_down_s,
        give_down_s,
        arrivals,
        leaving,
    ) = refs[8:]
    core = meta[3]
    first_core = core == 0

    def fetch(sources, target, first):
        return [
            pltpu.make_async_copy(
                sources[j], target.at[j * 160 : (j + 1) * 160], arrivals.at[first + j]
            )
            for j in range(4)
        ]

    @pl.when(first_core)
    def _():
        for copy in fetch(own, gate_w, 0) + fetch(other, up_w, 4):
            copy.start()

    @pl.when(jnp.logical_not(first_core))
    def _():
        for copy in fetch(other, gate_w, 0) + fetch(own, up_w, 4):
            copy.start()

    for j in range(4):

        def place(i, carry, j=j):
            here = pl.ds(pl.multiple_of(i * 16, 16), 16)
            mine, theirs = own_down[j][here, ATT_COLS:], other_down[j][here, ATT_COLS:]
            down_w[table[2, j * 16 + i]] = mine[:, OUT_COLS:]
            down_w[table[3, j * 16 + i]] = theirs[:, OUT_COLS:]
            mine, theirs = mine[:, :OUT_COLS], theirs[:, :OUT_COLS]
            output_w[table[0, j * 16 + i], :, :OUT_COLS] = jnp.where(first_core, mine, theirs)
            output_w[table[1, j * 16 + i], :, OUT_COLS:] = jnp.where(first_core, theirs, mine)[
                :, : WIDTH - OUT_COLS
            ]
            return carry

        lax.fori_loop(0, 16, place, 0, unroll=8)

    picks = []
    for order in (*GATHER, SCATTER[0]):
        shard, row = slab_rows(meta, order, 5)
        picks.append(one_hot(shard * 5 + row, WIDTH))
    post_attn_gain, ffn_gain, post_ffn_gain = gains[1:2], gains[2:3], gains[3:4]
    output_weight = output_w[...].reshape(HEADS * HEAD, WIDTH)
    all_attended = attended[...].reshape(TOKENS, HEADS * HEAD)
    projected = dot(all_attended, output_weight)
    proj_inverse = inverse_rms(projected)
    proj_unit = projected * proj_inverse
    tokens = jnp.concatenate([mine[j, :BLOCK] for j in range(4)], 0)
    middle = tokens.astype(F32) + proj_unit * post_attn_gain
    mid_inverse = inverse_rms(middle)
    mid_unit = middle * mid_inverse
    ffn_in = (mid_unit * ffn_gain).astype(BF16)
    input_a = dot(ffn_in, picks[0]).astype(BF16)
    input_b = dot(ffn_in, picks[1]).astype(BF16)
    inputs_s[core] = dot(ffn_in, picks[2]).astype(BF16)
    inputs_s[1 - core] = input_b
    for copy in fetch(own, gate_w, 0) + fetch(own, up_w, 4):
        copy.wait()
    down = jnp.zeros((TOKENS, WIDTH), F32)
    for n in range(HIDDEN // CHUNK):
        columns = slice(n * CHUNK, (n + 1) * CHUNK)
        gate = dot(input_a, gate_w[:, columns])
        up = dot(input_b, up_w[:, columns])
        active, slope = gelu_parts(gate)
        active_s[:, columns] = active.astype(BF16)
        slope_s[:, columns] = (slope * up).astype(BF16)
        inner = (active * up).astype(BF16)
        inner_s[:, columns] = inner
        blocks = slice(n * (CHUNK // 16), (n + 1) * (CHUNK // 16))
        down += dot(inner, down_w[blocks].reshape(CHUNK, WIDTH))
    down_inverse = inverse_rms(down)
    down_unit = down * down_inverse
    block_out = (middle + down_unit * post_ffn_gain).astype(BF16)
    block_out_ref[...] = block_out.reshape(4, BLOCK, WIDTH)
    out_grad = cotangent[...].reshape(TOKENS, WIDTH).astype(F32)
    gain_ref[16:24] = add_rows(out_grad * down_unit)
    down_grad = norm_backward(out_grad * post_ffn_gain, down_unit, down_inverse).astype(BF16)
    sum_a = jnp.zeros((TOKENS, WIDTH), F32)
    sum_b = jnp.zeros((TOKENS, WIDTH), F32)
    sent = []
    for n in range(HIDDEN // CHUNK):
        columns = slice(n * CHUNK, (n + 1) * CHUNK)
        blocks = slice(n * (CHUNK // 16), (n + 1) * (CHUNK // 16))
        inner_grad = dot_nt(down_grad, down_w[blocks].reshape(CHUNK, WIDTH))
        gate_grad = (inner_grad * slope_s[:, columns].astype(F32)).astype(BF16)
        up_grad = (inner_grad * active_s[:, columns].astype(F32)).astype(BF16)
        grads_s[core] = gate_grad
        grads_s[1 - core] = up_grad
        grad_down[blocks] = (
            dot_tn(inner_s[:, columns], down_grad).astype(BF16).reshape(CHUNK // 16, 16, WIDTH)
        )
        keep_s[:, columns] = dot_tn(inputs_s[0], grads_s[0]).astype(BF16)
        give_s[:, columns] = dot_tn(inputs_s[1], grads_s[1]).astype(BF16)
        for source, target, k in ((keep_s, keep_ref, n), (give_s, give_ref, 4 + n)):
            copy = pltpu.make_async_copy(
                source.at[:, columns], target.at[:, columns], leaving.at[k]
            )
            copy.start()
            sent.append(copy)
        sum_a += dot_nt(gate_grad, gate_w[:, columns])
        sum_b += dot_nt(up_grad, up_w[:, columns])
    ffn_in_grad = dot_nt(sum_a.astype(BF16), picks[0]) + dot_nt(sum_b.astype(BF16), picks[1])
    gain_ref[8:16] = add_rows(ffn_in_grad * mid_unit)
    middle_grad = out_grad + norm_backward(ffn_in_grad * ffn_gain, mid_unit, mid_inverse)
    middle_grad_ref[...] = middle_grad
    gain_ref[0:8] = add_rows(middle_grad * proj_unit)
    proj_grad = norm_backward(middle_grad * post_attn_gain, proj_unit, proj_inverse).astype(BF16)
    attended_grad_ref[...] = dot_nt(proj_grad, output_weight).astype(BF16)
    output_w[...] = dot_tn(all_attended, proj_grad).astype(BF16).reshape(64, 16, WIDTH)
    pad = jnp.zeros((16, 2 * OUT_COLS - WIDTH), BF16)

    def hand(i, carry):
        grad_a = output_w[table[4, i], :, :OUT_COLS]
        grad_b = jnp.concatenate([output_w[table[5, i], :, OUT_COLS:], pad], 1)
        keep_down_s[i, :, :OUT_COLS] = jnp.where(first_core, grad_a, grad_b)
        give_down_s[i, :, :OUT_COLS] = jnp.where(first_core, grad_b, grad_a)
        keep_down_s[i, :, OUT_COLS:] = grad_down[table[6, i]]
        give_down_s[i, :, OUT_COLS:] = grad_down[table[7, i]]
        return carry

    lax.fori_loop(0, 64, hand, 0, unroll=8)
    for source, target, k in (
        (keep_down_s, keep_down_ref, 8),
        (give_down_s, give_down_ref, 9),
    ):
        copy = pltpu.make_async_copy(source, target, leaving.at[k])
        copy.start()
        sent.append(copy)
    for copy in sent:
        copy.wait()


def feed_forward(
    meta, table, gains, mine, cotangent, attended, own, other, own_down, other_down
):
    return call(
        feed_kernel,
        "feed_forward",
        [
            ((4, BLOCK, WIDTH), BF16),
            ((TOKENS, WIDTH), F32),
            ((TOKENS, HEADS * HEAD), BF16),
            ((24, WIDTH), F32),
            ((WIDTH, HIDDEN), BF16),
            ((WIDTH, HIDDEN), BF16),
            ((64, 16, DOWN_PACK), BF16),
            ((64, 16, DOWN_PACK), BF16),
        ],
        [smem(), smem()] + [vmem()] * 4 + [anywhere()] * 8 + [vmem()] * 8,
        [meta, table, gains, mine, cotangent, attended, *own, *other, *own_down, *other_down],
        out_specs=[vmem()] * 4 + [anywhere()] * 4,
        scratch=[
            pltpu.VMEM((WIDTH, HIDDEN), BF16),
            pltpu.VMEM((WIDTH, HIDDEN), BF16),
            pltpu.VMEM((128, 16, WIDTH), BF16),
            pltpu.VMEM((64, 16, WIDTH), BF16),
            pltpu.VMEM((TOKENS, HIDDEN), BF16),
            pltpu.VMEM((TOKENS, HIDDEN), BF16),
            pltpu.VMEM((TOKENS, HIDDEN), BF16),
            pltpu.VMEM((2, TOKENS, WIDTH), BF16),
            pltpu.VMEM((2, TOKENS, CHUNK), BF16),
            pltpu.VMEM((WIDTH, HIDDEN), BF16),
            pltpu.VMEM((WIDTH, HIDDEN), BF16),
            pltpu.VMEM((128, 16, WIDTH), BF16),
            pltpu.VMEM((64, 16, DOWN_PACK), BF16),
            pltpu.VMEM((64, 16, DOWN_PACK), BF16),
            pltpu.SemaphoreType.DMA((8,)),
            pltpu.SemaphoreType.DMA((10,)),
        ],
        megabytes=60,
        flops=17 * 10**9,
        moved_bytes=30 * 10**6,
    )


def attention_back_kernel(starting, first, meta, attended_grad, probs, queries, keys, values, *refs):
    step = pl.program_id(0)
    if starting:
        key_sum, value_sum, query_sum = refs

        @pl.when(step == 0)
        def _():
            key_sum[...] = jnp.zeros_like(key_sum)
            value_sum[...] = jnp.zeros_like(value_sum)
    else:
        sources, outs = refs[:14], refs[14:18]
        key_sum, value_sum, query_sum, part_a, part_b, arrivals = refs[18:24]
        held = refs[24:]
        copies = [
            pltpu.make_async_copy(source, target, arrivals.at[j])
            for j, (source, target) in enumerate(zip(sources, held))
        ]

        @pl.when(step == 0)
        def _():
            for copy in copies:
                copy.start()
            key_sum[...] = jnp.zeros_like(key_sum)
            value_sum[...] = jnp.zeros_like(value_sum)

    window = pl.ds(pl.multiple_of((step + first) * BLOCK, BLOCK), SPAN)
    mixed_grad = jnp.concatenate(
        [attended_grad[:, h * HEAD : (h + 1) * HEAD] for h in range(HEADS)], 0
    )
    prob_grad = dot_nt(mixed_grad, values[window])
    soft = probs[0].astype(F32)
    row_dot = jnp.sum(soft * prob_grad, -1, keepdims=True)
    score_grad = (soft * (prob_grad - row_dot)).astype(BF16)
    query_sum[step] = dot(score_grad, keys[window])
    key_sum[window] += dot_tn(score_grad, queries[0])
    value_sum[window] += dot_tn(probs[0], mixed_grad)
    if starting:
        return

    @pl.when(step == pl.num_programs(0) - 1)
    def _():
        for copy in copies:
            copy.wait()
        key_sum[...] += held[0][...]
        value_sum[...] += held[1][...]
        finish_attention(
            meta, key_sum, value_sum, query_sum, held[2], part_a, part_b, *held[3:], *outs
        )


def finish_attention(
    meta,
    key_sum,
    value_sum,
    query_sum,
    query_last,
    part_a,
    part_b,
    weights,
    gains,
    head_gains,
    cosine,
    sine,
    mine,
    before,
    normed,
    key_pre,
    query_pre,
    feed_gain,
    own_ref,
    before_ref,
    keep_ref,
    give_ref,
):
    query_gain, key_gain = head_gains[4:5] * SCALE, head_gains[5:6] * SCALE
    cosine_own, sine_own = cosine[TOKENS:], -sine[TOKENS:]
    query_total = jnp.zeros((8, HEAD), F32)
    pre_grads = []
    for h in range(HEADS):
        pre = query_pre[:, h * HEAD : (h + 1) * HEAD].astype(F32)
        inverse = inverse_rms(pre)
        unit = pre * inverse
        rows = slice(h * BLOCK, (h + 1) * BLOCK)
        grad = jnp.concatenate([part[j, rows] for part in (query_sum, query_last) for j in range(2)], 0)
        turned = rotate(grad, cosine_own, sine_own)
        query_total += add_rows(turned * unit)
        pre_grads.append(norm_backward(turned * query_gain, unit, inverse).astype(BF16))
    query_pre_grad = jnp.concatenate(pre_grads, 1)
    pre = key_pre[...].astype(F32)
    inverse = inverse_rms(pre)
    unit = pre * inverse
    turned = rotate(key_sum[...], cosine[...], -sine[...])
    key_total = add_rows(turned * unit)
    key_pre_grad = norm_backward(turned * key_gain, unit, inverse).astype(BF16)
    both = jnp.concatenate([key_pre_grad, value_sum[...].astype(BF16)], 1)
    normed_grad = dot_nt(both, weights[:, HEADS * HEAD :])
    own = normed_grad[TOKENS:] + dot_nt(query_pre_grad, weights[:, : HEADS * HEAD])
    own_ref[...] = own
    before_ref[...] = normed_grad[:TOKENS].astype(BF16)
    normed_grad = jnp.concatenate([normed_grad[:TOKENS], own], 0)
    tokens = jnp.concatenate(
        [part[j, :BLOCK] for part in (before, mine) for j in range(4)], 0
    ).astype(F32)
    attn_total = add_rows(tokens * inverse_rms(tokens) * normed_grad)
    pick_a, pick_b, gain_shard = line_picks(meta, SCATTER)
    query_weight_grad = dot_tn(normed[TOKENS:], query_pre_grad).astype(BF16)
    part_a[...] = dot_tn(pick_a, query_weight_grad[:, :ATT_COLS]).astype(BF16)
    both_grad = dot_tn(normed[...], both).astype(BF16)
    part_b[:, 256:] = dot_tn(pick_b, both_grad).astype(BF16)
    pick, pick_head = gain_picks(gain_shard)
    wide = jnp.zeros((128, WIDTH), F32)
    totals = (attn_total, feed_gain[0:8], feed_gain[8:16], feed_gain[16:24])
    for g in range(4):
        line = jnp.sum(totals[g], 0, keepdims=True)
        wide += jnp.where(gain_lanes(128, WIDTH, 5, 5 * g), line, 0.0)
    head = jnp.zeros((128, HEAD), F32)
    for g, total in enumerate((query_total, key_total)):
        line = jnp.sum(total, 0, keepdims=True) * SCALE
        head += jnp.where(gain_lanes(128, HEAD, 2, 20 + 2 * g), line, 0.0)
    contract = (((0,), (1,)), ((), ()))
    gain_block = lax.dot_general(
        pick, wide.astype(BF16), contract, preferred_element_type=F32
    ) + lax.dot_general(pick_head, head.astype(BF16), contract, preferred_element_type=F32)
    left = dot_tn(pick_b, query_weight_grad[:, ATT_COLS:])
    part_b[:, :128] = (left[:, :128] + gain_block).astype(BF16)
    part_b[:, 128:256] = left[:, 128:].astype(BF16)
    first_core = meta[3] == 0
    keep_ref[...] = jnp.where(first_core, part_a[...], part_b[...])
    give_ref[...] = jnp.where(first_core, part_b[...], part_a[...])


def attention_back(first, count, meta, attended_grad, probs, kept, earlier, inputs, after):
    starting = earlier is None
    sums = [((KEYS, HEAD), F32), ((KEYS, HEAD), F32), ((count, HEADS * BLOCK, HEAD), F32)]
    in_specs = [
        smem(),
        pl.BlockSpec((BLOCK, HEADS * HEAD), lambda r: (r + first, 0)),
        from_row((HEADS * BLOCK, SPAN), first),
        from_row((HEADS * BLOCK, HEAD), first),
        whole((KEYS, HEAD)),
        whole((KEYS, HEAD)),
    ]
    args = [meta, attended_grad, probs, kept[5], kept[1], kept[2]]
    outs = sums
    if not starting:
        args += [*earlier, *inputs]
        in_specs += [anywhere()] * 14
        outs = [((TOKENS, WIDTH), F32), ((TOKENS, WIDTH), BF16)] + [((1024, ATT_COLS), BF16)] * 2
    return call(
        functools.partial(attention_back_kernel, starting, first),
        "attention_back",
        outs,
        in_specs,
        args,
        out_specs=[whole(s) for s, _ in outs],
        scratch=[]
        if starting
        else [pltpu.VMEM(s, d) for s, d in sums]
        + [pltpu.VMEM((1024, ATT_COLS), BF16)] * 2
        + [pltpu.SemaphoreType.DMA((14,))]
        + [pltpu.VMEM(value.shape, value.dtype) for value in (*earlier, *inputs)],
        after=after,
        grid=(count,),
        megabytes=60,
        flops=count * 5 * 10**9,
        moved_bytes=count * 12 * 10**6,
    )


def pack_kernel(meta, *refs):
    sources, keep_ref, give_ref, part = refs[:7], refs[7], refs[8], refs[9]
    held, arrivals = refs[10:17], refs[17]
    copies = [
        pltpu.make_async_copy(source, target, arrivals.at[j])
        for j, (source, target) in enumerate(zip(sources, held))
    ]
    for copy in copies:
        copy.start()
    for copy in copies:
        copy.wait()
    query, key, value, output, gate, up, gains = held
    for half in range(2):
        part[half] = jnp.zeros((8, PACK), F32)
    out_start = ATT_COLS
    feed_start = ATT_COLS + OUT_COLS
    left = HEADS * HEAD - ATT_COLS
    part[0, :5, :ATT_COLS] = query[:, :ATT_COLS].astype(F32)
    part[0, :, out_start:feed_start] = output[:, :OUT_COLS].astype(F32)
    part[0, :5, feed_start:] = gate[...].astype(F32)
    part[1, :5, :left] = query[:, ATT_COLS:].astype(F32)
    part[1, :5, left : left + HEAD] = key[...].astype(F32)
    part[1, :5, left + HEAD : ATT_COLS] = value[...].astype(F32)
    part[1, 5:6, :128] = gains[...].astype(F32)
    part[1, :, out_start : out_start + WIDTH - OUT_COLS] = output[:, OUT_COLS:].astype(F32)
    part[1, :5, feed_start:] = up[...].astype(F32)
    core = meta[3]
    keep_ref[...] = part[core].astype(BF16)
    give_ref[...] = part[1 - core].astype(BF16)


def pack_weights(meta, query, key, value, output, gate, up, gains):
    return call(
        pack_kernel,
        "pack_weights",
        [((8, PACK), BF16)] * 2,
        [smem()] + [anywhere()] * 7,
        [meta, query, key, value, output, gate, up, gains],
        scratch=[pltpu.VMEM((2, 8, PACK), F32)]
        + [
            pltpu.VMEM(held.shape, held.dtype)
            for held in (query, key, value, output, gate, up, gains)
        ]
        + [pltpu.SemaphoreType.DMA((7,))],
        megabytes=60,
        flops=10**6,
        moved_bytes=3 * 10**5,
    )


def pair_kernel(meta, kept, crossed, down, out_ref):
    first_core = meta[3] == 0
    mine, theirs = kept[...].astype(F32), crossed[...].astype(F32)
    upper = jnp.where(first_core, mine, theirs)
    lower = jnp.where(first_core, theirs, mine)
    out_ref[:, :PACK] = jnp.concatenate([upper, lower], 0).astype(BF16)
    out_ref[:, PACK:] = down[...]


def pair_up(meta, kept, crossed, down):
    return call(
        pair_kernel,
        "pair_up",
        [((16, PACK + WIDTH), BF16)],
        [smem()] + [vmem()] * 3,
        [meta, kept, crossed, down],
        megabytes=16,
        flops=10**6,
        moved_bytes=4 * 10**5,
    )[0]


def split_kernel(slot, meta, value, *refs):
    for j in range(4):
        refs[j][...] = value[meta[slot] ^ j]


def split_up(meta, slot, value, after):
    return call(
        functools.partial(split_kernel, slot),
        "split_up",
        [(value.shape[1:], value.dtype)] * 4,
        [smem(), vmem()],
        [meta, value],
        after=after,
        megabytes=16,
        flops=10**6,
        moved_bytes=10**6,
    )


def join_tokens_kernel(slot, meta, *refs):
    for j in range(4):
        refs[4][meta[slot] ^ j] = refs[j][:TAGGED]
        refs[5][meta[slot] ^ j] = refs[j][TAGGED:]


def join_tokens(meta, slot, pieces, after):
    return call(
        functools.partial(join_tokens_kernel, slot),
        "join_tokens",
        [((4, TAGGED, WIDTH), BF16), ((4, BLOCK, WIDTH), BF16)],
        [smem()] + [vmem()] * 4,
        [meta, *pieces],
        after=after,
        megabytes=16,
        flops=10**6,
        moved_bytes=10**6,
    )


def hold_kernel(*refs):
    pass


def hold(values, after):
    return call(
        hold_kernel,
        "hold",
        [(value.shape, value.dtype) for value in values],
        [anywhere()] * len(values),
        values,
        out_specs=[anywhere()] * len(values),
        after=after,
        aliases={j: j for j in range(len(values))},
        megabytes=60,
        flops=10**4,
        moved_bytes=10**4,
    )


def add_pieces_kernel(kept, crossed, *refs):
    rows = refs[0].shape[0]
    for j in range(4):
        here = slice(j * rows, (j + 1) * rows)
        refs[j][...] = (kept[here].astype(F32) + crossed[here].astype(F32)).astype(BF16)


def add_pieces(kept, crossed, after, megabytes=60):
    shape = (kept.shape[0] // 4,) + kept.shape[1:]
    return call(
        add_pieces_kernel,
        "add_pieces",
        [(shape, BF16)] * 4,
        [vmem()] * 2,
        [kept, crossed],
        after=after,
        megabytes=megabytes,
        flops=10**7,
        moved_bytes=8 * 10**6,
    )


def line_kernel(*refs):
    total = add_up(refs[0][...], [ref[...] for ref in refs[1:4]]).astype(BF16)
    for j in range(4):
        refs[4 + j][...] = total[j]


def line_up(own, others, after):
    return call(
        line_kernel,
        "line_up",
        [(own.shape[1:], BF16)] * 4,
        [vmem()] * 4,
        [own, *others],
        after=after,
        megabytes=16,
        flops=10**6,
        moved_bytes=2 * 10**6,
    )


def total_kernel(meta, *refs):
    total = add_up(refs[0][...], [ref[...] for ref in refs[1:4]])
    keep_ref, give_ref, down_ref = refs[4:]
    first_core = meta[3] == 0
    upper, lower = total[:8, :PACK], total[8:, :PACK]
    keep_ref[...] = jnp.where(first_core, upper, lower)
    give_ref[...] = jnp.where(first_core, lower, upper)
    down_ref[...] = total[:, PACK:]


def total_up(meta, own, others):
    return call(
        total_kernel,
        "total_up",
        [((8, PACK), F32)] * 2 + [((16, WIDTH), F32)],
        [smem()] + [vmem()] * 4,
        [meta, own, *others],
        megabytes=16,
        flops=10**6,
        moved_bytes=10**6,
    )


def output_kernel(slot, meta, gains, middle_grad, own, returned, mine, block_out, *refs):
    tokens = jnp.concatenate([mine[j, :BLOCK] for j in range(4)], 0).astype(F32)
    inverse = inverse_rms(tokens)
    normed_grad = own[...] + returned[...].astype(F32)
    grad = middle_grad[...] + norm_backward(normed_grad * gains[0:1], tokens * inverse, inverse)
    refs[4][...] = grad.astype(BF16).reshape(4, BLOCK, WIDTH)
    for j in range(4):
        refs[j][0] = block_out[meta[slot] ^ j]
        refs[j][1] = refs[4][meta[slot] ^ j]


def output_pieces(meta, slot, gains, middle_grad, own, returned, mine, block_out):
    return call(
        functools.partial(output_kernel, slot),
        "output_pieces",
        [((2, BLOCK, WIDTH), BF16)] * 4,
        [smem()] + [vmem()] * 6,
        [meta, gains, middle_grad, own, returned, mine, block_out],
        scratch=[pltpu.VMEM((4, BLOCK, WIDTH), BF16)],
        megabytes=16,
        flops=10**7,
        moved_bytes=5 * 10**6,
    )


def join_outputs_kernel(slot, meta, *refs):
    for j in range(4):
        for k in range(2):
            refs[4 + k][meta[slot] ^ j] = refs[j][k]


def join_outputs(meta, slot, pieces):
    return call(
        functools.partial(join_outputs_kernel, slot),
        "join_outputs",
        [((4, BLOCK, WIDTH), BF16)] * 2,
        [smem()] + [vmem()] * 4,
        [meta, *pieces],
        megabytes=16,
        flops=10**6,
        moved_bytes=2 * 10**6,
    )


def stack_kernel(*refs):
    for j in range(4):
        refs[4][j] = refs[j][...]


def stack_kernel(*refs):
    for j in range(4):
        refs[4][j] = refs[j][...]


def stack_both_kernel(*refs):
    for j in range(8):
        refs[8 + j // 4][j % 4] = refs[j][...]


def stack_both(first, second, after):
    return call(
        stack_both_kernel,
        "stack_both",
        [((4,) + first[0].shape, BF16), ((4,) + second[0].shape, BF16)],
        [vmem()] * 8,
        [*first, *second],
        after=after,
        megabytes=16,
        flops=10**6,
        moved_bytes=10**7,
    )


def stack_up(pieces, shape, after):
    return call(
        stack_kernel,
        "stack_up",
        [((4,) + shape, BF16)],
        [vmem()] * 4,
        pieces,
        after=after,
        megabytes=16,
        flops=10**6,
        moved_bytes=4 * 10**6,
    )[0]


def first_slab_kernel(*refs):
    for j in range(4):
        here = slice(j * 64, (j + 1) * 64)
        refs[4][here, :ATT_COLS] = refs[j][:, :, :ATT_COLS].reshape(64, ATT_COLS)
        refs[4][here, ATT_COLS : ATT_COLS + OUT_COLS] = refs[j][
            :, :, ATT_COLS : ATT_COLS + OUT_COLS
        ].reshape(64, OUT_COLS)
        refs[4][here, ATT_COLS + OUT_COLS :] = refs[j][:, :, PACK:].reshape(64, WIDTH)


def first_slab(pieces, after):
    return call(
        first_slab_kernel,
        "first_slab",
        [((256, FIRST_PACK), BF16)],
        [vmem()] * 4,
        pieces,
        after=after,
        megabytes=16,
        flops=10**6,
        moved_bytes=3 * 10**6,
    )[0]


def loose_rows():
    line = lax.broadcasted_iota(jnp.int32, (256, 160), 0)
    row = line & 7
    dense = lax.broadcasted_iota(jnp.int32, (256, 160), 1)
    same = ((line >> 3) * 5 + row == dense) & (row < 5)
    return jnp.where(same, 1.0, 0.0).astype(BF16)


def feed_slab_kernel(*refs):
    feed_ref, loose = refs[4:]
    for j in range(4):
        loose[j * 64 : (j + 1) * 64] = refs[j][:, :, ATT_COLS + OUT_COLS : PACK].reshape(
            64, HIDDEN
        )
    feed_ref[...] = dot_tn(loose_rows(), loose[...]).astype(BF16)


def feed_slab_of(pieces, after):
    return call(
        feed_slab_kernel,
        "feed_slab",
        [((160, HIDDEN), BF16)],
        [vmem()] * 4,
        pieces,
        scratch=[pltpu.VMEM((256, HIDDEN), BF16)],
        after=after,
        megabytes=16,
        flops=2 * 10**8,
        moved_bytes=4 * 10**6,
    )[0]


def merge_kernel(*refs):
    att, feed, down, outs = refs[:4], refs[4:8], refs[8:12], refs[12:]

    def total(pieces):
        return add_up(pieces[0][...], [piece[...] for piece in pieces[1:]]).astype(BF16)

    att_total = total(att).reshape(16, 16, ATT_COLS)
    feed_total = dot(loose_rows(), total(feed)).astype(BF16).reshape(16, 16, HIDDEN)
    down_total = total(down)
    for j in range(4):
        here = slice(j * 4, (j + 1) * 4)
        outs[j][:, :, :ATT_COLS] = att_total[here]
        outs[j][:, :, ATT_COLS : ATT_COLS + HIDDEN] = feed_total[here]
        outs[j][:, :, ATT_COLS + HIDDEN :] = down_total[here]


def merge_grads(att, feed, down):
    return call(
        merge_kernel,
        "merge_grads",
        [((4, 16, PACK + WIDTH), BF16)] * 4,
        [vmem()] * 12,
        [*att, *feed, *down],
        megabytes=60,
        flops=2 * 10**8,
        moved_bytes=8 * 10**6,
    )


def unpack_kernel(meta, mine, theirs, query, key, value, output, gate, up, gains):
    first_core = meta[3] == 0
    part_a = jnp.where(first_core, mine[...], theirs[...])
    part_b = jnp.where(first_core, theirs[...], mine[...])
    left = HEADS * HEAD - ATT_COLS
    feed_end = ATT_COLS + HIDDEN
    query[:, :ATT_COLS] = part_a[:5, :ATT_COLS]
    query[:, ATT_COLS:] = part_b[:5, :left]
    key[...] = part_b[:5, left : left + HEAD]
    value[...] = part_b[:5, left + HEAD : ATT_COLS]
    gate[...] = part_a[:5, ATT_COLS:feed_end]
    up[...] = part_b[:5, ATT_COLS:feed_end]
    output[:, :OUT_COLS] = part_a[:, feed_end:]
    output[:, OUT_COLS:] = part_b[:, feed_end : feed_end + WIDTH - OUT_COLS]
    gains[...] = part_b[5:6, :128]


def unpack_grads(meta, mine, theirs):
    return call(
        unpack_kernel,
        "unpack_grads",
        [
            ((5, HEADS * HEAD), F32),
            ((5, HEAD), F32),
            ((5, HEAD), F32),
            ((8, WIDTH), F32),
            ((5, HIDDEN), F32),
            ((5, HIDDEN), F32),
            ((1, 128), F32),
        ],
        [smem()] + [vmem()] * 2,
        [meta, mine, theirs],
        megabytes=16,
        flops=10**6,
        moved_bytes=4 * 10**5,
    )


def on_device(
    hidden_in,
    segment_ids,
    cotangent,
    attn_gain,
    query_weight,
    key_weight,
    value_weight,
    query_gain,
    key_gain,
    output_weight,
    post_attn_gain,
    ffn_gain,
    gate_weight,
    up_weight,
    down_weight,
    post_ffn_gain,
):
    me = my_place()
    core = me["c"]
    first_core = core == 0
    row = 2 * ((me["x"] ^ (me["x"] >> 1)) & 1) + core
    member = 2 * (me["x"] & 1) + core
    place = (me["y"] >> 1) * 1024 + (me["x"] >> 1) * TOKENS
    meta = jnp.stack([me["z"], me["y"], me["x"], core, place, row, member]).astype(jnp.int32)
    row_slot, member_slot = 5, 6

    def pick(value_first, value_second):
        return jnp.where(first_core, value_first, value_second)

    positions = place + jnp.arange(-TOKENS, TOKENS, dtype=jnp.int32)
    frequency = jnp.exp(
        jnp.arange(HEAD // 2, dtype=F32) * (-2.0 * math.log(ROPE_BASE) / HEAD)
    )
    angles = positions.astype(F32)[:, None] * frequency[None]
    tables = (jnp.cos(angles), jnp.sin(angles))

    gains = jnp.zeros((128,), F32)
    start = 0
    for gain in (attn_gain, post_attn_gain, ffn_gain, post_ffn_gain, query_gain, key_gain):
        size = gain.shape[0]
        gains = gains + jnp.pad(gain.astype(F32), (start, 128 - start - size))
        start += size
    kept, given = pack_weights(
        meta,
        query_weight,
        key_weight,
        value_weight,
        output_weight,
        gate_weight,
        up_weight,
        gains.reshape(1, 128),
    )
    pair = pair_up(meta, kept, swap(given), down_weight)
    near_chips = arrived(pair, 0)

    segments = segment_ids.reshape(4, 1, BLOCK).astype(BF16)
    segments = jnp.pad(segments, ((0, 0), (0, TAGGED - BLOCK - 1), (0, WIDTH - BLOCK)))
    dealing = jnp.concatenate(
        [
            hidden_in.reshape(4, BLOCK, WIDTH),
            segments,
            cotangent.reshape(4, BLOCK, WIDTH),
        ],
        1,
    )
    own, one, two, three = split_up(meta, row_slot, dealing, [])
    pieces = [own, swap(one), exchange(two, False), exchange(three, True)]
    mine, cotangent_mine = join_tokens(meta, member_slot, pieces, near_chips)
    near, before = next_chunk(mine, me["x"] < 2)

    line = stack_up([pair, *near_chips], pair.shape, [mine])
    plane = [line, *arrived(line, 1)]
    plane = [line, *arrived(line, 1)]
    slab = first_slab(plane, [*tables, near])
    first_own = [slab, *arrived(slab, 2)]
    first_other = [swap(value) for value in first_own]
    feed_slab = feed_slab_of(plane, first_own[1:])

    grid = jnp.arange(64, dtype=jnp.int32)
    table = []
    for orders in (GATHER, SCATTER):
        chips = [chip_of([me["z"], me["y"], me["x"]], order, grid) for order in orders]
        held, crossed = pick(chips[0], chips[1]), pick(chips[1], chips[0])
        table += [*chips, held * 2 + core, crossed * 2 + 1 - core]
    table = jnp.stack(table).astype(jnp.int32)

    forward = attention_blocks(0, 4, meta, mine, before, tables, first_own + first_other, None, [])
    made, kept_values, (attended, probs) = forward[:3], forward[3:9], forward[9:]
    feed_own = [feed_slab, *hold(arrived(feed_slab, 2), [attended])]
    (
        block_out,
        middle_grad,
        attended_grad,
        feed_gain,
        keep_feed,
        give_feed,
        keep_down,
        give_down,
    ) = feed_forward(
        meta,
        table,
        made[1],
        mine,
        cotangent_mine,
        attended,
        feed_own,
        [swap(value) for value in feed_own],
        first_own,
        first_other,
    )
    back = attention_back(2, 2, meta, attended_grad, probs, kept_values, None, None, [])
    feed_sum = add_pieces(keep_feed, swap(give_feed), [back[0]])
    down_sum = add_pieces(keep_down, swap(give_down), [back[0]])
    normed_grad, to_before, keep_att, give_att = attention_back(
        0,
        2,
        meta,
        attended_grad,
        probs,
        kept_values,
        back,
        (
            *made,
            *tables,
            mine,
            before,
            kept_values[0],
            kept_values[3],
            kept_values[4],
            feed_gain,
        ),
        [*feed_sum, *down_sum],
    )
    feed_in = received(feed_sum, 2)
    down_in = received(down_sum, 2)

    give_att = hold([give_att], [*feed_in, *down_in[:2]])[0]
    att_sum = add_pieces(keep_att, swap(give_att), [], 24)
    plane = merge_grads(
        [att_sum[0], *received(att_sum, 2)], [feed_sum[0], *feed_in], [down_sum[0], *down_in]
    )
    returned = chunk_before(to_before)
    own, one, two, three = output_pieces(
        meta, member_slot, made[1], middle_grad, normed_grad, returned, mine, block_out
    )
    line = line_up(plane[0], received(plane, 1), [own])
    kept_grads, given_grads, grad_down = total_up(meta, line[0], received(line, 0))
    grad_query, grad_key, grad_value, grad_output, grad_gate, grad_up, gain_grads = unpack_grads(
        meta, kept_grads, swap(given_grads)
    )
    gain_grads = gain_grads.reshape(128)

    block_out, input_grad = join_outputs(
        meta, row_slot, [own, swap(one), exchange(two, False), exchange(three, True)]
    )
    return (
        block_out.reshape(hidden_in.shape),
        input_grad.reshape(hidden_in.shape),
        gain_grads[0:5],
        grad_query,
        grad_key,
        grad_value,
        gain_grads[20:22],
        gain_grads[22:24],
        grad_output,
        gain_grads[5:10],
        gain_grads[10:15],
        grad_gate,
        grad_up,
        grad_down,
        gain_grads[15:20],
    )


def solution(mesh):
    rows = P(None, "dp", "seq", None)
    shard = P(("dp", "seq"), None)
    vector = P(("dp", "seq"))
    return jax.shard_map(
        on_device,
        mesh=mesh,
        in_specs=(rows, P(None, "dp", "seq"), rows)
        + (vector, shard, shard, shard, vector, vector, shard, vector)
        + (vector, shard, shard, shard, vector),
        out_specs=(rows, rows)
        + (vector, shard, shard, shard, vector, vector, shard, vector)
        + (vector, shard, shard, shard, vector),
        check_vma=False,
    )
```

```python
import functools
import math

import jax
import jax.numpy as jnp
from jax import lax
from jax.experimental import pallas as pl
from jax.experimental.pallas import tpu as pltpu
from jax.sharding import PartitionSpec as P

WINDOW = 512
HALO = 4
BLOCK = 128
TOKENS = 512
KEYS = 1024
WIDTH = 640
HEADS = 4
HEAD = 256
HIDDEN = 2048
SPAN = (HALO + 1) * BLOCK
CHUNK = 512
TAGGED = BLOCK + 16
EPSILON = 1e-06
ROPE_BASE = 10000.0
MASKED = -1e30
SCALE = HEAD ** (-0.5)
F32 = jnp.float32
BF16 = jnp.bfloat16

AXES = ("dp", "seq")
SIZE = {"x": 4, "y": 4, "z": 4, "c": 2}
GATHER = (("x", "y", "z"), ("y", "z", "x"))
SCATTER = (("y", "x", "z"), ("y", "z", "x"))
ATT_COLS = 768
OUT_COLS = 384
DOWN_PACK = OUT_COLS + WIDTH
PACK = ATT_COLS + OUT_COLS + HIDDEN
FIRST_PACK = ATT_COLS + DOWN_PACK


def shard_of(z, y, x, c):
    return z * 32 + (y % 2) * 16 + (y // 2) * 8 + x * 2 + c


def moved(axis_of_core, by):
    pairs = []
    for z in range(4):
        for y in range(4):
            for x in range(4):
                for c in range(2):
                    place = {"z": z, "y": y, "x": x, "c": c}
                    axis = axis_of_core[c]
                    place[axis] = (place[axis] + by) % SIZE[axis]
                    pairs.append((shard_of(z, y, x, c), shard_of(**place)))
    return pairs


def send(value, orders, phase, by):
    axes = (orders[0][phase], orders[1][phase])
    return lax.ppermute(value, AXES, moved(axes, by))


def swap(value):
    return lax.ppermute(value, AXES, moved(("c", "c"), 1))


def exchange(value, flip):
    pairs = []
    for i in range(128):
        pairs.append((i, i ^ (3 if flip else 2)))
    return lax.ppermute(value, AXES, pairs)


def next_chunk(value, first_half):
    along, across = [], []
    for dp in range(8):
        for c in range(2):
            for x in range(4):
                for yh in range(2):
                    if x >= 2 and yh == 1:
                        continue
                    here = dp * 16 + yh * 8 + x * 2 + c
                    along.append((here, here + (3 - 2 * x) * 2))
            for x in range(2):
                here = dp * 16 + x * 2 + c
                across.append((here, here + 8))
    near = lax.ppermute(value, AXES, along)
    return near, jnp.where(first_half, lax.ppermute(near, AXES, across), near)


def chunk_before(value):
    pairs = []
    for dp in range(8):
        for yh in range(2):
            for x in range(4):
                for c in range(2):
                    if x >= 2 and yh == 1:
                        continue
                    here = dp * 16 + yh * 8 + x * 2 + c
                    there = dp * 16 + (yh + (x >= 2)) * 8 + (3 - x) * 2 + c
                    pairs.append((there, here))
    return lax.ppermute(value, AXES, pairs)


def my_place():
    dp, seq = lax.axis_index("dp"), lax.axis_index("seq")
    return {"z": dp // 2, "y": (seq // 8) * 2 + dp % 2, "x": (seq // 2) % 4, "c": seq % 2}


def arrived(value, phase):
    one, three, two = [send(value, GATHER, phase, -by) for by in (1, 3, 2)]
    return [one, two, three]


def received(pieces, phase):
    return [send(pieces[by], SCATTER, phase, by) for by in (1, 3, 2)]


def add_up(own, others):
    total = own.astype(F32)
    for other in others:
        total = total + other.astype(F32)
    return total


def chip_at(meta, order, j3, j2, j1):
    place = {
        order[2]: (meta["zyx".index(order[2])] + j3) & 3,
        order[1]: (meta["zyx".index(order[1])] + j2) & 3,
        order[0]: (meta["zyx".index(order[0])] + j1) & 3,
    }
    z, y, x = place["z"], place["y"], place["x"]
    return z * 16 + (y & 1) * 8 + (y >> 1) * 4 + x


def chip_of(meta, order, i):
    return chip_at(meta, order, i >> 4, (i >> 2) & 3, i & 3)


def slab_rows(meta, order, rows_held):
    line = lax.broadcasted_iota(jnp.int32, (1, 128 * rows_held), 1)
    if rows_held == 8:
        both, row = line >> 3, line & 7
    else:
        both = lax.shift_right_logical(line * 52429, 18)
        row = line - both * 5
    return chip_of(meta, order, both >> 1) * 2 + (both & 1), row


def dot(a, b):
    return jnp.dot(a, b, preferred_element_type=F32)


def dot_nt(a, b):
    return lax.dot_general(a, b, (((1,), (1,)), ((), ())), preferred_element_type=F32)


def dot_tn(a, b):
    return lax.dot_general(a, b, (((0,), (0,)), ((), ())), preferred_element_type=F32)


def add_rows(values):
    total = values[:8]
    for first in range(8, values.shape[0], 8):
        total = total + values[first : first + 8]
    return total


def one_hot(index_row, count):
    places = lax.broadcasted_iota(jnp.int32, (count, index_row.shape[1]), 0)
    return jnp.where(places == index_row, 1.0, 0.0).astype(BF16)


def inverse_rms(values):
    return lax.rsqrt(jnp.mean(values * values, -1, keepdims=True) + EPSILON)


def norm_backward(grad_hat, unit_value, inverse):
    return inverse * (grad_hat - unit_value * jnp.mean(grad_hat * unit_value, -1, keepdims=True))


def rotate(values, cosine, sine):
    first, second = values[:, : HEAD // 2], values[:, HEAD // 2 :]
    return jnp.concatenate(
        [first * cosine - second * sine, second * cosine + first * sine], axis=-1
    )


def vmem():
    return pl.BlockSpec(memory_space=pltpu.VMEM)


def smem():
    return pl.BlockSpec(memory_space=pltpu.SMEM)


def anywhere():
    return pl.BlockSpec(memory_space=pl.ANY)


def whole(shape):
    return pl.BlockSpec(shape, lambda r: (0,) * len(shape))


def by_row(shape):
    return pl.BlockSpec((1,) + shape, lambda r: (r,) + (0,) * len(shape))


def from_row(shape, first):
    return pl.BlockSpec((1,) + shape, lambda r: (r + first,) + (0,) * len(shape))


def call(
    kernel,
    name,
    outs,
    in_specs,
    args,
    out_specs=None,
    scratch=(),
    after=(),
    aliases=None,
    grid=(),
    megabytes=58,
    flops=0,
    moved_bytes=0,
):
    after = list(after)
    count = len(in_specs)

    def body(*refs):
        kernel(*refs[:count], *refs[count + len(after) :])

    return pl.pallas_call(
        body,
        grid=grid,
        out_shape=[jax.ShapeDtypeStruct(s, d) for s, d in outs],
        in_specs=list(in_specs) + [anywhere()] * len(after),
        out_specs=[vmem()] * len(outs) if out_specs is None else out_specs,
        scratch_shapes=list(scratch),
        input_output_aliases=aliases or {},
        compiler_params=pltpu.CompilerParams(vmem_limit_bytes=megabytes * 2**20),
        cost_estimate=pl.CostEstimate(
            flops=flops, bytes_accessed=moved_bytes, transcendentals=0
        ),
        name=name,
    )(*args, *after)


def line_picks(meta, orders):
    shard_a, row_a = slab_rows(meta, orders[0], 8)
    shard_b, row_b = slab_rows(meta, orders[1], 8)
    pick_a = one_hot(jnp.where(row_a < 5, shard_a * 5 + row_a, -1), WIDTH)
    pick_b = one_hot(jnp.where(row_b < 5, shard_b * 5 + row_b, -1), WIDTH)
    return pick_a, pick_b, jnp.where(row_b == 5, shard_b, -1)


def gain_picks(shard_line):
    wide = lax.broadcasted_iota(jnp.int32, (WIDTH, shard_line.shape[1]), 0)
    first = shard_line * 5
    pick = jnp.where((wide >= first) & (wide < first + 5) & (first >= 0), 1.0, 0.0).astype(BF16)
    head = lax.broadcasted_iota(jnp.int32, (HEAD, shard_line.shape[1]), 0)
    pick_head = jnp.where((head >> 1) == shard_line, 1.0, 0.0).astype(BF16)
    return pick, pick_head


def gain_lanes(count, width, per_shard, first):
    lane = lax.broadcasted_iota(jnp.int32, (count, width), 0)
    entry = lax.broadcasted_iota(jnp.int32, (count, width), 1)
    if per_shard == 5:
        place = entry - lax.shift_right_logical(entry * 52429, 18) * 5
    else:
        place = entry & 1
    return lane == place + first


def both_parts(meta, own, other, part_a, part_b, rows):
    @pl.when(meta[3] == 0)
    def _():
        for j in range(4):
            part_a[j * rows : (j + 1) * rows] = own[j][...]
            part_b[j * rows : (j + 1) * rows] = other[j][...]

    @pl.when(meta[3] != 0)
    def _():
        for j in range(4):
            part_a[j * rows : (j + 1) * rows] = other[j][...]
            part_b[j * rows : (j + 1) * rows] = own[j][...]


def weights_kernel(meta, *refs):
    own, other = refs[:4], refs[4:8]
    weights_ref, gains_ref, head_gains_ref, part_a, part_b = refs[8:]
    both_parts(meta, own, other, part_a, part_b, 256)
    pick_a, pick_b, gain_shard = line_picks(meta, GATHER)
    weights_ref[:, :ATT_COLS] = dot(pick_a, part_a[...]).astype(BF16)
    weights_ref[:, ATT_COLS:] = dot(pick_b, part_b[...]).astype(BF16)
    pick, pick_head = gain_picks(gain_shard)
    block = part_b[:, :128]
    contract = (((0,), (1,)), ((), ()))
    wide = lax.dot_general(block, pick, contract, preferred_element_type=F32)[:24]
    head = lax.dot_general(block, pick_head, contract, preferred_element_type=F32)[:24]
    gains_ref[...] = jnp.zeros_like(gains_ref)
    head_gains_ref[...] = jnp.zeros_like(head_gains_ref)
    for g in range(4):
        chosen = jnp.where(gain_lanes(24, WIDTH, 5, 5 * g), wide, 0.0)
        gains_ref[g : g + 1] = jnp.sum(chosen, 0, keepdims=True)
    for g in range(2):
        chosen = jnp.where(gain_lanes(24, HEAD, 2, 20 + 2 * g), head, 0.0)
        head_gains_ref[4 + g : 5 + g] = jnp.sum(chosen, 0, keepdims=True)


def prepare_kernel(weights, gains, head_gains, cosine, sine, mine, before, *refs):
    normed_ref, keys_ref, values_ref, key_pre_ref, query_pre_ref, queries_ref = refs
    tokens = jnp.concatenate(
        [part[j, :BLOCK] for part in (before, mine) for j in range(4)], 0
    ).astype(F32)
    normed = (tokens * inverse_rms(tokens) * gains[0:1]).astype(BF16)
    normed_ref[...] = normed
    key_value = dot(normed, weights[:, HEADS * HEAD :])
    key_pre = key_value[:, :HEAD]
    key_pre_ref[...] = key_pre.astype(BF16)
    values_ref[...] = key_value[:, HEAD:].astype(BF16)
    query_pre = dot(normed[TOKENS:], weights[:, : HEADS * HEAD])
    query_pre_ref[...] = query_pre.astype(BF16)
    query_gain, key_gain = head_gains[4:5], head_gains[5:6]
    keys = rotate(key_pre * inverse_rms(key_pre) * key_gain, cosine[...], sine[...])
    keys_ref[...] = keys.astype(BF16)
    for h in range(HEADS):
        pre = query_pre[:, h * HEAD : (h + 1) * HEAD]
        turned = rotate(
            pre * inverse_rms(pre) * query_gain, cosine[TOKENS:], sine[TOKENS:]
        ).astype(BF16)
        for j in range(4):
            queries_ref[j, h * BLOCK : (h + 1) * BLOCK] = turned[j * BLOCK : (j + 1) * BLOCK]


def attention_kernel(first, meta, mine, before, *refs):
    step = pl.program_id(0)
    if first == 0:
        cosine, sine, slabs, refs = refs[0], refs[1], refs[2:10], refs[10:]
        results, refs = refs[:9], refs[9:]
        held, leaving = refs[5:14], refs[14]
        made, kept = held[:3], held[3:]
        copies = [
            pltpu.make_async_copy(source, target, leaving.at[j])
            for j, (source, target) in enumerate(zip(held, results))
        ]

        @pl.when(step == 0)
        def _():
            weights_kernel(meta, *slabs, *made, refs[3], refs[4])
            prepare_kernel(*made, cosine, sine, mine, before, *kept)
            for copy in copies:
                copy.start()

        @pl.when(step == pl.num_programs(0) - 1)
        def _():
            for copy in copies:
                copy.wait()

        _, keys_ref, values_ref, _, _, queries_ref = kept
    else:
        keys_ref, values_ref, queries_ref = refs[:3]
        refs = refs[3:]
    attended_ref, probs_ref, line_s = refs[:3]
    place = step + first
    lines = [
        part[j, BLOCK:].astype(F32)[0:1, :BLOCK] for part in (before, mine) for j in range(4)
    ]
    line_s[...] = jnp.broadcast_to(jnp.concatenate(lines, 1), line_s.shape)
    start = pl.multiple_of(place * BLOCK, BLOCK)
    window = pl.ds(start, SPAN)
    square = (BLOCK, BLOCK)
    diagonal = lax.broadcasted_iota(jnp.int32, square, 0) == lax.broadcasted_iota(
        jnp.int32, square, 1
    )
    own_line = line_s[0:1, pl.ds(pl.multiple_of(start + TOKENS, BLOCK), BLOCK)]
    own_column = jnp.sum(jnp.where(diagonal, own_line, 0.0), 1, keepdims=True)
    query_place = lax.broadcasted_iota(jnp.int32, (BLOCK, SPAN), 0)
    key_place = lax.broadcasted_iota(jnp.int32, (BLOCK, SPAN), 1) - HALO * BLOCK
    visible = (
        (key_place <= query_place)
        & (query_place - key_place < WINDOW)
        & (key_place + meta[4] + start >= 0)
        & (own_column == line_s[0:1, window])
    )
    bias = jnp.where(visible, 0.0, MASKED)
    queries = queries_ref[place if first == 0 else 0]
    scores = dot_nt(queries, keys_ref[window]) * SCALE + jnp.concatenate([bias] * HEADS, 0)
    terms = jnp.exp(scores - jnp.max(scores, -1, keepdims=True))
    probs = (terms * (1.0 / jnp.sum(terms, -1, keepdims=True))).astype(BF16)
    probs_ref[0] = probs
    mixed = dot(probs, values_ref[window]).astype(BF16)
    for h in range(HEADS):
        attended_ref[0, :, h * HEAD : (h + 1) * HEAD] = mixed[h * BLOCK : (h + 1) * BLOCK]


MADE = [((WIDTH, 1536), BF16), ((8, WIDTH), F32), ((8, HEAD), F32)]
KEPT = [
    ((KEYS, WIDTH), BF16),
    ((KEYS, HEAD), BF16),
    ((KEYS, HEAD), BF16),
    ((KEYS, HEAD), BF16),
    ((TOKENS, HEADS * HEAD), BF16),
    ((4, HEADS * BLOCK, HEAD), BF16),
]


def attention_blocks(first, count, meta, mine, before, tables, slabs, kept, after):
    outs = [((count, BLOCK, HEADS * HEAD), BF16), ((count, HEADS * BLOCK, SPAN), BF16)]
    making = first == 0
    fixed = MADE + KEPT if making else []
    if making:
        more = [*tables, *slabs]
        more_specs = [whole((KEYS, HEAD // 2))] * 2 + [whole((256, ATT_COLS))] * 8
    else:
        more = [kept[1], kept[2], kept[5]]
        more_specs = [whole((KEYS, HEAD))] * 2 + [from_row((HEADS * BLOCK, HEAD), first)]
    return call(
        functools.partial(attention_kernel, first),
        "attention_blocks",
        fixed + outs,
        [smem()] + [whole((4, TAGGED, WIDTH))] * 2 + more_specs,
        [meta, mine, before, *more],
        out_specs=[anywhere()] * len(fixed) + [by_row(s[1:]) for s, _ in outs],
        scratch=[pltpu.VMEM((8, KEYS), F32)]
        + [pltpu.VMEM((1024, ATT_COLS), BF16)] * 2
        + [pltpu.VMEM(s, d) for s, d in fixed]
        + [pltpu.SemaphoreType.DMA((9,))],
        after=after,
        grid=(count,),
        megabytes=60,
        flops=count * 4 * 10**9,
        moved_bytes=count * 10**7,
    )


def gelu_parts(gate):
    square = gate * gate
    bent = jnp.tanh(gate * (0.7978845608 + (0.7978845608 * 0.044715) * square))
    half = 0.5 + 0.5 * bent
    slope = half + gate * (1.0 - bent * bent) * (
        (0.5 * 0.7978845608) + (0.5 * 0.7978845608 * 3 * 0.044715) * square
    )
    return gate * half, slope


def feed_kernel(meta, table, gains, mine, cotangent, *refs):
    attended, refs = refs[0], refs[1:]
    own, other, own_down, other_down = refs[:4], refs[4:8], refs[8:12], refs[12:16]
    refs = refs[16:]
    block_out_ref, middle_grad_ref, attended_grad_ref, gain_ref = refs[:4]
    keep_ref, give_ref, keep_down_ref, give_down_ref = refs[4:8]
    (
        gate_w,
        up_w,
        down_w,
        output_w,
        active_s,
        slope_s,
        inner_s,
        inputs_s,
        grads_s,
        keep_s,
        give_s,
        grad_down,
        keep_down_s,
        give_down_s,
        arrivals,
        leaving,
    ) = refs[8:]
    core = meta[3]
    first_core = core == 0

    def fetch(sources, target, first):
        return [
            pltpu.make_async_copy(
                sources[j], target.at[j * 160 : (j + 1) * 160], arrivals.at[first + j]
            )
            for j in range(4)
        ]

    @pl.when(first_core)
    def _():
        for copy in fetch(own, gate_w, 0) + fetch(other, up_w, 4):
            copy.start()

    @pl.when(jnp.logical_not(first_core))
    def _():
        for copy in fetch(other, gate_w, 0) + fetch(own, up_w, 4):
            copy.start()

    for j in range(4):

        def place(i, carry, j=j):
            here = pl.ds(pl.multiple_of(i * 16, 16), 16)
            mine, theirs = own_down[j][here, ATT_COLS:], other_down[j][here, ATT_COLS:]
            down_w[table[2, j * 16 + i]] = mine[:, OUT_COLS:]
            down_w[table[3, j * 16 + i]] = theirs[:, OUT_COLS:]
            mine, theirs = mine[:, :OUT_COLS], theirs[:, :OUT_COLS]
            output_w[table[0, j * 16 + i], :, :OUT_COLS] = jnp.where(first_core, mine, theirs)
            output_w[table[1, j * 16 + i], :, OUT_COLS:] = jnp.where(first_core, theirs, mine)[
                :, : WIDTH - OUT_COLS
            ]
            return carry

        lax.fori_loop(0, 16, place, 0, unroll=8)

    picks = []
    for order in (*GATHER, SCATTER[0]):
        shard, row = slab_rows(meta, order, 5)
        picks.append(one_hot(shard * 5 + row, WIDTH))
    post_attn_gain, ffn_gain, post_ffn_gain = gains[1:2], gains[2:3], gains[3:4]
    output_weight = output_w[...].reshape(HEADS * HEAD, WIDTH)
    all_attended = attended[...].reshape(TOKENS, HEADS * HEAD)
    projected = dot(all_attended, output_weight)
    proj_inverse = inverse_rms(projected)
    proj_unit = projected * proj_inverse
    tokens = jnp.concatenate([mine[j, :BLOCK] for j in range(4)], 0)
    middle = tokens.astype(F32) + proj_unit * post_attn_gain
    mid_inverse = inverse_rms(middle)
    mid_unit = middle * mid_inverse
    ffn_in = (mid_unit * ffn_gain).astype(BF16)
    input_a = dot(ffn_in, picks[0]).astype(BF16)
    input_b = dot(ffn_in, picks[1]).astype(BF16)
    inputs_s[core] = dot(ffn_in, picks[2]).astype(BF16)
    inputs_s[1 - core] = input_b
    for copy in fetch(own, gate_w, 0) + fetch(own, up_w, 4):
        copy.wait()
    down = jnp.zeros((TOKENS, WIDTH), F32)
    for n in range(HIDDEN // CHUNK):
        columns = slice(n * CHUNK, (n + 1) * CHUNK)
        gate = dot(input_a, gate_w[:, columns])
        up = dot(input_b, up_w[:, columns])
        active, slope = gelu_parts(gate)
        active_s[:, columns] = active.astype(BF16)
        slope_s[:, columns] = (slope * up).astype(BF16)
        inner = (active * up).astype(BF16)
        inner_s[:, columns] = inner
        blocks = slice(n * (CHUNK // 16), (n + 1) * (CHUNK // 16))
        down += dot(inner, down_w[blocks].reshape(CHUNK, WIDTH))
    down_inverse = inverse_rms(down)
    down_unit = down * down_inverse
    block_out = (middle + down_unit * post_ffn_gain).astype(BF16)
    block_out_ref[...] = block_out.reshape(4, BLOCK, WIDTH)
    out_grad = cotangent[...].reshape(TOKENS, WIDTH).astype(F32)
    gain_ref[16:24] = add_rows(out_grad * down_unit)
    down_grad = norm_backward(out_grad * post_ffn_gain, down_unit, down_inverse).astype(BF16)
    sum_a = jnp.zeros((TOKENS, WIDTH), F32)
    sum_b = jnp.zeros((TOKENS, WIDTH), F32)
    sent = []
    for n in range(HIDDEN // CHUNK):
        columns = slice(n * CHUNK, (n + 1) * CHUNK)
        blocks = slice(n * (CHUNK // 16), (n + 1) * (CHUNK // 16))
        inner_grad = dot_nt(down_grad, down_w[blocks].reshape(CHUNK, WIDTH))
        gate_grad = (inner_grad * slope_s[:, columns].astype(F32)).astype(BF16)
        up_grad = (inner_grad * active_s[:, columns].astype(F32)).astype(BF16)
        grads_s[core] = gate_grad
        grads_s[1 - core] = up_grad
        grad_down[blocks] = (
            dot_tn(inner_s[:, columns], down_grad).astype(BF16).reshape(CHUNK // 16, 16, WIDTH)
        )
        keep_s[:, columns] = dot_tn(inputs_s[0], grads_s[0]).astype(BF16)
        give_s[:, columns] = dot_tn(inputs_s[1], grads_s[1]).astype(BF16)
        for source, target, k in ((keep_s, keep_ref, n), (give_s, give_ref, 4 + n)):
            copy = pltpu.make_async_copy(
                source.at[:, columns], target.at[:, columns], leaving.at[k]
            )
            copy.start()
            sent.append(copy)
        sum_a += dot_nt(gate_grad, gate_w[:, columns])
        sum_b += dot_nt(up_grad, up_w[:, columns])
    ffn_in_grad = dot_nt(sum_a.astype(BF16), picks[0]) + dot_nt(sum_b.astype(BF16), picks[1])
    gain_ref[8:16] = add_rows(ffn_in_grad * mid_unit)
    middle_grad = out_grad + norm_backward(ffn_in_grad * ffn_gain, mid_unit, mid_inverse)
    middle_grad_ref[...] = middle_grad
    gain_ref[0:8] = add_rows(middle_grad * proj_unit)
    proj_grad = norm_backward(middle_grad * post_attn_gain, proj_unit, proj_inverse).astype(BF16)
    attended_grad_ref[...] = dot_nt(proj_grad, output_weight).astype(BF16)
    output_w[...] = dot_tn(all_attended, proj_grad).astype(BF16).reshape(64, 16, WIDTH)
    pad = jnp.zeros((16, 2 * OUT_COLS - WIDTH), BF16)

    def hand(i, carry):
        grad_a = output_w[table[4, i], :, :OUT_COLS]
        grad_b = jnp.concatenate([output_w[table[5, i], :, OUT_COLS:], pad], 1)
        keep_down_s[i, :, :OUT_COLS] = jnp.where(first_core, grad_a, grad_b)
        give_down_s[i, :, :OUT_COLS] = jnp.where(first_core, grad_b, grad_a)
        keep_down_s[i, :, OUT_COLS:] = grad_down[table[6, i]]
        give_down_s[i, :, OUT_COLS:] = grad_down[table[7, i]]
        return carry

    lax.fori_loop(0, 64, hand, 0, unroll=8)
    for source, target, k in (
        (keep_down_s, keep_down_ref, 8),
        (give_down_s, give_down_ref, 9),
    ):
        copy = pltpu.make_async_copy(source, target, leaving.at[k])
        copy.start()
        sent.append(copy)
    for copy in sent:
        copy.wait()


def feed_forward(
    meta, table, gains, mine, cotangent, attended, own, other, own_down, other_down
):
    return call(
        feed_kernel,
        "feed_forward",
        [
            ((4, BLOCK, WIDTH), BF16),
            ((TOKENS, WIDTH), F32),
            ((TOKENS, HEADS * HEAD), BF16),
            ((24, WIDTH), F32),
            ((WIDTH, HIDDEN), BF16),
            ((WIDTH, HIDDEN), BF16),
            ((64, 16, DOWN_PACK), BF16),
            ((64, 16, DOWN_PACK), BF16),
        ],
        [smem(), smem()] + [vmem()] * 4 + [anywhere()] * 8 + [vmem()] * 8,
        [meta, table, gains, mine, cotangent, attended, *own, *other, *own_down, *other_down],
        out_specs=[vmem()] * 4 + [anywhere()] * 4,
        scratch=[
            pltpu.VMEM((WIDTH, HIDDEN), BF16),
            pltpu.VMEM((WIDTH, HIDDEN), BF16),
            pltpu.VMEM((128, 16, WIDTH), BF16),
            pltpu.VMEM((64, 16, WIDTH), BF16),
            pltpu.VMEM((TOKENS, HIDDEN), BF16),
            pltpu.VMEM((TOKENS, HIDDEN), BF16),
            pltpu.VMEM((TOKENS, HIDDEN), BF16),
            pltpu.VMEM((2, TOKENS, WIDTH), BF16),
            pltpu.VMEM((2, TOKENS, CHUNK), BF16),
            pltpu.VMEM((WIDTH, HIDDEN), BF16),
            pltpu.VMEM((WIDTH, HIDDEN), BF16),
            pltpu.VMEM((128, 16, WIDTH), BF16),
            pltpu.VMEM((64, 16, DOWN_PACK), BF16),
            pltpu.VMEM((64, 16, DOWN_PACK), BF16),
            pltpu.SemaphoreType.DMA((8,)),
            pltpu.SemaphoreType.DMA((10,)),
        ],
        megabytes=60,
        flops=17 * 10**9,
        moved_bytes=30 * 10**6,
    )


def attention_back_kernel(starting, first, meta, attended_grad, probs, queries, keys, values, *refs):
    step = pl.program_id(0)
    if starting:
        key_sum, value_sum, query_sum = refs

        @pl.when(step == 0)
        def _():
            key_sum[...] = jnp.zeros_like(key_sum)
            value_sum[...] = jnp.zeros_like(value_sum)
    else:
        sources, outs = refs[:14], refs[14:18]
        key_sum, value_sum, query_sum, part_a, part_b, arrivals = refs[18:24]
        held = refs[24:]
        copies = [
            pltpu.make_async_copy(source, target, arrivals.at[j])
            for j, (source, target) in enumerate(zip(sources, held))
        ]

        @pl.when(step == 0)
        def _():
            for copy in copies:
                copy.start()
            key_sum[...] = jnp.zeros_like(key_sum)
            value_sum[...] = jnp.zeros_like(value_sum)

    window = pl.ds(pl.multiple_of((step + first) * BLOCK, BLOCK), SPAN)
    mixed_grad = jnp.concatenate(
        [attended_grad[:, h * HEAD : (h + 1) * HEAD] for h in range(HEADS)], 0
    )
    prob_grad = dot_nt(mixed_grad, values[window])
    soft = probs[0].astype(F32)
    row_dot = jnp.sum(soft * prob_grad, -1, keepdims=True)
    score_grad = (soft * (prob_grad - row_dot)).astype(BF16)
    query_sum[step] = dot(score_grad, keys[window])
    key_sum[window] += dot_tn(score_grad, queries[0])
    value_sum[window] += dot_tn(probs[0], mixed_grad)
    if starting:
        return

    @pl.when(step == pl.num_programs(0) - 1)
    def _():
        for copy in copies:
            copy.wait()
        key_sum[...] += held[0][...]
        value_sum[...] += held[1][...]
        finish_attention(
            meta, key_sum, value_sum, query_sum, held[2], part_a, part_b, *held[3:], *outs
        )


def finish_attention(
    meta,
    key_sum,
    value_sum,
    query_sum,
    query_last,
    part_a,
    part_b,
    weights,
    gains,
    head_gains,
    cosine,
    sine,
    mine,
    before,
    normed,
    key_pre,
    query_pre,
    feed_gain,
    own_ref,
    before_ref,
    keep_ref,
    give_ref,
):
    query_gain, key_gain = head_gains[4:5] * SCALE, head_gains[5:6] * SCALE
    cosine_own, sine_own = cosine[TOKENS:], -sine[TOKENS:]
    query_total = jnp.zeros((8, HEAD), F32)
    pre_grads = []
    for h in range(HEADS):
        pre = query_pre[:, h * HEAD : (h + 1) * HEAD].astype(F32)
        inverse = inverse_rms(pre)
        unit = pre * inverse
        rows = slice(h * BLOCK, (h + 1) * BLOCK)
        grad = jnp.concatenate([part[j, rows] for part in (query_sum, query_last) for j in range(2)], 0)
        turned = rotate(grad, cosine_own, sine_own)
        query_total += add_rows(turned * unit)
        pre_grads.append(norm_backward(turned * query_gain, unit, inverse).astype(BF16))
    query_pre_grad = jnp.concatenate(pre_grads, 1)
    pre = key_pre[...].astype(F32)
    inverse = inverse_rms(pre)
    unit = pre * inverse
    turned = rotate(key_sum[...], cosine[...], -sine[...])
    key_total = add_rows(turned * unit)
    key_pre_grad = norm_backward(turned * key_gain, unit, inverse).astype(BF16)
    both = jnp.concatenate([key_pre_grad, value_sum[...].astype(BF16)], 1)
    normed_grad = dot_nt(both, weights[:, HEADS * HEAD :])
    own = normed_grad[TOKENS:] + dot_nt(query_pre_grad, weights[:, : HEADS * HEAD])
    own_ref[...] = own
    before_ref[...] = normed_grad[:TOKENS].astype(BF16)
    normed_grad = jnp.concatenate([normed_grad[:TOKENS], own], 0)
    tokens = jnp.concatenate(
        [part[j, :BLOCK] for part in (before, mine) for j in range(4)], 0
    ).astype(F32)
    attn_total = add_rows(tokens * inverse_rms(tokens) * normed_grad)
    pick_a, pick_b, gain_shard = line_picks(meta, SCATTER)
    query_weight_grad = dot_tn(normed[TOKENS:], query_pre_grad).astype(BF16)
    part_a[...] = dot_tn(pick_a, query_weight_grad[:, :ATT_COLS]).astype(BF16)
    both_grad = dot_tn(normed[...], both).astype(BF16)
    part_b[:, 256:] = dot_tn(pick_b, both_grad).astype(BF16)
    pick, pick_head = gain_picks(gain_shard)
    wide = jnp.zeros((128, WIDTH), F32)
    totals = (attn_total, feed_gain[0:8], feed_gain[8:16], feed_gain[16:24])
    for g in range(4):
        line = jnp.sum(totals[g], 0, keepdims=True)
        wide += jnp.where(gain_lanes(128, WIDTH, 5, 5 * g), line, 0.0)
    head = jnp.zeros((128, HEAD), F32)
    for g, total in enumerate((query_total, key_total)):
        line = jnp.sum(total, 0, keepdims=True) * SCALE
        head += jnp.where(gain_lanes(128, HEAD, 2, 20 + 2 * g), line, 0.0)
    contract = (((0,), (1,)), ((), ()))
    gain_block = lax.dot_general(
        pick, wide.astype(BF16), contract, preferred_element_type=F32
    ) + lax.dot_general(pick_head, head.astype(BF16), contract, preferred_element_type=F32)
    left = dot_tn(pick_b, query_weight_grad[:, ATT_COLS:])
    part_b[:, :128] = (left[:, :128] + gain_block).astype(BF16)
    part_b[:, 128:256] = left[:, 128:].astype(BF16)
    first_core = meta[3] == 0
    keep_ref[...] = jnp.where(first_core, part_a[...], part_b[...])
    give_ref[...] = jnp.where(first_core, part_b[...], part_a[...])


def attention_back(first, count, meta, attended_grad, probs, kept, earlier, inputs, after):
    starting = earlier is None
    sums = [((KEYS, HEAD), F32), ((KEYS, HEAD), F32), ((count, HEADS * BLOCK, HEAD), F32)]
    in_specs = [
        smem(),
        pl.BlockSpec((BLOCK, HEADS * HEAD), lambda r: (r + first, 0)),
        from_row((HEADS * BLOCK, SPAN), first),
        from_row((HEADS * BLOCK, HEAD), first),
        whole((KEYS, HEAD)),
        whole((KEYS, HEAD)),
    ]
    args = [meta, attended_grad, probs, kept[5], kept[1], kept[2]]
    outs = sums
    if not starting:
        args += [*earlier, *inputs]
        in_specs += [anywhere()] * 14
        outs = [((TOKENS, WIDTH), F32), ((TOKENS, WIDTH), BF16)] + [((1024, ATT_COLS), BF16)] * 2
    return call(
        functools.partial(attention_back_kernel, starting, first),
        "attention_back",
        outs,
        in_specs,
        args,
        out_specs=[whole(s) for s, _ in outs],
        scratch=[]
        if starting
        else [pltpu.VMEM(s, d) for s, d in sums]
        + [pltpu.VMEM((1024, ATT_COLS), BF16)] * 2
        + [pltpu.SemaphoreType.DMA((14,))]
        + [pltpu.VMEM(value.shape, value.dtype) for value in (*earlier, *inputs)],
        after=after,
        grid=(count,),
        megabytes=60,
        flops=count * 5 * 10**9,
        moved_bytes=count * 12 * 10**6,
    )


def pack_kernel(meta, query, key, value, output, gate, up, gains, keep_ref, give_ref, part):
    for half in range(2):
        part[half] = jnp.zeros((8, PACK), F32)
    out_start = ATT_COLS
    feed_start = ATT_COLS + OUT_COLS
    left = HEADS * HEAD - ATT_COLS
    part[0, :5, :ATT_COLS] = query[:, :ATT_COLS].astype(F32)
    part[0, :, out_start:feed_start] = output[:, :OUT_COLS].astype(F32)
    part[0, :5, feed_start:] = gate[...].astype(F32)
    part[1, :5, :left] = query[:, ATT_COLS:].astype(F32)
    part[1, :5, left : left + HEAD] = key[...].astype(F32)
    part[1, :5, left + HEAD : ATT_COLS] = value[...].astype(F32)
    part[1, 5:6, :128] = gains[...].astype(F32)
    part[1, :, out_start : out_start + WIDTH - OUT_COLS] = output[:, OUT_COLS:].astype(F32)
    part[1, :5, feed_start:] = up[...].astype(F32)
    core = meta[3]
    keep_ref[...] = part[core].astype(BF16)
    give_ref[...] = part[1 - core].astype(BF16)


def pack_weights(meta, query, key, value, output, gate, up, gains):
    return call(
        pack_kernel,
        "pack_weights",
        [((8, PACK), BF16)] * 2,
        [smem()] + [vmem()] * 7,
        [meta, query, key, value, output, gate, up, gains],
        scratch=[pltpu.VMEM((2, 8, PACK), F32)],
        megabytes=60,
        flops=10**6,
        moved_bytes=3 * 10**5,
    )


def pair_kernel(meta, kept, crossed, down, out_ref):
    first_core = meta[3] == 0
    mine, theirs = kept[...].astype(F32), crossed[...].astype(F32)
    upper = jnp.where(first_core, mine, theirs)
    lower = jnp.where(first_core, theirs, mine)
    out_ref[:, :PACK] = jnp.concatenate([upper, lower], 0).astype(BF16)
    out_ref[:, PACK:] = down[...]


def pair_up(meta, kept, crossed, down):
    return call(
        pair_kernel,
        "pair_up",
        [((16, PACK + WIDTH), BF16)],
        [smem()] + [vmem()] * 3,
        [meta, kept, crossed, down],
        megabytes=16,
        flops=10**6,
        moved_bytes=4 * 10**5,
    )[0]


def split_kernel(slot, meta, value, *refs):
    for j in range(4):
        refs[j][...] = value[meta[slot] ^ j]


def split_up(meta, slot, value, after):
    return call(
        functools.partial(split_kernel, slot),
        "split_up",
        [(value.shape[1:], value.dtype)] * 4,
        [smem(), vmem()],
        [meta, value],
        after=after,
        megabytes=16,
        flops=10**6,
        moved_bytes=10**6,
    )


def join_tokens_kernel(slot, meta, *refs):
    for j in range(4):
        refs[4][meta[slot] ^ j] = refs[j][:TAGGED]
        refs[5][meta[slot] ^ j] = refs[j][TAGGED:]


def join_tokens(meta, slot, pieces, after):
    return call(
        functools.partial(join_tokens_kernel, slot),
        "join_tokens",
        [((4, TAGGED, WIDTH), BF16), ((4, BLOCK, WIDTH), BF16)],
        [smem()] + [vmem()] * 4,
        [meta, *pieces],
        after=after,
        megabytes=16,
        flops=10**6,
        moved_bytes=10**6,
    )


def hold_kernel(*refs):
    pass


def hold(values, after):
    return call(
        hold_kernel,
        "hold",
        [(value.shape, value.dtype) for value in values],
        [anywhere()] * len(values),
        values,
        out_specs=[anywhere()] * len(values),
        after=after,
        aliases={j: j for j in range(len(values))},
        megabytes=60,
        flops=10**4,
        moved_bytes=10**4,
    )


def add_pieces_kernel(kept, crossed, *refs):
    rows = refs[0].shape[0]
    for j in range(4):
        here = slice(j * rows, (j + 1) * rows)
        refs[j][...] = (kept[here].astype(F32) + crossed[here].astype(F32)).astype(BF16)


def add_pieces(kept, crossed, after, megabytes=60):
    shape = (kept.shape[0] // 4,) + kept.shape[1:]
    return call(
        add_pieces_kernel,
        "add_pieces",
        [(shape, BF16)] * 4,
        [vmem()] * 2,
        [kept, crossed],
        after=after,
        megabytes=megabytes,
        flops=10**7,
        moved_bytes=8 * 10**6,
    )


def line_kernel(*refs):
    total = add_up(refs[0][...], [ref[...] for ref in refs[1:4]]).astype(BF16)
    for j in range(4):
        refs[4 + j][...] = total[j]


def line_up(own, others, after):
    return call(
        line_kernel,
        "line_up",
        [(own.shape[1:], BF16)] * 4,
        [vmem()] * 4,
        [own, *others],
        after=after,
        megabytes=16,
        flops=10**6,
        moved_bytes=2 * 10**6,
    )


def total_kernel(meta, *refs):
    total = add_up(refs[0][...], [ref[...] for ref in refs[1:4]])
    keep_ref, give_ref, down_ref = refs[4:]
    first_core = meta[3] == 0
    upper, lower = total[:8, :PACK], total[8:, :PACK]
    keep_ref[...] = jnp.where(first_core, upper, lower)
    give_ref[...] = jnp.where(first_core, lower, upper)
    down_ref[...] = total[:, PACK:]


def total_up(meta, own, others):
    return call(
        total_kernel,
        "total_up",
        [((8, PACK), F32)] * 2 + [((16, WIDTH), F32)],
        [smem()] + [vmem()] * 4,
        [meta, own, *others],
        megabytes=16,
        flops=10**6,
        moved_bytes=10**6,
    )


def output_kernel(slot, meta, gains, middle_grad, own, returned, mine, block_out, *refs):
    tokens = jnp.concatenate([mine[j, :BLOCK] for j in range(4)], 0).astype(F32)
    inverse = inverse_rms(tokens)
    normed_grad = own[...] + returned[...].astype(F32)
    grad = middle_grad[...] + norm_backward(normed_grad * gains[0:1], tokens * inverse, inverse)
    refs[4][...] = grad.astype(BF16).reshape(4, BLOCK, WIDTH)
    for j in range(4):
        refs[j][0] = block_out[meta[slot] ^ j]
        refs[j][1] = refs[4][meta[slot] ^ j]


def output_pieces(meta, slot, gains, middle_grad, own, returned, mine, block_out):
    return call(
        functools.partial(output_kernel, slot),
        "output_pieces",
        [((2, BLOCK, WIDTH), BF16)] * 4,
        [smem()] + [vmem()] * 6,
        [meta, gains, middle_grad, own, returned, mine, block_out],
        scratch=[pltpu.VMEM((4, BLOCK, WIDTH), BF16)],
        megabytes=16,
        flops=10**7,
        moved_bytes=5 * 10**6,
    )


def join_outputs_kernel(slot, meta, *refs):
    for j in range(4):
        for k in range(2):
            refs[4 + k][meta[slot] ^ j] = refs[j][k]


def join_outputs(meta, slot, pieces):
    return call(
        functools.partial(join_outputs_kernel, slot),
        "join_outputs",
        [((4, BLOCK, WIDTH), BF16)] * 2,
        [smem()] + [vmem()] * 4,
        [meta, *pieces],
        megabytes=16,
        flops=10**6,
        moved_bytes=2 * 10**6,
    )


def stack_kernel(*refs):
    for j in range(4):
        refs[4][j] = refs[j][...]


def stack_kernel(*refs):
    for j in range(4):
        refs[4][j] = refs[j][...]


def stack_both_kernel(*refs):
    for j in range(8):
        refs[8 + j // 4][j % 4] = refs[j][...]


def stack_both(first, second, after):
    return call(
        stack_both_kernel,
        "stack_both",
        [((4,) + first[0].shape, BF16), ((4,) + second[0].shape, BF16)],
        [vmem()] * 8,
        [*first, *second],
        after=after,
        megabytes=16,
        flops=10**6,
        moved_bytes=10**7,
    )


def stack_up(pieces, shape, after):
    return call(
        stack_kernel,
        "stack_up",
        [((4,) + shape, BF16)],
        [vmem()] * 4,
        pieces,
        after=after,
        megabytes=16,
        flops=10**6,
        moved_bytes=4 * 10**6,
    )[0]


def first_slab_kernel(*refs):
    for j in range(4):
        here = slice(j * 64, (j + 1) * 64)
        refs[4][here, :ATT_COLS] = refs[j][:, :, :ATT_COLS].reshape(64, ATT_COLS)
        refs[4][here, ATT_COLS : ATT_COLS + OUT_COLS] = refs[j][
            :, :, ATT_COLS : ATT_COLS + OUT_COLS
        ].reshape(64, OUT_COLS)
        refs[4][here, ATT_COLS + OUT_COLS :] = refs[j][:, :, PACK:].reshape(64, WIDTH)


def first_slab(pieces, after):
    return call(
        first_slab_kernel,
        "first_slab",
        [((256, FIRST_PACK), BF16)],
        [vmem()] * 4,
        pieces,
        after=after,
        megabytes=16,
        flops=10**6,
        moved_bytes=3 * 10**6,
    )[0]


def loose_rows():
    line = lax.broadcasted_iota(jnp.int32, (256, 160), 0)
    row = line & 7
    dense = lax.broadcasted_iota(jnp.int32, (256, 160), 1)
    same = ((line >> 3) * 5 + row == dense) & (row < 5)
    return jnp.where(same, 1.0, 0.0).astype(BF16)


def feed_slab_kernel(*refs):
    feed_ref, loose = refs[4:]
    for j in range(4):
        loose[j * 64 : (j + 1) * 64] = refs[j][:, :, ATT_COLS + OUT_COLS : PACK].reshape(
            64, HIDDEN
        )
    feed_ref[...] = dot_tn(loose_rows(), loose[...]).astype(BF16)


def feed_slab_of(pieces, after):
    return call(
        feed_slab_kernel,
        "feed_slab",
        [((160, HIDDEN), BF16)],
        [vmem()] * 4,
        pieces,
        scratch=[pltpu.VMEM((256, HIDDEN), BF16)],
        after=after,
        megabytes=16,
        flops=2 * 10**8,
        moved_bytes=4 * 10**6,
    )[0]


def merge_kernel(*refs):
    sources, outs, held, arrivals = refs[:12], refs[12:16], refs[16:28], refs[28]
    copies = [
        pltpu.make_async_copy(source, target, arrivals.at[j])
        for j, (source, target) in enumerate(zip(sources, held))
    ]
    for copy in copies:
        copy.start()

    def total(first):
        for copy in copies[first : first + 4]:
            copy.wait()
        pieces = held[first : first + 4]
        return add_up(pieces[0][...], [piece[...] for piece in pieces[1:]]).astype(BF16)

    def hand_out(value, start):
        for j in range(4):
            outs[j][:, :, start : start + value.shape[2]] = value[j * 4 : (j + 1) * 4]

    hand_out(total(0).reshape(16, 16, ATT_COLS), 0)
    hand_out(total(8), ATT_COLS + HIDDEN)
    feed_total = dot(loose_rows(), total(4)).astype(BF16)
    hand_out(feed_total.reshape(16, 16, HIDDEN), ATT_COLS)


def merge_grads(att, feed, down):
    pieces = [*att, *feed, *down]
    return call(
        merge_kernel,
        "merge_grads",
        [((4, 16, PACK + WIDTH), BF16)] * 4,
        [anywhere()] * 12,
        pieces,
        scratch=[pltpu.VMEM(piece.shape, piece.dtype) for piece in pieces]
        + [pltpu.SemaphoreType.DMA((12,))],
        megabytes=30,
        flops=2 * 10**8,
        moved_bytes=8 * 10**6,
    )


def unpack_kernel(meta, mine, theirs, query, key, value, output, gate, up, gains):
    first_core = meta[3] == 0
    part_a = jnp.where(first_core, mine[...], theirs[...])
    part_b = jnp.where(first_core, theirs[...], mine[...])
    left = HEADS * HEAD - ATT_COLS
    feed_end = ATT_COLS + HIDDEN
    query[:, :ATT_COLS] = part_a[:5, :ATT_COLS]
    query[:, ATT_COLS:] = part_b[:5, :left]
    key[...] = part_b[:5, left : left + HEAD]
    value[...] = part_b[:5, left + HEAD : ATT_COLS]
    gate[...] = part_a[:5, ATT_COLS:feed_end]
    up[...] = part_b[:5, ATT_COLS:feed_end]
    output[:, :OUT_COLS] = part_a[:, feed_end:]
    output[:, OUT_COLS:] = part_b[:, feed_end : feed_end + WIDTH - OUT_COLS]
    gains[...] = part_b[5:6, :128]


def unpack_grads(meta, mine, theirs):
    return call(
        unpack_kernel,
        "unpack_grads",
        [
            ((5, HEADS * HEAD), F32),
            ((5, HEAD), F32),
            ((5, HEAD), F32),
            ((8, WIDTH), F32),
            ((5, HIDDEN), F32),
            ((5, HIDDEN), F32),
            ((1, 128), F32),
        ],
        [smem()] + [vmem()] * 2,
        [meta, mine, theirs],
        megabytes=16,
        flops=10**6,
        moved_bytes=4 * 10**5,
    )


def on_device(
    hidden_in,
    segment_ids,
    cotangent,
    attn_gain,
    query_weight,
    key_weight,
    value_weight,
    query_gain,
    key_gain,
    output_weight,
    post_attn_gain,
    ffn_gain,
    gate_weight,
    up_weight,
    down_weight,
    post_ffn_gain,
):
    me = my_place()
    core = me["c"]
    first_core = core == 0
    row = 2 * ((me["x"] ^ (me["x"] >> 1)) & 1) + core
    member = 2 * (me["x"] & 1) + core
    place = (me["y"] >> 1) * 1024 + (me["x"] >> 1) * TOKENS
    meta = jnp.stack([me["z"], me["y"], me["x"], core, place, row, member]).astype(jnp.int32)
    row_slot, member_slot = 5, 6

    def pick(value_first, value_second):
        return jnp.where(first_core, value_first, value_second)

    positions = place + jnp.arange(-TOKENS, TOKENS, dtype=jnp.int32)
    frequency = jnp.exp(
        jnp.arange(HEAD // 2, dtype=F32) * (-2.0 * math.log(ROPE_BASE) / HEAD)
    )
    angles = positions.astype(F32)[:, None] * frequency[None]
    tables = (jnp.cos(angles), jnp.sin(angles))

    gains = jnp.zeros((128,), F32)
    start = 0
    for gain in (attn_gain, post_attn_gain, ffn_gain, post_ffn_gain, query_gain, key_gain):
        size = gain.shape[0]
        gains = gains + jnp.pad(gain.astype(F32), (start, 128 - start - size))
        start += size
    kept, given = pack_weights(
        meta,
        query_weight,
        key_weight,
        value_weight,
        output_weight,
        gate_weight,
        up_weight,
        gains.reshape(1, 128),
    )
    pair = pair_up(meta, kept, swap(given), down_weight)
    near_chips = arrived(pair, 0)

    segments = segment_ids.reshape(4, 1, BLOCK).astype(BF16)
    segments = jnp.pad(segments, ((0, 0), (0, TAGGED - BLOCK - 1), (0, WIDTH - BLOCK)))
    dealing = jnp.concatenate(
        [
            hidden_in.reshape(4, BLOCK, WIDTH),
            segments,
            cotangent.reshape(4, BLOCK, WIDTH),
        ],
        1,
    )
    own, one, two, three = split_up(meta, row_slot, dealing, [])
    pieces = [own, swap(one), exchange(two, False), exchange(three, True)]
    mine, cotangent_mine = join_tokens(meta, member_slot, pieces, near_chips)
    near, before = next_chunk(mine, me["x"] < 2)

    line = stack_up([pair, *near_chips], pair.shape, [mine])
    plane = [line, *arrived(line, 1)]
    plane = [line, *arrived(line, 1)]
    slab = first_slab(plane, [*tables, near])
    first_own = [slab, *arrived(slab, 2)]
    first_other = [swap(value) for value in first_own]
    feed_slab = feed_slab_of(plane, first_own[1:])

    grid = jnp.arange(64, dtype=jnp.int32)
    table = []
    for orders in (GATHER, SCATTER):
        chips = [chip_of([me["z"], me["y"], me["x"]], order, grid) for order in orders]
        held, crossed = pick(chips[0], chips[1]), pick(chips[1], chips[0])
        table += [*chips, held * 2 + core, crossed * 2 + 1 - core]
    table = jnp.stack(table).astype(jnp.int32)

    forward = attention_blocks(0, 4, meta, mine, before, tables, first_own + first_other, None, [])
    made, kept_values, (attended, probs) = forward[:3], forward[3:9], forward[9:]
    feed_own = [feed_slab, *hold(arrived(feed_slab, 2), [attended])]
    (
        block_out,
        middle_grad,
        attended_grad,
        feed_gain,
        keep_feed,
        give_feed,
        keep_down,
        give_down,
    ) = feed_forward(
        meta,
        table,
        made[1],
        mine,
        cotangent_mine,
        attended,
        feed_own,
        [swap(value) for value in feed_own],
        first_own,
        first_other,
    )
    back = attention_back(2, 2, meta, attended_grad, probs, kept_values, None, None, [])
    feed_sum = add_pieces(keep_feed, swap(give_feed), [back[0]])
    down_sum = add_pieces(keep_down, swap(give_down), [back[0]])
    normed_grad, to_before, keep_att, give_att = attention_back(
        0,
        2,
        meta,
        attended_grad,
        probs,
        kept_values,
        back,
        (
            *made,
            *tables,
            mine,
            before,
            kept_values[0],
            kept_values[3],
            kept_values[4],
            feed_gain,
        ),
        [*feed_sum, *down_sum],
    )
    feed_in = received(feed_sum, 2)
    down_in = received(down_sum, 2)

    give_att = hold([give_att], [*feed_in, *down_in[:2]])[0]
    att_sum = add_pieces(keep_att, swap(give_att), [], 24)
    plane = merge_grads(
        [att_sum[0], *received(att_sum, 2)], [feed_sum[0], *feed_in], [down_sum[0], *down_in]
    )
    returned = chunk_before(to_before)
    own, one, two, three = output_pieces(
        meta, member_slot, made[1], middle_grad, normed_grad, returned, mine, block_out
    )
    line = line_up(plane[0], received(plane, 1), [own])
    kept_grads, given_grads, grad_down = total_up(meta, line[0], received(line, 0))
    grad_query, grad_key, grad_value, grad_output, grad_gate, grad_up, gain_grads = unpack_grads(
        meta, kept_grads, swap(given_grads)
    )
    gain_grads = gain_grads.reshape(128)

    block_out, input_grad = join_outputs(
        meta, row_slot, [own, swap(one), exchange(two, False), exchange(three, True)]
    )
    return (
        block_out.reshape(hidden_in.shape),
        input_grad.reshape(hidden_in.shape),
        gain_grads[0:5],
        grad_query,
        grad_key,
        grad_value,
        gain_grads[20:22],
        gain_grads[22:24],
        grad_output,
        gain_grads[5:10],
        gain_grads[10:15],
        grad_gate,
        grad_up,
        grad_down,
        gain_grads[15:20],
    )


def solution(mesh):
    rows = P(None, "dp", "seq", None)
    shard = P(("dp", "seq"), None)
    vector = P(("dp", "seq"))
    return jax.shard_map(
        on_device,
        mesh=mesh,
        in_specs=(rows, P(None, "dp", "seq"), rows)
        + (vector, shard, shard, shard, vector, vector, shard, vector)
        + (vector, shard, shard, shard, vector),
        out_specs=(rows, rows)
        + (vector, shard, shard, shard, vector, vector, shard, vector)
        + (vector, shard, shard, shard, vector),
        check_vma=False,
    )
```

```python
import functools
import math

import jax
import jax.numpy as jnp
from jax import lax
from jax.experimental import pallas as pl
from jax.experimental.pallas import tpu as pltpu
from jax.sharding import PartitionSpec as P

WINDOW = 512
HALO = 4
BLOCK = 128
TOKENS = 512
KEYS = 1024
WIDTH = 640
HEADS = 4
HEAD = 256
HIDDEN = 2048
SPAN = (HALO + 1) * BLOCK
CHUNK = 512
TAGGED = BLOCK + 16
EPSILON = 1e-06
ROPE_BASE = 10000.0
MASKED = -1e30
SCALE = HEAD ** (-0.5)
F32 = jnp.float32
BF16 = jnp.bfloat16

AXES = ("dp", "seq")
SIZE = {"x": 4, "y": 4, "z": 4, "c": 2}
GATHER = (("x", "y", "z"), ("y", "z", "x"))
SCATTER = (("y", "x", "z"), ("y", "z", "x"))
ATT_COLS = 768
OUT_COLS = 384
DOWN_PACK = OUT_COLS + WIDTH
PACK = ATT_COLS + OUT_COLS + HIDDEN
FIRST_PACK = ATT_COLS + DOWN_PACK


def shard_of(z, y, x, c):
    return z * 32 + (y % 2) * 16 + (y // 2) * 8 + x * 2 + c


def moved(axis_of_core, by):
    pairs = []
    for z in range(4):
        for y in range(4):
            for x in range(4):
                for c in range(2):
                    place = {"z": z, "y": y, "x": x, "c": c}
                    axis = axis_of_core[c]
                    place[axis] = (place[axis] + by) % SIZE[axis]
                    pairs.append((shard_of(z, y, x, c), shard_of(**place)))
    return pairs


def send(value, orders, phase, by):
    axes = (orders[0][phase], orders[1][phase])
    return lax.ppermute(value, AXES, moved(axes, by))


def swap(value):
    return lax.ppermute(value, AXES, moved(("c", "c"), 1))


def exchange(value, flip):
    pairs = []
    for i in range(128):
        pairs.append((i, i ^ (3 if flip else 2)))
    return lax.ppermute(value, AXES, pairs)


def next_chunk(value, first_half):
    along, across = [], []
    for dp in range(8):
        for c in range(2):
            for x in range(4):
                for yh in range(2):
                    if x >= 2 and yh == 1:
                        continue
                    here = dp * 16 + yh * 8 + x * 2 + c
                    along.append((here, here + (3 - 2 * x) * 2))
            for x in range(2):
                here = dp * 16 + x * 2 + c
                across.append((here, here + 8))
    near = lax.ppermute(value, AXES, along)
    return near, jnp.where(first_half, lax.ppermute(near, AXES, across), near)


def chunk_before(value):
    pairs = []
    for dp in range(8):
        for yh in range(2):
            for x in range(4):
                for c in range(2):
                    if x >= 2 and yh == 1:
                        continue
                    here = dp * 16 + yh * 8 + x * 2 + c
                    there = dp * 16 + (yh + (x >= 2)) * 8 + (3 - x) * 2 + c
                    pairs.append((there, here))
    return lax.ppermute(value, AXES, pairs)


def my_place():
    dp, seq = lax.axis_index("dp"), lax.axis_index("seq")
    return {"z": dp // 2, "y": (seq // 8) * 2 + dp % 2, "x": (seq // 2) % 4, "c": seq % 2}


def arrived(value, phase):
    one, three, two = [send(value, GATHER, phase, -by) for by in (1, 3, 2)]
    return [one, two, three]


def received(pieces, phase):
    return [send(pieces[by], SCATTER, phase, by) for by in (1, 3, 2)]


def add_up(own, others):
    total = own.astype(F32)
    for other in others:
        total = total + other.astype(F32)
    return total


def chip_at(meta, order, j3, j2, j1):
    place = {
        order[2]: (meta["zyx".index(order[2])] + j3) & 3,
        order[1]: (meta["zyx".index(order[1])] + j2) & 3,
        order[0]: (meta["zyx".index(order[0])] + j1) & 3,
    }
    z, y, x = place["z"], place["y"], place["x"]
    return z * 16 + (y & 1) * 8 + (y >> 1) * 4 + x


def chip_of(meta, order, i):
    return chip_at(meta, order, i >> 4, (i >> 2) & 3, i & 3)


def slab_rows(meta, order, rows_held):
    line = lax.broadcasted_iota(jnp.int32, (1, 128 * rows_held), 1)
    if rows_held == 8:
        both, row = line >> 3, line & 7
    else:
        both = lax.shift_right_logical(line * 52429, 18)
        row = line - both * 5
    return chip_of(meta, order, both >> 1) * 2 + (both & 1), row


def dot(a, b):
    return jnp.dot(a, b, preferred_element_type=F32)


def dot_nt(a, b):
    return lax.dot_general(a, b, (((1,), (1,)), ((), ())), preferred_element_type=F32)


def dot_tn(a, b):
    return lax.dot_general(a, b, (((0,), (0,)), ((), ())), preferred_element_type=F32)


def add_rows(values):
    total = values[:8]
    for first in range(8, values.shape[0], 8):
        total = total + values[first : first + 8]
    return total


def one_hot(index_row, count):
    places = lax.broadcasted_iota(jnp.int32, (count, index_row.shape[1]), 0)
    return jnp.where(places == index_row, 1.0, 0.0).astype(BF16)


def inverse_rms(values):
    return lax.rsqrt(jnp.mean(values * values, -1, keepdims=True) + EPSILON)


def norm_backward(grad_hat, unit_value, inverse):
    return inverse * (grad_hat - unit_value * jnp.mean(grad_hat * unit_value, -1, keepdims=True))


def rotate(values, cosine, sine):
    first, second = values[:, : HEAD // 2], values[:, HEAD // 2 :]
    return jnp.concatenate(
        [first * cosine - second * sine, second * cosine + first * sine], axis=-1
    )


def vmem():
    return pl.BlockSpec(memory_space=pltpu.VMEM)


def smem():
    return pl.BlockSpec(memory_space=pltpu.SMEM)


def anywhere():
    return pl.BlockSpec(memory_space=pl.ANY)


def whole(shape):
    return pl.BlockSpec(shape, lambda r: (0,) * len(shape))


def by_row(shape):
    return pl.BlockSpec((1,) + shape, lambda r: (r,) + (0,) * len(shape))


def from_row(shape, first):
    return pl.BlockSpec((1,) + shape, lambda r: (r + first,) + (0,) * len(shape))


def call(
    kernel,
    name,
    outs,
    in_specs,
    args,
    out_specs=None,
    scratch=(),
    after=(),
    aliases=None,
    grid=(),
    megabytes=58,
    flops=0,
    moved_bytes=0,
):
    after = list(after)
    count = len(in_specs)

    def body(*refs):
        kernel(*refs[:count], *refs[count + len(after) :])

    return pl.pallas_call(
        body,
        grid=grid,
        out_shape=[jax.ShapeDtypeStruct(s, d) for s, d in outs],
        in_specs=list(in_specs) + [anywhere()] * len(after),
        out_specs=[vmem()] * len(outs) if out_specs is None else out_specs,
        scratch_shapes=list(scratch),
        input_output_aliases=aliases or {},
        compiler_params=pltpu.CompilerParams(vmem_limit_bytes=megabytes * 2**20),
        cost_estimate=pl.CostEstimate(
            flops=flops, bytes_accessed=moved_bytes, transcendentals=0
        ),
        name=name,
    )(*args, *after)


def line_picks(meta, orders):
    shard_a, row_a = slab_rows(meta, orders[0], 8)
    shard_b, row_b = slab_rows(meta, orders[1], 8)
    pick_a = one_hot(jnp.where(row_a < 5, shard_a * 5 + row_a, -1), WIDTH)
    pick_b = one_hot(jnp.where(row_b < 5, shard_b * 5 + row_b, -1), WIDTH)
    return pick_a, pick_b, jnp.where(row_b == 5, shard_b, -1)


def gain_picks(shard_line):
    wide = lax.broadcasted_iota(jnp.int32, (WIDTH, shard_line.shape[1]), 0)
    first = shard_line * 5
    pick = jnp.where((wide >= first) & (wide < first + 5) & (first >= 0), 1.0, 0.0).astype(BF16)
    head = lax.broadcasted_iota(jnp.int32, (HEAD, shard_line.shape[1]), 0)
    pick_head = jnp.where((head >> 1) == shard_line, 1.0, 0.0).astype(BF16)
    return pick, pick_head


def gain_lanes(count, width, per_shard, first):
    lane = lax.broadcasted_iota(jnp.int32, (count, width), 0)
    entry = lax.broadcasted_iota(jnp.int32, (count, width), 1)
    if per_shard == 5:
        place = entry - lax.shift_right_logical(entry * 52429, 18) * 5
    else:
        place = entry & 1
    return lane == place + first


def both_parts(meta, own, other, part_a, part_b, rows):
    @pl.when(meta[3] == 0)
    def _():
        for j in range(4):
            part_a[j * rows : (j + 1) * rows] = own[j][...]
            part_b[j * rows : (j + 1) * rows] = other[j][...]

    @pl.when(meta[3] != 0)
    def _():
        for j in range(4):
            part_a[j * rows : (j + 1) * rows] = other[j][...]
            part_b[j * rows : (j + 1) * rows] = own[j][...]


def weights_kernel(meta, *refs):
    own, other = refs[:4], refs[4:8]
    weights_ref, gains_ref, head_gains_ref, part_a, part_b = refs[8:]
    both_parts(meta, own, other, part_a, part_b, 256)
    pick_a, pick_b, gain_shard = line_picks(meta, GATHER)
    weights_ref[:, :ATT_COLS] = dot(pick_a, part_a[...]).astype(BF16)
    weights_ref[:, ATT_COLS:] = dot(pick_b, part_b[...]).astype(BF16)
    pick, pick_head = gain_picks(gain_shard)
    block = part_b[:, :128]
    contract = (((0,), (1,)), ((), ()))
    wide = lax.dot_general(block, pick, contract, preferred_element_type=F32)[:24]
    head = lax.dot_general(block, pick_head, contract, preferred_element_type=F32)[:24]
    gains_ref[...] = jnp.zeros_like(gains_ref)
    head_gains_ref[...] = jnp.zeros_like(head_gains_ref)
    for g in range(4):
        chosen = jnp.where(gain_lanes(24, WIDTH, 5, 5 * g), wide, 0.0)
        gains_ref[g : g + 1] = jnp.sum(chosen, 0, keepdims=True)
    for g in range(2):
        chosen = jnp.where(gain_lanes(24, HEAD, 2, 20 + 2 * g), head, 0.0)
        head_gains_ref[4 + g : 5 + g] = jnp.sum(chosen, 0, keepdims=True)


def prepare_kernel(weights, gains, head_gains, cosine, sine, mine, before, *refs):
    normed_ref, keys_ref, values_ref, key_pre_ref, query_pre_ref, queries_ref = refs
    tokens = jnp.concatenate(
        [part[j, :BLOCK] for part in (before, mine) for j in range(4)], 0
    ).astype(F32)
    normed = (tokens * inverse_rms(tokens) * gains[0:1]).astype(BF16)
    normed_ref[...] = normed
    key_value = dot(normed, weights[:, HEADS * HEAD :])
    key_pre = key_value[:, :HEAD]
    key_pre_ref[...] = key_pre.astype(BF16)
    values_ref[...] = key_value[:, HEAD:].astype(BF16)
    query_pre = dot(normed[TOKENS:], weights[:, : HEADS * HEAD])
    query_pre_ref[...] = query_pre.astype(BF16)
    query_gain, key_gain = head_gains[4:5], head_gains[5:6]
    keys = rotate(key_pre * inverse_rms(key_pre) * key_gain, cosine[...], sine[...])
    keys_ref[...] = keys.astype(BF16)
    for h in range(HEADS):
        pre = query_pre[:, h * HEAD : (h + 1) * HEAD]
        turned = rotate(
            pre * inverse_rms(pre) * query_gain, cosine[TOKENS:], sine[TOKENS:]
        ).astype(BF16)
        for j in range(4):
            queries_ref[j, h * BLOCK : (h + 1) * BLOCK] = turned[j * BLOCK : (j + 1) * BLOCK]


def attention_kernel(first, meta, mine, before, *refs):
    step = pl.program_id(0)
    if first == 0:
        cosine, sine, slabs, refs = refs[0], refs[1], refs[2:10], refs[10:]
        results, refs = refs[:9], refs[9:]
        held, leaving = refs[5:14], refs[14]
        made, kept = held[:3], held[3:]
        copies = [
            pltpu.make_async_copy(source, target, leaving.at[j])
            for j, (source, target) in enumerate(zip(held, results))
        ]

        @pl.when(step == 0)
        def _():
            weights_kernel(meta, *slabs, *made, refs[3], refs[4])
            prepare_kernel(*made, cosine, sine, mine, before, *kept)
            for copy in copies:
                copy.start()

        @pl.when(step == pl.num_programs(0) - 1)
        def _():
            for copy in copies:
                copy.wait()

        _, keys_ref, values_ref, _, _, queries_ref = kept
    else:
        keys_ref, values_ref, queries_ref = refs[:3]
        refs = refs[3:]
    attended_ref, probs_ref, line_s = refs[:3]
    place = step + first
    lines = [
        part[j, BLOCK:].astype(F32)[0:1, :BLOCK] for part in (before, mine) for j in range(4)
    ]
    line_s[...] = jnp.broadcast_to(jnp.concatenate(lines, 1), line_s.shape)
    start = pl.multiple_of(place * BLOCK, BLOCK)
    window = pl.ds(start, SPAN)
    square = (BLOCK, BLOCK)
    diagonal = lax.broadcasted_iota(jnp.int32, square, 0) == lax.broadcasted_iota(
        jnp.int32, square, 1
    )
    own_line = line_s[0:1, pl.ds(pl.multiple_of(start + TOKENS, BLOCK), BLOCK)]
    own_column = jnp.sum(jnp.where(diagonal, own_line, 0.0), 1, keepdims=True)
    query_place = lax.broadcasted_iota(jnp.int32, (BLOCK, SPAN), 0)
    key_place = lax.broadcasted_iota(jnp.int32, (BLOCK, SPAN), 1) - HALO * BLOCK
    visible = (
        (key_place <= query_place)
        & (query_place - key_place < WINDOW)
        & (key_place + meta[4] + start >= 0)
        & (own_column == line_s[0:1, window])
    )
    bias = jnp.where(visible, 0.0, MASKED)
    queries = queries_ref[place if first == 0 else 0]
    scores = dot_nt(queries, keys_ref[window]) * SCALE + jnp.concatenate([bias] * HEADS, 0)
    terms = jnp.exp(scores - jnp.max(scores, -1, keepdims=True))
    probs = (terms * (1.0 / jnp.sum(terms, -1, keepdims=True))).astype(BF16)
    probs_ref[0] = probs
    mixed = dot(probs, values_ref[window]).astype(BF16)
    for h in range(HEADS):
        attended_ref[0, :, h * HEAD : (h + 1) * HEAD] = mixed[h * BLOCK : (h + 1) * BLOCK]


MADE = [((WIDTH, 1536), BF16), ((8, WIDTH), F32), ((8, HEAD), F32)]
KEPT = [
    ((KEYS, WIDTH), BF16),
    ((KEYS, HEAD), BF16),
    ((KEYS, HEAD), BF16),
    ((KEYS, HEAD), BF16),
    ((TOKENS, HEADS * HEAD), BF16),
    ((4, HEADS * BLOCK, HEAD), BF16),
]


def attention_blocks(first, count, meta, mine, before, tables, slabs, kept, after):
    outs = [((count, BLOCK, HEADS * HEAD), BF16), ((count, HEADS * BLOCK, SPAN), BF16)]
    making = first == 0
    fixed = MADE + KEPT if making else []
    if making:
        more = [*tables, *slabs]
        more_specs = [whole((KEYS, HEAD // 2))] * 2 + [whole((256, ATT_COLS))] * 8
    else:
        more = [kept[1], kept[2], kept[5]]
        more_specs = [whole((KEYS, HEAD))] * 2 + [from_row((HEADS * BLOCK, HEAD), first)]
    return call(
        functools.partial(attention_kernel, first),
        "attention_blocks",
        fixed + outs,
        [smem()] + [whole((4, TAGGED, WIDTH))] * 2 + more_specs,
        [meta, mine, before, *more],
        out_specs=[anywhere()] * len(fixed) + [by_row(s[1:]) for s, _ in outs],
        scratch=[pltpu.VMEM((8, KEYS), F32)]
        + [pltpu.VMEM((1024, ATT_COLS), BF16)] * 2
        + [pltpu.VMEM(s, d) for s, d in fixed]
        + [pltpu.SemaphoreType.DMA((9,))],
        after=after,
        grid=(count,),
        megabytes=60,
        flops=count * 4 * 10**9,
        moved_bytes=count * 10**7,
    )


def gelu_parts(gate):
    square = gate * gate
    bent = jnp.tanh(gate * (0.7978845608 + (0.7978845608 * 0.044715) * square))
    half = 0.5 + 0.5 * bent
    slope = half + gate * (1.0 - bent * bent) * (
        (0.5 * 0.7978845608) + (0.5 * 0.7978845608 * 3 * 0.044715) * square
    )
    return gate * half, slope


def feed_kernel(meta, table, gains, mine, cotangent, *refs):
    attended, refs = refs[0], refs[1:]
    own, other, own_down, other_down = refs[:4], refs[4:8], refs[8:12], refs[12:16]
    refs = refs[16:]
    block_out_ref, middle_grad_ref, attended_grad_ref, gain_ref = refs[:4]
    keep_ref, give_ref, keep_down_ref, give_down_ref = refs[4:8]
    (
        gate_w,
        up_w,
        down_w,
        output_w,
        active_s,
        slope_s,
        inner_s,
        inputs_s,
        grads_s,
        keep_s,
        give_s,
        grad_down,
        keep_down_s,
        give_down_s,
        arrivals,
        leaving,
    ) = refs[8:]
    core = meta[3]
    first_core = core == 0

    def fetch(sources, target, first):
        return [
            pltpu.make_async_copy(
                sources[j], target.at[j * 160 : (j + 1) * 160], arrivals.at[first + j]
            )
            for j in range(4)
        ]

    @pl.when(first_core)
    def _():
        for copy in fetch(own, gate_w, 0) + fetch(other, up_w, 4):
            copy.start()

    @pl.when(jnp.logical_not(first_core))
    def _():
        for copy in fetch(other, gate_w, 0) + fetch(own, up_w, 4):
            copy.start()

    for j in range(4):

        def place(i, carry, j=j):
            here = pl.ds(pl.multiple_of(i * 16, 16), 16)
            mine, theirs = own_down[j][here, ATT_COLS:], other_down[j][here, ATT_COLS:]
            down_w[table[2, j * 16 + i]] = mine[:, OUT_COLS:]
            down_w[table[3, j * 16 + i]] = theirs[:, OUT_COLS:]
            mine, theirs = mine[:, :OUT_COLS], theirs[:, :OUT_COLS]
            output_w[table[0, j * 16 + i], :, :OUT_COLS] = jnp.where(first_core, mine, theirs)
            output_w[table[1, j * 16 + i], :, OUT_COLS:] = jnp.where(first_core, theirs, mine)[
                :, : WIDTH - OUT_COLS
            ]
            return carry

        lax.fori_loop(0, 16, place, 0, unroll=8)

    picks = []
    for order in (*GATHER, SCATTER[0]):
        shard, row = slab_rows(meta, order, 5)
        picks.append(one_hot(shard * 5 + row, WIDTH))
    post_attn_gain, ffn_gain, post_ffn_gain = gains[1:2], gains[2:3], gains[3:4]
    output_weight = output_w[...].reshape(HEADS * HEAD, WIDTH)
    all_attended = attended[...].reshape(TOKENS, HEADS * HEAD)
    projected = dot(all_attended, output_weight)
    proj_inverse = inverse_rms(projected)
    proj_unit = projected * proj_inverse
    tokens = jnp.concatenate([mine[j, :BLOCK] for j in range(4)], 0)
    middle = tokens.astype(F32) + proj_unit * post_attn_gain
    mid_inverse = inverse_rms(middle)
    mid_unit = middle * mid_inverse
    ffn_in = (mid_unit * ffn_gain).astype(BF16)
    input_a = dot(ffn_in, picks[0]).astype(BF16)
    input_b = dot(ffn_in, picks[1]).astype(BF16)
    inputs_s[core] = dot(ffn_in, picks[2]).astype(BF16)
    inputs_s[1 - core] = input_b
    for copy in fetch(own, gate_w, 0) + fetch(own, up_w, 4):
        copy.wait()
    down = jnp.zeros((TOKENS, WIDTH), F32)
    for n in range(HIDDEN // CHUNK):
        columns = slice(n * CHUNK, (n + 1) * CHUNK)
        gate = dot(input_a, gate_w[:, columns])
        up = dot(input_b, up_w[:, columns])
        active, slope = gelu_parts(gate)
        active_s[:, columns] = active.astype(BF16)
        slope_s[:, columns] = (slope * up).astype(BF16)
        inner = (active * up).astype(BF16)
        inner_s[:, columns] = inner
        blocks = slice(n * (CHUNK // 16), (n + 1) * (CHUNK // 16))
        down += dot(inner, down_w[blocks].reshape(CHUNK, WIDTH))
    down_inverse = inverse_rms(down)
    down_unit = down * down_inverse
    block_out = (middle + down_unit * post_ffn_gain).astype(BF16)
    block_out_ref[...] = block_out.reshape(4, BLOCK, WIDTH)
    out_grad = cotangent[...].reshape(TOKENS, WIDTH).astype(F32)
    gain_ref[16:24] = add_rows(out_grad * down_unit)
    down_grad = norm_backward(out_grad * post_ffn_gain, down_unit, down_inverse).astype(BF16)
    sum_a = jnp.zeros((TOKENS, WIDTH), F32)
    sum_b = jnp.zeros((TOKENS, WIDTH), F32)
    sent = []
    for n in range(HIDDEN // CHUNK):
        columns = slice(n * CHUNK, (n + 1) * CHUNK)
        blocks = slice(n * (CHUNK // 16), (n + 1) * (CHUNK // 16))
        inner_grad = dot_nt(down_grad, down_w[blocks].reshape(CHUNK, WIDTH))
        gate_grad = (inner_grad * slope_s[:, columns].astype(F32)).astype(BF16)
        up_grad = (inner_grad * active_s[:, columns].astype(F32)).astype(BF16)
        grads_s[core] = gate_grad
        grads_s[1 - core] = up_grad
        grad_down[blocks] = (
            dot_tn(inner_s[:, columns], down_grad).astype(BF16).reshape(CHUNK // 16, 16, WIDTH)
        )
        keep_s[:, columns] = dot_tn(inputs_s[0], grads_s[0]).astype(BF16)
        give_s[:, columns] = dot_tn(inputs_s[1], grads_s[1]).astype(BF16)
        for source, target, k in ((keep_s, keep_ref, n), (give_s, give_ref, 4 + n)):
            copy = pltpu.make_async_copy(
                source.at[:, columns], target.at[:, columns], leaving.at[k]
            )
            copy.start()
            sent.append(copy)
        sum_a += dot_nt(gate_grad, gate_w[:, columns])
        sum_b += dot_nt(up_grad, up_w[:, columns])
    ffn_in_grad = dot_nt(sum_a.astype(BF16), picks[0]) + dot_nt(sum_b.astype(BF16), picks[1])
    gain_ref[8:16] = add_rows(ffn_in_grad * mid_unit)
    middle_grad = out_grad + norm_backward(ffn_in_grad * ffn_gain, mid_unit, mid_inverse)
    middle_grad_ref[...] = middle_grad
    gain_ref[0:8] = add_rows(middle_grad * proj_unit)
    proj_grad = norm_backward(middle_grad * post_attn_gain, proj_unit, proj_inverse).astype(BF16)
    attended_grad_ref[...] = dot_nt(proj_grad, output_weight).astype(BF16)
    output_w[...] = dot_tn(all_attended, proj_grad).astype(BF16).reshape(64, 16, WIDTH)
    pad = jnp.zeros((16, 2 * OUT_COLS - WIDTH), BF16)

    def hand(i, carry):
        grad_a = output_w[table[4, i], :, :OUT_COLS]
        grad_b = jnp.concatenate([output_w[table[5, i], :, OUT_COLS:], pad], 1)
        keep_down_s[i, :, :OUT_COLS] = jnp.where(first_core, grad_a, grad_b)
        give_down_s[i, :, :OUT_COLS] = jnp.where(first_core, grad_b, grad_a)
        keep_down_s[i, :, OUT_COLS:] = grad_down[table[6, i]]
        give_down_s[i, :, OUT_COLS:] = grad_down[table[7, i]]
        return carry

    lax.fori_loop(0, 64, hand, 0, unroll=8)
    for source, target, k in (
        (keep_down_s, keep_down_ref, 8),
        (give_down_s, give_down_ref, 9),
    ):
        copy = pltpu.make_async_copy(source, target, leaving.at[k])
        copy.start()
        sent.append(copy)
    for copy in sent:
        copy.wait()


def feed_forward(
    meta, table, gains, mine, cotangent, attended, own, other, own_down, other_down
):
    return call(
        feed_kernel,
        "feed_forward",
        [
            ((4, BLOCK, WIDTH), BF16),
            ((TOKENS, WIDTH), F32),
            ((TOKENS, HEADS * HEAD), BF16),
            ((24, WIDTH), F32),
            ((WIDTH, HIDDEN), BF16),
            ((WIDTH, HIDDEN), BF16),
            ((64, 16, DOWN_PACK), BF16),
            ((64, 16, DOWN_PACK), BF16),
        ],
        [smem(), smem()] + [vmem()] * 4 + [anywhere()] * 8 + [vmem()] * 8,
        [meta, table, gains, mine, cotangent, attended, *own, *other, *own_down, *other_down],
        out_specs=[vmem()] * 4 + [anywhere()] * 4,
        scratch=[
            pltpu.VMEM((WIDTH, HIDDEN), BF16),
            pltpu.VMEM((WIDTH, HIDDEN), BF16),
            pltpu.VMEM((128, 16, WIDTH), BF16),
            pltpu.VMEM((64, 16, WIDTH), BF16),
            pltpu.VMEM((TOKENS, HIDDEN), BF16),
            pltpu.VMEM((TOKENS, HIDDEN), BF16),
            pltpu.VMEM((TOKENS, HIDDEN), BF16),
            pltpu.VMEM((2, TOKENS, WIDTH), BF16),
            pltpu.VMEM((2, TOKENS, CHUNK), BF16),
            pltpu.VMEM((WIDTH, HIDDEN), BF16),
            pltpu.VMEM((WIDTH, HIDDEN), BF16),
            pltpu.VMEM((128, 16, WIDTH), BF16),
            pltpu.VMEM((64, 16, DOWN_PACK), BF16),
            pltpu.VMEM((64, 16, DOWN_PACK), BF16),
            pltpu.SemaphoreType.DMA((8,)),
            pltpu.SemaphoreType.DMA((10,)),
        ],
        megabytes=60,
        flops=17 * 10**9,
        moved_bytes=30 * 10**6,
    )


def attention_back_kernel(starting, first, meta, attended_grad, probs, queries, keys, values, *refs):
    step = pl.program_id(0)
    if starting:
        key_sum, value_sum, query_sum = refs

        @pl.when(step == 0)
        def _():
            key_sum[...] = jnp.zeros_like(key_sum)
            value_sum[...] = jnp.zeros_like(value_sum)
    else:
        sources, outs = refs[:14], refs[14:18]
        key_sum, value_sum, query_sum, part_a, part_b, arrivals = refs[18:24]
        held = refs[24:]
        copies = [
            pltpu.make_async_copy(source, target, arrivals.at[j])
            for j, (source, target) in enumerate(zip(sources, held))
        ]

        @pl.when(step == 0)
        def _():
            for copy in copies:
                copy.start()
            key_sum[...] = jnp.zeros_like(key_sum)
            value_sum[...] = jnp.zeros_like(value_sum)

    window = pl.ds(pl.multiple_of((step + first) * BLOCK, BLOCK), SPAN)
    mixed_grad = jnp.concatenate(
        [attended_grad[:, h * HEAD : (h + 1) * HEAD] for h in range(HEADS)], 0
    )
    prob_grad = dot_nt(mixed_grad, values[window])
    soft = probs[0].astype(F32)
    row_dot = jnp.sum(soft * prob_grad, -1, keepdims=True)
    score_grad = (soft * (prob_grad - row_dot)).astype(BF16)
    query_sum[step] = dot(score_grad, keys[window])
    key_sum[window] += dot_tn(score_grad, queries[0])
    value_sum[window] += dot_tn(probs[0], mixed_grad)
    if starting:
        return

    @pl.when(step == pl.num_programs(0) - 1)
    def _():
        for copy in copies:
            copy.wait()
        key_sum[...] += held[0][...]
        value_sum[...] += held[1][...]
        finish_attention(
            meta, key_sum, value_sum, query_sum, held[2], part_a, part_b, *held[3:], *outs
        )


def finish_attention(
    meta,
    key_sum,
    value_sum,
    query_sum,
    query_last,
    part_a,
    part_b,
    weights,
    gains,
    head_gains,
    cosine,
    sine,
    mine,
    before,
    normed,
    key_pre,
    query_pre,
    feed_gain,
    own_ref,
    before_ref,
    keep_ref,
    give_ref,
):
    query_gain, key_gain = head_gains[4:5] * SCALE, head_gains[5:6] * SCALE
    cosine_own, sine_own = cosine[TOKENS:], -sine[TOKENS:]
    query_total = jnp.zeros((8, HEAD), F32)
    pre_grads = []
    for h in range(HEADS):
        pre = query_pre[:, h * HEAD : (h + 1) * HEAD].astype(F32)
        inverse = inverse_rms(pre)
        unit = pre * inverse
        rows = slice(h * BLOCK, (h + 1) * BLOCK)
        grad = jnp.concatenate([part[j, rows] for part in (query_sum, query_last) for j in range(2)], 0)
        turned = rotate(grad, cosine_own, sine_own)
        query_total += add_rows(turned * unit)
        pre_grads.append(norm_backward(turned * query_gain, unit, inverse).astype(BF16))
    query_pre_grad = jnp.concatenate(pre_grads, 1)
    pre = key_pre[...].astype(F32)
    inverse = inverse_rms(pre)
    unit = pre * inverse
    turned = rotate(key_sum[...], cosine[...], -sine[...])
    key_total = add_rows(turned * unit)
    key_pre_grad = norm_backward(turned * key_gain, unit, inverse).astype(BF16)
    both = jnp.concatenate([key_pre_grad, value_sum[...].astype(BF16)], 1)
    normed_grad = dot_nt(both, weights[:, HEADS * HEAD :])
    own = normed_grad[TOKENS:] + dot_nt(query_pre_grad, weights[:, : HEADS * HEAD])
    own_ref[...] = own
    before_ref[...] = normed_grad[:TOKENS].astype(BF16)
    normed_grad = jnp.concatenate([normed_grad[:TOKENS], own], 0)
    tokens = jnp.concatenate(
        [part[j, :BLOCK] for part in (before, mine) for j in range(4)], 0
    ).astype(F32)
    attn_total = add_rows(tokens * inverse_rms(tokens) * normed_grad)
    pick_a, pick_b, gain_shard = line_picks(meta, SCATTER)
    query_weight_grad = dot_tn(normed[TOKENS:], query_pre_grad).astype(BF16)
    part_a[...] = dot_tn(pick_a, query_weight_grad[:, :ATT_COLS]).astype(BF16)
    both_grad = dot_tn(normed[...], both).astype(BF16)
    part_b[:, 256:] = dot_tn(pick_b, both_grad).astype(BF16)
    pick, pick_head = gain_picks(gain_shard)
    wide = jnp.zeros((128, WIDTH), F32)
    totals = (attn_total, feed_gain[0:8], feed_gain[8:16], feed_gain[16:24])
    for g in range(4):
        line = jnp.sum(totals[g], 0, keepdims=True)
        wide += jnp.where(gain_lanes(128, WIDTH, 5, 5 * g), line, 0.0)
    head = jnp.zeros((128, HEAD), F32)
    for g, total in enumerate((query_total, key_total)):
        line = jnp.sum(total, 0, keepdims=True) * SCALE
        head += jnp.where(gain_lanes(128, HEAD, 2, 20 + 2 * g), line, 0.0)
    contract = (((0,), (1,)), ((), ()))
    gain_block = lax.dot_general(
        pick, wide.astype(BF16), contract, preferred_element_type=F32
    ) + lax.dot_general(pick_head, head.astype(BF16), contract, preferred_element_type=F32)
    left = dot_tn(pick_b, query_weight_grad[:, ATT_COLS:])
    part_b[:, :128] = (left[:, :128] + gain_block).astype(BF16)
    part_b[:, 128:256] = left[:, 128:].astype(BF16)
    first_core = meta[3] == 0
    keep_ref[...] = jnp.where(first_core, part_a[...], part_b[...])
    give_ref[...] = jnp.where(first_core, part_b[...], part_a[...])


def attention_back(first, count, meta, attended_grad, probs, kept, earlier, inputs, after):
    starting = earlier is None
    sums = [((KEYS, HEAD), F32), ((KEYS, HEAD), F32), ((count, HEADS * BLOCK, HEAD), F32)]
    in_specs = [
        smem(),
        pl.BlockSpec((BLOCK, HEADS * HEAD), lambda r: (r + first, 0)),
        from_row((HEADS * BLOCK, SPAN), first),
        from_row((HEADS * BLOCK, HEAD), first),
        whole((KEYS, HEAD)),
        whole((KEYS, HEAD)),
    ]
    args = [meta, attended_grad, probs, kept[5], kept[1], kept[2]]
    outs = sums
    if not starting:
        args += [*earlier, *inputs]
        in_specs += [anywhere()] * 14
        outs = [((TOKENS, WIDTH), F32), ((TOKENS, WIDTH), BF16)] + [((1024, ATT_COLS), BF16)] * 2
    return call(
        functools.partial(attention_back_kernel, starting, first),
        "attention_back",
        outs,
        in_specs,
        args,
        out_specs=[whole(s) for s, _ in outs],
        scratch=[]
        if starting
        else [pltpu.VMEM(s, d) for s, d in sums]
        + [pltpu.VMEM((1024, ATT_COLS), BF16)] * 2
        + [pltpu.SemaphoreType.DMA((14,))]
        + [pltpu.VMEM(value.shape, value.dtype) for value in (*earlier, *inputs)],
        after=after,
        grid=(count,),
        megabytes=60,
        flops=count * 5 * 10**9,
        moved_bytes=count * 12 * 10**6,
    )


def pack_kernel(meta, query, key, value, output, gate, up, gains, keep_ref, give_ref, part):
    for half in range(2):
        part[half] = jnp.zeros((8, PACK), F32)
    out_start = ATT_COLS
    feed_start = ATT_COLS + OUT_COLS
    left = HEADS * HEAD - ATT_COLS
    part[0, :5, :ATT_COLS] = query[:, :ATT_COLS].astype(F32)
    part[0, :, out_start:feed_start] = output[:, :OUT_COLS].astype(F32)
    part[0, :5, feed_start:] = gate[...].astype(F32)
    part[1, :5, :left] = query[:, ATT_COLS:].astype(F32)
    part[1, :5, left : left + HEAD] = key[...].astype(F32)
    part[1, :5, left + HEAD : ATT_COLS] = value[...].astype(F32)
    part[1, 5:6, :128] = gains[...].astype(F32)
    part[1, :, out_start : out_start + WIDTH - OUT_COLS] = output[:, OUT_COLS:].astype(F32)
    part[1, :5, feed_start:] = up[...].astype(F32)
    core = meta[3]
    keep_ref[...] = part[core].astype(BF16)
    give_ref[...] = part[1 - core].astype(BF16)


def pack_weights(meta, query, key, value, output, gate, up, gains):
    return call(
        pack_kernel,
        "pack_weights",
        [((8, PACK), BF16)] * 2,
        [smem()] + [vmem()] * 7,
        [meta, query, key, value, output, gate, up, gains],
        scratch=[pltpu.VMEM((2, 8, PACK), F32)],
        megabytes=60,
        flops=10**6,
        moved_bytes=3 * 10**5,
    )


def pair_kernel(meta, kept, crossed, down, out_ref):
    first_core = meta[3] == 0
    mine, theirs = kept[...].astype(F32), crossed[...].astype(F32)
    upper = jnp.where(first_core, mine, theirs)
    lower = jnp.where(first_core, theirs, mine)
    out_ref[:, :PACK] = jnp.concatenate([upper, lower], 0).astype(BF16)
    out_ref[:, PACK:] = down[...]


def pair_up(meta, kept, crossed, down):
    return call(
        pair_kernel,
        "pair_up",
        [((16, PACK + WIDTH), BF16)],
        [smem()] + [vmem()] * 3,
        [meta, kept, crossed, down],
        megabytes=16,
        flops=10**6,
        moved_bytes=4 * 10**5,
    )[0]


def split_kernel(slot, meta, value, *refs):
    for j in range(4):
        refs[j][...] = value[meta[slot] ^ j]


def split_up(meta, slot, value, after):
    return call(
        functools.partial(split_kernel, slot),
        "split_up",
        [(value.shape[1:], value.dtype)] * 4,
        [smem(), vmem()],
        [meta, value],
        after=after,
        megabytes=16,
        flops=10**6,
        moved_bytes=10**6,
    )


def join_tokens_kernel(slot, meta, *refs):
    for j in range(4):
        refs[4][meta[slot] ^ j] = refs[j][:TAGGED]
        refs[5][meta[slot] ^ j] = refs[j][TAGGED:]


def join_tokens(meta, slot, pieces, after):
    return call(
        functools.partial(join_tokens_kernel, slot),
        "join_tokens",
        [((4, TAGGED, WIDTH), BF16), ((4, BLOCK, WIDTH), BF16)],
        [smem()] + [vmem()] * 4,
        [meta, *pieces],
        after=after,
        megabytes=16,
        flops=10**6,
        moved_bytes=10**6,
    )


def hold_kernel(*refs):
    pass


def hold(values, after):
    return call(
        hold_kernel,
        "hold",
        [(value.shape, value.dtype) for value in values],
        [anywhere()] * len(values),
        values,
        out_specs=[anywhere()] * len(values),
        after=after,
        aliases={j: j for j in range(len(values))},
        megabytes=60,
        flops=10**4,
        moved_bytes=10**4,
    )


def add_pieces_kernel(kept, crossed, *refs):
    rows = refs[0].shape[0]
    for j in range(4):
        here = slice(j * rows, (j + 1) * rows)
        refs[j][...] = (kept[here].astype(F32) + crossed[here].astype(F32)).astype(BF16)


def add_pieces(kept, crossed, after, megabytes=60):
    shape = (kept.shape[0] // 4,) + kept.shape[1:]
    return call(
        add_pieces_kernel,
        "add_pieces",
        [(shape, BF16)] * 4,
        [vmem()] * 2,
        [kept, crossed],
        after=after,
        megabytes=megabytes,
        flops=10**7,
        moved_bytes=8 * 10**6,
    )


def line_kernel(*refs):
    total = add_up(refs[0][...], [ref[...] for ref in refs[1:4]]).astype(BF16)
    for j in range(4):
        refs[4 + j][...] = total[j]


def line_up(own, others, after):
    return call(
        line_kernel,
        "line_up",
        [(own.shape[1:], BF16)] * 4,
        [vmem()] * 4,
        [own, *others],
        after=after,
        megabytes=16,
        flops=10**6,
        moved_bytes=2 * 10**6,
    )


def total_kernel(meta, *refs):
    total = add_up(refs[0][...], [ref[...] for ref in refs[1:4]])
    keep_ref, give_ref, down_ref = refs[4:]
    first_core = meta[3] == 0
    upper, lower = total[:8, :PACK], total[8:, :PACK]
    keep_ref[...] = jnp.where(first_core, upper, lower)
    give_ref[...] = jnp.where(first_core, lower, upper)
    down_ref[...] = total[:, PACK:]


def total_up(meta, own, others):
    return call(
        total_kernel,
        "total_up",
        [((8, PACK), F32)] * 2 + [((16, WIDTH), F32)],
        [smem()] + [vmem()] * 4,
        [meta, own, *others],
        megabytes=16,
        flops=10**6,
        moved_bytes=10**6,
    )


def output_kernel(slot, meta, gains, middle_grad, own, returned, mine, *refs):
    tokens = jnp.concatenate([mine[j, :BLOCK] for j in range(4)], 0).astype(F32)
    inverse = inverse_rms(tokens)
    normed_grad = own[...] + returned[...].astype(F32)
    grad = middle_grad[...] + norm_backward(normed_grad * gains[0:1], tokens * inverse, inverse)
    refs[4][...] = grad.astype(BF16).reshape(4, BLOCK, WIDTH)
    for j in range(4):
        refs[j][...] = refs[4][meta[slot] ^ j]


def output_pieces(meta, slot, gains, middle_grad, own, returned, mine):
    return call(
        functools.partial(output_kernel, slot),
        "output_pieces",
        [((BLOCK, WIDTH), BF16)] * 4,
        [smem()] + [vmem()] * 5,
        [meta, gains, middle_grad, own, returned, mine],
        scratch=[pltpu.VMEM((4, BLOCK, WIDTH), BF16)],
        megabytes=24,
        flops=10**7,
        moved_bytes=5 * 10**6,
    )


def join_outputs_kernel(slot, meta, *refs):
    for j in range(4):
        refs[8][meta[slot] ^ j] = refs[j][...]
        refs[9][meta[slot] ^ j] = refs[4 + j][...]


def join_outputs(meta, slot, first, second):
    return call(
        functools.partial(join_outputs_kernel, slot),
        "join_outputs",
        [((4, BLOCK, WIDTH), BF16)] * 2,
        [smem()] + [vmem()] * 8,
        [meta, *first, *second],
        megabytes=16,
        flops=10**6,
        moved_bytes=2 * 10**6,
    )


def stack_kernel(*refs):
    for j in range(4):
        refs[4][j] = refs[j][...]


def stack_kernel(*refs):
    for j in range(4):
        refs[4][j] = refs[j][...]


def stack_both_kernel(*refs):
    for j in range(8):
        refs[8 + j // 4][j % 4] = refs[j][...]


def stack_both(first, second, after):
    return call(
        stack_both_kernel,
        "stack_both",
        [((4,) + first[0].shape, BF16), ((4,) + second[0].shape, BF16)],
        [vmem()] * 8,
        [*first, *second],
        after=after,
        megabytes=16,
        flops=10**6,
        moved_bytes=10**7,
    )


def stack_up(pieces, shape, after):
    return call(
        stack_kernel,
        "stack_up",
        [((4,) + shape, BF16)],
        [vmem()] * 4,
        pieces,
        after=after,
        megabytes=16,
        flops=10**6,
        moved_bytes=4 * 10**6,
    )[0]


def first_slab_kernel(*refs):
    for j in range(4):
        here = slice(j * 64, (j + 1) * 64)
        refs[4][here, :ATT_COLS] = refs[j][:, :, :ATT_COLS].reshape(64, ATT_COLS)
        refs[4][here, ATT_COLS : ATT_COLS + OUT_COLS] = refs[j][
            :, :, ATT_COLS : ATT_COLS + OUT_COLS
        ].reshape(64, OUT_COLS)
        refs[4][here, ATT_COLS + OUT_COLS :] = refs[j][:, :, PACK:].reshape(64, WIDTH)


def first_slab(pieces, after):
    return call(
        first_slab_kernel,
        "first_slab",
        [((256, FIRST_PACK), BF16)],
        [vmem()] * 4,
        pieces,
        after=after,
        megabytes=16,
        flops=10**6,
        moved_bytes=3 * 10**6,
    )[0]


def loose_rows():
    line = lax.broadcasted_iota(jnp.int32, (256, 160), 0)
    row = line & 7
    dense = lax.broadcasted_iota(jnp.int32, (256, 160), 1)
    same = ((line >> 3) * 5 + row == dense) & (row < 5)
    return jnp.where(same, 1.0, 0.0).astype(BF16)


def feed_slab_kernel(*refs):
    feed_ref, loose = refs[4:]
    for j in range(4):
        loose[j * 64 : (j + 1) * 64] = refs[j][:, :, ATT_COLS + OUT_COLS : PACK].reshape(
            64, HIDDEN
        )
    feed_ref[...] = dot_tn(loose_rows(), loose[...]).astype(BF16)


def feed_slab_of(pieces, after):
    return call(
        feed_slab_kernel,
        "feed_slab",
        [((160, HIDDEN), BF16)],
        [vmem()] * 4,
        pieces,
        scratch=[pltpu.VMEM((256, HIDDEN), BF16)],
        after=after,
        megabytes=16,
        flops=2 * 10**8,
        moved_bytes=4 * 10**6,
    )[0]


def merge_kernel(*refs):
    sources, outs, held, arrivals = refs[:12], refs[12:16], refs[16:28], refs[28]
    copies = [
        pltpu.make_async_copy(source, target, arrivals.at[j])
        for j, (source, target) in enumerate(zip(sources, held))
    ]
    for copy in copies:
        copy.start()

    def total(first):
        for copy in copies[first : first + 4]:
            copy.wait()
        pieces = held[first : first + 4]
        return add_up(pieces[0][...], [piece[...] for piece in pieces[1:]]).astype(BF16)

    def hand_out(value, start):
        for j in range(4):
            outs[j][:, :, start : start + value.shape[2]] = value[j * 4 : (j + 1) * 4]

    hand_out(total(0).reshape(16, 16, ATT_COLS), 0)
    hand_out(total(8), ATT_COLS + HIDDEN)
    feed_total = dot(loose_rows(), total(4)).astype(BF16)
    hand_out(feed_total.reshape(16, 16, HIDDEN), ATT_COLS)


def merge_grads(att, feed, down):
    pieces = [*att, *feed, *down]
    return call(
        merge_kernel,
        "merge_grads",
        [((4, 16, PACK + WIDTH), BF16)] * 4,
        [anywhere()] * 12,
        pieces,
        scratch=[pltpu.VMEM(piece.shape, piece.dtype) for piece in pieces]
        + [pltpu.SemaphoreType.DMA((12,))],
        megabytes=30,
        flops=2 * 10**8,
        moved_bytes=8 * 10**6,
    )


def unpack_kernel(meta, mine, theirs, query, key, value, output, gate, up, gains):
    first_core = meta[3] == 0
    part_a = jnp.where(first_core, mine[...], theirs[...])
    part_b = jnp.where(first_core, theirs[...], mine[...])
    left = HEADS * HEAD - ATT_COLS
    feed_end = ATT_COLS + HIDDEN
    query[:, :ATT_COLS] = part_a[:5, :ATT_COLS]
    query[:, ATT_COLS:] = part_b[:5, :left]
    key[...] = part_b[:5, left : left + HEAD]
    value[...] = part_b[:5, left + HEAD : ATT_COLS]
    gate[...] = part_a[:5, ATT_COLS:feed_end]
    up[...] = part_b[:5, ATT_COLS:feed_end]
    output[:, :OUT_COLS] = part_a[:, feed_end:]
    output[:, OUT_COLS:] = part_b[:, feed_end : feed_end + WIDTH - OUT_COLS]
    gains[...] = part_b[5:6, :128]


def unpack_grads(meta, mine, theirs):
    return call(
        unpack_kernel,
        "unpack_grads",
        [
            ((5, HEADS * HEAD), F32),
            ((5, HEAD), F32),
            ((5, HEAD), F32),
            ((8, WIDTH), F32),
            ((5, HIDDEN), F32),
            ((5, HIDDEN), F32),
            ((1, 128), F32),
        ],
        [smem()] + [vmem()] * 2,
        [meta, mine, theirs],
        megabytes=16,
        flops=10**6,
        moved_bytes=4 * 10**5,
    )


def on_device(
    hidden_in,
    segment_ids,
    cotangent,
    attn_gain,
    query_weight,
    key_weight,
    value_weight,
    query_gain,
    key_gain,
    output_weight,
    post_attn_gain,
    ffn_gain,
    gate_weight,
    up_weight,
    down_weight,
    post_ffn_gain,
):
    me = my_place()
    core = me["c"]
    first_core = core == 0
    row = 2 * ((me["x"] ^ (me["x"] >> 1)) & 1) + core
    member = 2 * (me["x"] & 1) + core
    place = (me["y"] >> 1) * 1024 + (me["x"] >> 1) * TOKENS
    meta = jnp.stack([me["z"], me["y"], me["x"], core, place, row, member]).astype(jnp.int32)
    row_slot, member_slot = 5, 6

    def pick(value_first, value_second):
        return jnp.where(first_core, value_first, value_second)

    positions = place + jnp.arange(-TOKENS, TOKENS, dtype=jnp.int32)
    frequency = jnp.exp(
        jnp.arange(HEAD // 2, dtype=F32) * (-2.0 * math.log(ROPE_BASE) / HEAD)
    )
    angles = positions.astype(F32)[:, None] * frequency[None]
    tables = (jnp.cos(angles), jnp.sin(angles))

    gains = jnp.zeros((128,), F32)
    start = 0
    for gain in (attn_gain, post_attn_gain, ffn_gain, post_ffn_gain, query_gain, key_gain):
        size = gain.shape[0]
        gains = gains + jnp.pad(gain.astype(F32), (start, 128 - start - size))
        start += size
    kept, given = pack_weights(
        meta,
        query_weight,
        key_weight,
        value_weight,
        output_weight,
        gate_weight,
        up_weight,
        gains.reshape(1, 128),
    )
    pair = pair_up(meta, kept, swap(given), down_weight)
    near_chips = arrived(pair, 0)

    def sent_around(pieces):
        own, one, two, three = pieces
        return [own, swap(one), exchange(two, False), exchange(three, True)]

    segments = segment_ids.reshape(4, 1, BLOCK).astype(BF16)
    segments = jnp.pad(segments, ((0, 0), (0, TAGGED - BLOCK - 1), (0, WIDTH - BLOCK)))
    dealing = jnp.concatenate(
        [
            hidden_in.reshape(4, BLOCK, WIDTH),
            segments,
            cotangent.reshape(4, BLOCK, WIDTH),
        ],
        1,
    )
    pieces = sent_around(split_up(meta, row_slot, dealing, []))
    mine, cotangent_mine = join_tokens(meta, member_slot, pieces, near_chips)
    near, before = next_chunk(mine, me["x"] < 2)

    line = stack_up([pair, *near_chips], pair.shape, [mine])
    plane = [line, *arrived(line, 1)]
    plane = [line, *arrived(line, 1)]
    slab = first_slab(plane, [*tables, near])
    first_own = [slab, *arrived(slab, 2)]
    first_other = [swap(value) for value in first_own]
    feed_slab = feed_slab_of(plane, first_own[1:])

    grid = jnp.arange(64, dtype=jnp.int32)
    table = []
    for orders in (GATHER, SCATTER):
        chips = [chip_of([me["z"], me["y"], me["x"]], order, grid) for order in orders]
        held, crossed = pick(chips[0], chips[1]), pick(chips[1], chips[0])
        table += [*chips, held * 2 + core, crossed * 2 + 1 - core]
    table = jnp.stack(table).astype(jnp.int32)

    forward = attention_blocks(0, 4, meta, mine, before, tables, first_own + first_other, None, [])
    made, kept_values, (attended, probs) = forward[:3], forward[3:9], forward[9:]
    feed_own = [feed_slab, *hold(arrived(feed_slab, 2), [attended])]
    (
        block_out,
        middle_grad,
        attended_grad,
        feed_gain,
        keep_feed,
        give_feed,
        keep_down,
        give_down,
    ) = feed_forward(
        meta,
        table,
        made[1],
        mine,
        cotangent_mine,
        attended,
        feed_own,
        [swap(value) for value in feed_own],
        first_own,
        first_other,
    )
    block_pieces = sent_around(split_up(meta, member_slot, block_out, []))
    back = attention_back(2, 2, meta, attended_grad, probs, kept_values, None, None, [])
    feed_sum = add_pieces(keep_feed, swap(give_feed), [back[0]])
    down_sum = add_pieces(keep_down, swap(give_down), [back[0]])
    normed_grad, to_before, keep_att, give_att = attention_back(
        0,
        2,
        meta,
        attended_grad,
        probs,
        kept_values,
        back,
        (
            *made,
            *tables,
            mine,
            before,
            kept_values[0],
            kept_values[3],
            kept_values[4],
            feed_gain,
        ),
        [*feed_sum, *down_sum, *block_pieces[1:]],
    )
    feed_in = received(feed_sum, 2)
    down_in = received(down_sum, 2)

    give_att = hold([give_att], [*feed_in, *down_in[:2]])[0]
    att_sum = add_pieces(keep_att, swap(give_att), [], 24)
    plane = merge_grads(
        [att_sum[0], *received(att_sum, 2)], [feed_sum[0], *feed_in], [down_sum[0], *down_in]
    )
    returned = chunk_before(to_before)
    pieces = output_pieces(
        meta, member_slot, made[1], middle_grad, normed_grad, returned, mine
    )
    line = line_up(plane[0], received(plane, 1), [pieces[0]])
    kept_grads, given_grads, grad_down = total_up(meta, line[0], received(line, 0))
    grad_query, grad_key, grad_value, grad_output, grad_gate, grad_up, gain_grads = unpack_grads(
        meta, kept_grads, swap(given_grads)
    )
    gain_grads = gain_grads.reshape(128)

    block_out, input_grad = join_outputs(meta, row_slot, block_pieces, sent_around(pieces))
    return (
        block_out.reshape(hidden_in.shape),
        input_grad.reshape(hidden_in.shape),
        gain_grads[0:5],
        grad_query,
        grad_key,
        grad_value,
        gain_grads[20:22],
        gain_grads[22:24],
        grad_output,
        gain_grads[5:10],
        gain_grads[10:15],
        grad_gate,
        grad_up,
        grad_down,
        gain_grads[15:20],
    )


def solution(mesh):
    rows = P(None, "dp", "seq", None)
    shard = P(("dp", "seq"), None)
    vector = P(("dp", "seq"))
    return jax.shard_map(
        on_device,
        mesh=mesh,
        in_specs=(rows, P(None, "dp", "seq"), rows)
        + (vector, shard, shard, shard, vector, vector, shard, vector)
        + (vector, shard, shard, shard, vector),
        out_specs=(rows, rows)
        + (vector, shard, shard, shard, vector, vector, shard, vector)
        + (vector, shard, shard, shard, vector),
        check_vma=False,
    )
```
